32 devices in a mesh: expert: 16 (over z, y, core), tp: 2 (over x).
Axes of the slice: x: 2, y: 2, z: 4, core: 2. Of those that a mesh axis runs over, the one named last changes fastest.
Arguments:
- cotangent: bfloat16 [2048, 2048], P('expert'), may hold values from -6 to 6
- gates: float32 [2048, 8], P('expert'), may hold values from 0.05 to 0.6
- expert_ids: int32 [2048, 8], P('expert'), may hold values from 0 to 31, all different within a row; in each aligned block of 128 rows (0 to 127, 128 to 255, ...) at most 48 rows name the same one
- saved_gate: bfloat16 [32, 768, 768], P('expert', 'tp'), may hold values from -6 to 6
- saved_up: bfloat16 [32, 768, 768], P('expert', 'tp'), may hold values from -6 to 6
- w_gate: bfloat16 [32, 768, 2048], P('expert', 'tp'), may hold values from -0.125 to 0.125
- w_up: bfloat16 [32, 768, 2048], P('expert', 'tp'), may hold values from -0.125 to 0.125
- w_down: bfloat16 [32, 768, 2048], P('expert', 'tp'), may hold values from -0.21875 to 0.21875
Outputs:
- token_grad: float32 [2048, 2048], P(('expert', 'tp'))
The draws below stay inside these ranges and needn't reach their ends.
Inputs may be any that keep to these rules, and one draw needn't show every extreme that they name: `expert_ids`: within the 128 tokens of one group, no expert is named by more than 48 route rows, a bound that some block reaches; a token names 8 different experts.
All inputs are finite; a program needn't handle non-finite values.
Results may differ from the reference program's by a relative error of at most 0.0049.
Values may be sent and summed in bfloat16 or wider, within the bound.
No kernel may reach another device: no remote copies, remote signals or barrier semaphores. Data moves between devices by JAX's collectives and lax.ppermute only.
A program may use at most 64 MiB of HBM per device.

```python
import math
import jax
import jax.numpy as jnp
import numpy as np
from jax import lax

D = 2048
FF = 768
TOP = 8
TOK_GROUP = 128
EXPERTS = 32
TOKENS = 2048
CAP = 48
N_EXPERT = 16
N_TP = 2


def steps_of(key, dims, pieces, smallest, top_value):
    factor_of, own = 1.0, jax.random.fold_in(key, 6)
    for dim, shards_of in pieces:
        draws = jnp.exp(jax.random.uniform(jax.random.fold_in(own, dim), (shards_of,), jnp.float32, smallest / len(pieces), top_value / len(pieces)))
        factor_of = factor_of * jnp.repeat(draws, dims[dim] // shards_of).reshape([-1 if axis == dim else 1 for axis in range(len(dims))])
    return factor_of


def shared_out(rng, own, number, rows, number_of, top, limit, skew):
    order = jax.random.permutation(rng, number_of)
    heavy_load, common = portions_of(number_of, rows * top, limit, skew, True), portions_of(number_of, rows * top, limit, skew, False)
    places = jnp.arange(number_of)

    def named(sizes, rotation):
        used = int((sizes > 0).sum())
        fixed = max(1, used // 4)
        passed = fixed + (places - fixed + rotation * (used - fixed)) % max(1, number_of - fixed)
        return jnp.zeros((number_of,), jnp.int32).at[order[jnp.where(places < fixed, places, passed)]].set(jnp.asarray(sizes, jnp.int32))

    sizes = jnp.where(number % 4 == 0, named(heavy_load, number // 4), named(common, number - number // 4 - 1))
    mixed = jax.random.permutation(jax.random.fold_in(own, 3), number_of)
    donor, sink = mixed[0:number_of // 2 * 2:2], mixed[1:number_of // 2 * 2:2]
    room = jnp.minimum(sizes[donor] - 1, limit - sizes[sink]) // 2
    room = jnp.where((donor == order[0]) | (sink == order[0]) | (sizes[sink] == 0), 0, jnp.maximum(room, 0))
    passed = jax.random.randint(jax.random.fold_in(own, 4), (number_of // 2,), 0, 1 << 20) % (room + 1)
    sizes = sizes.at[donor].add(-passed).at[sink].add(passed)
    items = jnp.searchsorted(jnp.cumsum(sizes), jnp.arange(rows * top), side="right").astype(jnp.int32)
    table = items.reshape(top, rows).T
    table = table[jax.random.permutation(jax.random.fold_in(own, 1), rows)]
    rotation = jax.random.randint(jax.random.fold_in(own, 2), (rows, 1), 0, top)
    return jnp.take_along_axis(table, (jnp.arange(top)[None, :] + rotation) % top, axis=1)


def portions_of(number_of, total, reach, lean, full):
    weights = [(1 << 20) // math.isqrt(grade ** lean) + 1 for grade in range(1, number_of + 1)]
    largest = reach if full else min(reach, max(-(-total // number_of), total * weights[0] // sum(weights)))
    least = 1 if total - largest >= number_of - 1 else 0
    counts, rest = [largest] + [least] * (number_of - 1), total - largest - least * (number_of - 1)
    while rest > 0:
        candidates = [i for i in range(1, number_of) if counts[i] < largest] or [i for i in range(1, number_of) if counts[i] < reach]
        pool, budget = sum([weights[i] for i in candidates]), rest
        for i in candidates:
            more = min(reach - counts[i], max(1, budget * weights[i] // pool), rest)
            counts[i] = counts[i] + more
            rest = rest - more
    return np.array(counts)


def centred(key, extent, spread, most, split=(), kind=jnp.bfloat16):
    drawn = jax.random.normal(key, extent, jnp.float32) * spread
    if len(split) > 0:
        drawn = steps_of(key, extent, split, -0.22, 0.18) * drawn
    return jnp.clip(drawn, min=-most, max=most).astype(kind)


def setup_inputs(seed: int = 0) -> dict:
    streams_of = jax.random.split(jax.random.key(seed), 9)
    cotangent = centred(streams_of[0], (TOKENS, D), 1.0, 6.0, ((0, 16),))
    gates = jnp.clip(jnp.exp(math.log(0.6) - 2.4849067 * jax.random.uniform(streams_of[1], (TOKENS, TOP), jnp.float32) ** steps_of(streams_of[1], (TOKENS, TOP), ((0, 16),), -0.2, 0.2)), 0.05, 0.6)
    expert_ids_keys = jax.random.split(jax.random.fold_in(streams_of[2], 1), TOKENS // TOK_GROUP)
    expert_ids_turns = jax.random.permutation(jax.random.fold_in(streams_of[2], 3), TOKENS // TOK_GROUP)
    expert_ids = jax.vmap(lambda own, number: shared_out(jax.random.fold_in(streams_of[2], 2), own, number, TOK_GROUP, EXPERTS, TOP, CAP, 2))(expert_ids_keys, expert_ids_turns).reshape((TOKENS, TOP))
    saved_gate = centred(streams_of[3], (EXPERTS, FF, N_EXPERT * CAP), 1.0, 6.0, ((0, 16), (1, 2)))
    saved_up = centred(streams_of[4], (EXPERTS, FF, N_EXPERT * CAP), 1.0, 6.0, ((0, 16), (1, 2)))
    w_gate = centred(streams_of[5], (EXPERTS, FF, D), D ** -0.5, 0.125, ((0, 16), (1, 2)))
    w_up = centred(streams_of[6], (EXPERTS, FF, D), D ** -0.5, 0.125, ((0, 16), (1, 2)))
    w_down = centred(streams_of[7], (EXPERTS, FF, D), FF ** -0.5, 0.21875, ((0, 16), (1, 2)))
    return dict(cotangent=cotangent, gates=gates, expert_ids=expert_ids, saved_gate=saved_gate, saved_up=saved_up, w_gate=w_gate, w_up=w_up, w_down=w_down)


def slot_positions(group_ids):
    one_hot = (group_ids[:, None] == jnp.arange(EXPERTS, dtype=jnp.int32)[None, :]).astype(jnp.int32)
    before = jnp.cumsum(one_hot, axis=0) - one_hot
    return lax.optimization_barrier(jnp.sum(before * one_hot, axis=1)).astype(jnp.int32)

def expert_grad(operands):
    arrived, pre_gate, pre_up, weight_gate, weight_up, weight_down = operands
    hidden_grad = jnp.dot(weight_down, arrived.T, preferred_element_type=jnp.float32)
    gate_value = pre_gate.astype(jnp.float32)
    up_value = pre_up.astype(jnp.float32)
    sigmoid_gate = jax.nn.sigmoid(gate_value)
    up_grad = (hidden_grad * gate_value * sigmoid_gate).astype(jnp.bfloat16)
    gate_grad = (hidden_grad * up_value * sigmoid_gate * (1.0 + gate_value * (1.0 - sigmoid_gate))).astype(jnp.bfloat16)
    shard_width = FF // N_TP
    slot_total = arrived.shape[0]
    gate_split = gate_grad.astype(jnp.float32).reshape(N_TP, shard_width, slot_total)
    up_split = up_grad.astype(jnp.float32).reshape(N_TP, shard_width, slot_total)
    gate_weight_split = weight_gate.astype(jnp.float32).reshape(N_TP, shard_width, D)
    up_weight_split = weight_up.astype(jnp.float32).reshape(N_TP, shard_width, D)
    partial_value = jnp.einsum('tfs,tfd->tsd', gate_split, gate_weight_split) + jnp.einsum('tfs,tfd->tsd', up_split, up_weight_split)
    rounded = lax.optimization_barrier(partial_value.astype(jnp.bfloat16))
    return lax.optimization_barrier(jnp.sum(rounded.astype(jnp.float32), axis=0))

def reference(cotangent, gates, expert_ids, saved_gate, saved_up, w_gate, w_up, w_down):
    route_total = TOKENS * TOP
    group_ids = expert_ids.reshape(N_EXPERT, TOK_GROUP * TOP)
    slot_pos = lax.map(slot_positions, group_ids)
    group_index = jnp.arange(N_EXPERT, dtype=jnp.int32)[:, None]
    target = ((group_ids * N_EXPERT + group_index) * CAP + slot_pos).reshape(route_total).astype(jnp.int32)
    scaled = (gates[:, :, None] * cotangent.astype(jnp.float32)[:, None, :]).astype(jnp.bfloat16).reshape(route_total, D)
    buffer = jnp.zeros((EXPERTS * N_EXPERT * CAP, D), jnp.bfloat16).at[target].set(scaled)
    buffer = buffer.reshape(EXPERTS, N_EXPERT * CAP, D)
    summed = lax.map(expert_grad, (buffer, saved_gate, saved_up, w_gate, w_up, w_down))
    picked = summed.reshape(EXPERTS * N_EXPERT * CAP, D)[target]
    return lax.optimization_barrier(jnp.sum(picked.reshape(TOKENS, TOP, D), axis=1))
```

```python
import jax
import jax.numpy as jnp
from jax import lax
from jax.sharding import PartitionSpec as P


def route_slots(expert_ids, expert_total):
    flat_ids = expert_ids.reshape(-1)
    one_hot = (flat_ids[:, None] == jnp.arange(expert_total, dtype=jnp.int32)[None, :]).astype(
        jnp.int32
    )
    before = jnp.cumsum(one_hot, axis=0) - one_hot
    return (flat_ids, jnp.sum(before * one_hot, axis=1))


def expert_step(arrived, saved_gate, saved_up, w_gate, w_up, w_down):
    hidden_grad = jnp.einsum("efd,esd->efs", w_down, arrived, preferred_element_type=jnp.float32)
    gate_value = saved_gate.astype(jnp.float32)
    up_value = saved_up.astype(jnp.float32)
    sigmoid_gate = jax.nn.sigmoid(gate_value)
    up_grad = (hidden_grad * gate_value * sigmoid_gate).astype(jnp.bfloat16)
    gate_grad = (
        hidden_grad * up_value * sigmoid_gate * (1.0 + gate_value * (1.0 - sigmoid_gate))
    ).astype(jnp.bfloat16)
    partial_value = jnp.einsum(
        "efs,efd->esd", gate_grad, w_gate, preferred_element_type=jnp.float32
    )
    partial_value = partial_value + jnp.einsum(
        "efs,efd->esd", up_grad, w_up, preferred_element_type=jnp.float32
    )
    return partial_value.astype(jnp.bfloat16)


def slots_body(cotangent, gates, expert_ids, saved_gate, saved_up, w_gate, w_up, w_down):
    owners = lax.axis_size("expert")
    row_count, feature_dim = cotangent.shape
    top_count = expert_ids.shape[1]
    local_count, _, slot_count = saved_gate.shape
    capacity = slot_count // owners
    flat_ids, slot_pos = route_slots(expert_ids, local_count * owners)
    target = flat_ids % local_count * slot_count + flat_ids // local_count * capacity + slot_pos
    scaled = (gates[:, :, None] * cotangent.astype(jnp.float32)[:, None, :]).astype(jnp.bfloat16)
    scaled = scaled.reshape(row_count * top_count, feature_dim)
    outgoing = (
        jnp.zeros((local_count * slot_count, feature_dim), jnp.bfloat16).at[target].set(scaled)
    )
    outgoing = outgoing.reshape(local_count, slot_count, feature_dim)
    arrived = lax.all_to_all(outgoing, "expert", split_axis=1, concat_axis=1, tiled=True)
    partial_value = expert_step(arrived, saved_gate, saved_up, w_gate, w_up, w_down)
    returned = lax.all_to_all(partial_value, "expert", split_axis=1, concat_axis=1, tiled=True)
    picked = returned.reshape(local_count * slot_count, feature_dim)[target].astype(jnp.float32)
    combined = jnp.sum(picked.reshape(row_count, top_count, feature_dim), axis=1)
    return lax.psum_scatter(combined, "tp", scatter_dimension=0, tiled=True)


def swap(value, axis, step):
    count = lax.axis_size(axis)
    return lax.ppermute(value, axis, [(i, i ^ step) for i in range(count)])


def half(value, axis, index):
    return lax.index_in_dim(value, 0, axis, keepdims=False) if value.shape[axis] == 1 else (
        lax.dynamic_index_in_dim(value, index, axis, keepdims=False)
    )


def add(kept, came):
    return (kept.astype(jnp.float32) + came.astype(jnp.float32)).astype(jnp.bfloat16)


def scatter_sums(total):
    owners = lax.axis_size("expert")
    shards = lax.axis_size("tp")
    outer = owners // 4
    row_count, feature_dim = total.shape
    piece = row_count // owners // shards
    me = lax.axis_index("expert")
    core, row, line = me % 2, me // 2 % 2, me // 4
    side = lax.axis_index("tp")
    total = total.reshape(outer, 2, 2, shards, piece, feature_dim)
    came = swap(half(total, 2, 1 - core), "expert", 1)
    total = add(half(total, 2, core), came)
    left, right = total[..., :feature_dim // 2], total[..., feature_dim // 2:]
    left_came = swap(half(left, 2, 1 - side), "tp", 1)
    right_came = swap(half(right, 1, 1 - row), "expert", 2)
    left = add(half(left, 2, side), left_came)
    right = add(half(right, 1, row), right_came)
    left_came = swap(half(left, 1, 1 - row), "expert", 2)
    right_came = swap(half(right, 1, 1 - side), "tp", 1)
    left = add(half(left, 1, row), left_came)
    right = add(half(right, 1, side), right_came)
    total = jnp.concatenate([left, right], axis=-1)
    result = half(total, 0, line).astype(jnp.float32)
    for shift in range(1, outer):
        perm = [(i, (i + 4 * shift) % owners) for i in range(owners)]
        came = lax.ppermute(half(total, 0, (line + shift) % outer), "expert", perm)
        result = result + came.astype(jnp.float32)
    return result


def tokens_body(cotangent, gates, expert_ids, saved_gate, saved_up, w_gate, w_up, w_down):
    owners = lax.axis_size("expert")
    shards = lax.axis_size("tp")
    row_count, feature_dim = cotangent.shape
    local_count, _, slot_count = saved_gate.shape
    capacity = slot_count // owners
    piece = row_count // shards
    start = lax.axis_index("tp") * piece
    high = lax.reduce_precision(gates, 8, 7)
    middle = lax.reduce_precision(gates - high, 8, 7)
    low = gates - high - middle
    side = jnp.concatenate(
        [high, middle, low, expert_ids.astype(jnp.float32)], axis=1
    ).astype(jnp.bfloat16)
    side = jnp.pad(side, ((0, 0), (0, 128 - side.shape[1])))
    own = lax.dynamic_slice_in_dim(jnp.concatenate([cotangent, side], axis=1), start, piece, 0)
    every = lax.all_gather(own, ("expert", "tp"), axis=0, tiled=True)
    every = every.reshape(owners, row_count, feature_dim + 128)
    tokens = every[:, :, :feature_dim]
    top = gates.shape[1]
    sides = every[:, :, feature_dim:].astype(jnp.float32)
    every_gate = sides[:, :, :top] + sides[:, :, top:2 * top] + sides[:, :, 2 * top:3 * top]
    every_id = sides[:, :, 3 * top:4 * top].astype(jnp.int32)
    mine = lax.axis_index("expert") * local_count + jnp.arange(local_count, dtype=jnp.int32)
    named = every_id[None] == mine[:, None, None, None]
    gate_of = jnp.sum(jnp.where(named, every_gate[None], 0.0), axis=-1)
    hit = jnp.any(named, axis=-1)
    ones = hit.astype(jnp.int32)
    slot = jnp.cumsum(ones, axis=2) - ones
    pick = (
        (slot[:, :, None, :] == jnp.arange(capacity, dtype=jnp.int32)[None, None, :, None])
        & hit[:, :, None, :]
    )
    slot_gate = jnp.sum(jnp.where(pick, gate_of[:, :, None, :], 0.0), axis=-1)
    pick = pick.astype(jnp.bfloat16)
    rows = jnp.einsum("egst,gtd->egsd", pick, tokens, preferred_element_type=jnp.float32)
    arrived = (rows * slot_gate[..., None]).astype(jnp.bfloat16)
    arrived = arrived.reshape(local_count, slot_count, feature_dim)
    partial_value = expert_step(arrived, saved_gate, saved_up, w_gate, w_up, w_down)
    partial_value = partial_value.reshape(local_count, owners, capacity, feature_dim)
    total = jnp.einsum("egst,egsd->gtd", pick, partial_value, preferred_element_type=jnp.float32)
    total = total.astype(jnp.bfloat16).reshape(owners * row_count, feature_dim)
    return scatter_sums(total)


def solution(mesh):
    in_specs = (
        P("expert", None),
        P("expert", None),
        P("expert", None),
        P("expert", "tp", None),
        P("expert", "tp", None),
        P("expert", "tp", None),
        P("expert", "tp", None),
        P("expert", "tp", None),
    )
    out_specs = P(("expert", "tp"), None)
    fits = mesh.shape["expert"] in (4, 8, 16) and mesh.shape["tp"] == 2
    body = tokens_body if fits else slots_body
    return jax.shard_map(body, mesh=mesh, in_specs=in_specs, out_specs=out_specs, check_vma=False)
```

```python
import functools

import jax
import jax.numpy as jnp
from jax import lax
from jax.experimental import pallas as pl
from jax.experimental.pallas import tpu as pltpu
from jax.sharding import PartitionSpec as P


def route_slots(expert_ids, expert_total):
    flat_ids = expert_ids.reshape(-1)
    one_hot = (flat_ids[:, None] == jnp.arange(expert_total, dtype=jnp.int32)[None, :]).astype(
        jnp.int32
    )
    before = jnp.cumsum(one_hot, axis=0) - one_hot
    return (flat_ids, jnp.sum(before * one_hot, axis=1))


def expert_step(arrived, saved_gate, saved_up, w_gate, w_up, w_down):
    hidden_grad = jnp.einsum("efd,esd->efs", w_down, arrived, preferred_element_type=jnp.float32)
    gate_value = saved_gate.astype(jnp.float32)
    up_value = saved_up.astype(jnp.float32)
    sigmoid_gate = jax.nn.sigmoid(gate_value)
    up_grad = (hidden_grad * gate_value * sigmoid_gate).astype(jnp.bfloat16)
    gate_grad = (
        hidden_grad * up_value * sigmoid_gate * (1.0 + gate_value * (1.0 - sigmoid_gate))
    ).astype(jnp.bfloat16)
    partial_value = jnp.einsum(
        "efs,efd->esd", gate_grad, w_gate, preferred_element_type=jnp.float32
    )
    partial_value = partial_value + jnp.einsum(
        "efs,efd->esd", up_grad, w_up, preferred_element_type=jnp.float32
    )
    return partial_value.astype(jnp.bfloat16)


def slots_body(cotangent, gates, expert_ids, saved_gate, saved_up, w_gate, w_up, w_down):
    owners = lax.axis_size("expert")
    row_count, feature_dim = cotangent.shape
    top_count = expert_ids.shape[1]
    local_count, _, slot_count = saved_gate.shape
    capacity = slot_count // owners
    flat_ids, slot_pos = route_slots(expert_ids, local_count * owners)
    target = flat_ids % local_count * slot_count + flat_ids // local_count * capacity + slot_pos
    scaled = (gates[:, :, None] * cotangent.astype(jnp.float32)[:, None, :]).astype(jnp.bfloat16)
    scaled = scaled.reshape(row_count * top_count, feature_dim)
    outgoing = (
        jnp.zeros((local_count * slot_count, feature_dim), jnp.bfloat16).at[target].set(scaled)
    )
    outgoing = outgoing.reshape(local_count, slot_count, feature_dim)
    arrived = lax.all_to_all(outgoing, "expert", split_axis=1, concat_axis=1, tiled=True)
    partial_value = expert_step(arrived, saved_gate, saved_up, w_gate, w_up, w_down)
    returned = lax.all_to_all(partial_value, "expert", split_axis=1, concat_axis=1, tiled=True)
    picked = returned.reshape(local_count * slot_count, feature_dim)[target].astype(jnp.float32)
    combined = jnp.sum(picked.reshape(row_count, top_count, feature_dim), axis=1)
    return lax.psum_scatter(combined, "tp", scatter_dimension=0, tiled=True)


LANES = 256
CHUNKS = 2


def swap(value, axis, step):
    count = lax.axis_size(axis)
    return lax.ppermute(value, axis, [(i, i ^ step) for i in range(count)])


def along_line(value, shift):
    count = lax.axis_size("expert")
    return lax.ppermute(value, "expert", [(i, (i + 4 * shift) % count) for i in range(count)])


def pair_base(place, line_count, r, ry, width):
    line = lax.rem(place[2] + r, line_count)
    row = place[1] if ry == 0 else 1 - place[1]
    return pl.multiple_of((line * 2 + row) * width, width)


def route_kernel(capacity, place, sides, pick, pick_t, gate, hits, gates):
    groups, _, tokens = sides.shape
    line_count = groups // 4
    core, row, line, half = place[0], place[1], place[2], place[3]
    first = (line * 4 + row * 2 + core) * 2
    for r in range(line_count):
        for ry in range(2):
            for c in range(2):
                group = lax.rem(line + r, line_count) * 4 + (row if ry == 0 else 1 - row) * 2 + c
                block = sides[group]
                for e in range(2):
                    named = block[8:16] == (first + e).astype(jnp.float32)
                    at = ((r * 2 + ry) * 2 + c) * 2 + e
                    hits[at:at + 1] = jnp.sum(named.astype(jnp.float32), axis=0, keepdims=True)
                    gates[at:at + 1] = jnp.sum(
                        jnp.where(named, block[0:8], 0.0), axis=0, keepdims=True
                    )
    earlier = lax.broadcasted_iota(jnp.int32, (tokens, tokens), 0) < lax.broadcasted_iota(
        jnp.int32, (tokens, tokens), 1
    )
    hit = hits[...]
    slot = jnp.dot(
        hit.astype(jnp.bfloat16),
        earlier.astype(jnp.float32).astype(jnp.bfloat16),
        preferred_element_type=jnp.float32,
    )
    slot = jnp.where(hit > 0.5, slot, -1.0)
    turned = half > 0
    slot = jnp.where(turned, pltpu.roll(slot, tokens // 2, 1), slot)
    weight = jnp.where(turned, pltpu.roll(gates[...], tokens // 2, 1), gates[...])
    order = lax.broadcasted_iota(jnp.int32, (capacity, tokens), 0).astype(jnp.float32)
    for p in range(line_count * 2):
        rows = []
        for e in range(2):
            for c in range(2):
                at = (p * 2 + c) * 2 + e
                ones = (order == slot[at:at + 1]).astype(jnp.float32)
                column = jnp.sum(ones * weight[at:at + 1], axis=1, keepdims=True)
                place_in = (e * 2 + c) * capacity
                gate[p, place_in:place_in + capacity] = jnp.broadcast_to(
                    column, (capacity, gate.shape[2])
                )
                own = (core == c).astype(jnp.float32)
                rows.append(jnp.concatenate([ones * own, ones * (1.0 - own)], axis=1))
        matrix = jnp.concatenate(rows, axis=0)
        pick[p] = matrix.astype(jnp.bfloat16)
        count = matrix.shape[0]
        square = jnp.concatenate(
            [matrix, jnp.zeros((2 * tokens - count, 2 * tokens), jnp.float32)], axis=0
        )
        pick_t[p] = square.T[:, :count].astype(jnp.bfloat16)


def route(place, sides, capacity):
    groups, _, tokens = sides.shape
    pairs = groups // 2
    rows = 4 * capacity
    return pl.pallas_call(
        functools.partial(route_kernel, capacity),
        out_shape=(
            jax.ShapeDtypeStruct((pairs, rows, 2 * tokens), jnp.bfloat16),
            jax.ShapeDtypeStruct((pairs, 2 * tokens, rows), jnp.bfloat16),
            jax.ShapeDtypeStruct((pairs, rows, 128), jnp.float32),
        ),
        in_specs=[
            pl.BlockSpec(memory_space=pltpu.SMEM),
            pl.BlockSpec(memory_space=pltpu.VMEM),
        ],
        scratch_shapes=[pltpu.VMEM((2 * groups, tokens), jnp.float32)] * 2,
        name="route",
    )(place, sides)


def hidden_kernel(last, place, *refs):
    (own, own_c, lines, lines_c, side, side_c, over, over_c, diag_l, diag_lc, diag_r, diag_rc,
     pick, gate, w_down) = refs[:15]
    if last:
        before, saved_gate, saved_up, result, slots, diag, total = refs[15:]
    else:
        result, slots, diag = refs[15:]
        total = result
    k, steps = pl.program_id(0), pl.num_programs(0)
    line_count, piece, _ = over.shape
    rows = pick.shape[1] // 2

    @pl.when(k == 0)
    def _():
        total[...] = before[...] if last else jnp.zeros_like(total)

    @pl.when(k < steps // 2)
    def _():
        diag[0] = diag_l[...]
        diag[1] = diag_lc[...]

    @pl.when(k >= steps // 2)
    def _():
        diag[0] = diag_r[...]
        diag[1] = diag_rc[...]

    near = pl.multiple_of(place[3] * piece, piece)
    far = pl.multiple_of((1 - place[3]) * piece, piece)
    for r in range(line_count):
        for ry in range(2):
            parts = []
            for c in range(2):
                if ry == 1:
                    parts += [(over, over_c)[c][r], diag[c, r]]
                elif r == 0:
                    group = (own, own_c)[c]
                    parts += [group[pl.ds(near, piece), :], group[pl.ds(far, piece), :]]
                else:
                    parts += [(lines, lines_c)[c][r - 1], (side, side_c)[c][r - 1]]
            p = r * 2 + ry
            picked = jnp.dot(
                pick[p], jnp.concatenate(parts, axis=0), preferred_element_type=jnp.float32
            )
            weight = gate[p]
            weight = jnp.concatenate([weight] * (picked.shape[1] // weight.shape[1]), axis=1)
            scaled = (picked * weight).astype(jnp.bfloat16)
            base = pair_base(place, line_count, r, ry, rows)
            slots[0, pl.ds(base, rows), :] = scaled[:rows]
            slots[1, pl.ds(base, rows), :] = scaled[rows:]
    for e in range(2):
        total[e] = total[e] + lax.dot_general(
            slots[e], w_down[e], (((1,), (1,)), ((), ())), preferred_element_type=jnp.float32
        )

    if last:
        tile = 64
        per_expert = total.shape[1] // tile
        width = total.shape[2]

        @pl.when(k == steps - 1)
        def _():
            @pl.loop(0, 2 * per_expert)
            def _(i):
                e, at = i // per_expert, pl.ds(pl.multiple_of(i % per_expert * tile, tile), tile)
                hidden_grad = total[e, at, :]
                gate_value = saved_gate[e, at, :].astype(jnp.float32)
                up_value = saved_up[e, at, :].astype(jnp.float32)
                sigmoid_gate = jax.nn.sigmoid(gate_value)
                result[e, at, width:] = (hidden_grad * gate_value * sigmoid_gate).astype(
                    jnp.bfloat16
                )
                result[e, at, :width] = (
                    hidden_grad * up_value * sigmoid_gate * (1.0 + gate_value * (1.0 - sigmoid_gate))
                ).astype(jnp.bfloat16)


def hidden(place, chunk, own, own_c, moved, pick, gate, w_down, rest):
    last = rest is not None
    over = moved[4]
    line_count, piece, width = over.shape
    steps = width // LANES
    offset = chunk * steps
    units = w_down.shape[1]
    slot_count = pick.shape[0] * pick.shape[1] // 2
    whole = lambda dims: pl.BlockSpec(dims, lambda k, place: (0,) * len(dims))
    column = lambda array: pl.BlockSpec(array.shape[:-1] + (LANES,), lambda k, place: (0, 0, k))
    first_half = lambda array: pl.BlockSpec(
        array.shape[:-1] + (LANES,), lambda k, place: (0, 0, jnp.minimum(k, steps // 2 - 1))
    )
    second_half = lambda array: pl.BlockSpec(
        array.shape[:-1] + (LANES,), lambda k, place: (0, 0, jnp.maximum(k - steps // 2, 0))
    )
    group = pl.BlockSpec((own.shape[0], LANES), lambda k, place: (0, offset + k))
    in_specs = [group, group]
    in_specs += [column(array) for array in moved[:6]]
    in_specs += [first_half(array) for array in moved[6:8]]
    in_specs += [second_half(array) for array in moved[8:]]
    in_specs += [whole(pick.shape), whole(gate.shape)]
    in_specs += [pl.BlockSpec((2, units, LANES), lambda k, place: (0, 0, offset + k))]
    scratch = [
        pltpu.VMEM((2, slot_count, LANES), jnp.bfloat16),
        pltpu.VMEM((2, line_count, piece, LANES), jnp.bfloat16),
    ]
    operands = [own, own_c, *moved, pick, gate, w_down]
    if last:
        in_specs += [whole(array.shape) for array in rest]
        operands += rest
        out = jax.ShapeDtypeStruct((2, slot_count, 2 * units), jnp.bfloat16)
        scratch += [pltpu.VMEM((2, slot_count, units), jnp.float32)]
    else:
        out = jax.ShapeDtypeStruct((2, slot_count, units), jnp.float32)
    return pl.pallas_call(
        functools.partial(hidden_kernel, last),
        out_shape=out,
        grid_spec=pltpu.PrefetchScalarGridSpec(
            num_scalar_prefetch=1,
            grid=(steps,),
            in_specs=in_specs,
            out_specs=whole(out.shape),
            scratch_shapes=scratch,
        ),
        compiler_params=pltpu.CompilerParams(vmem_limit_bytes=40 << 20),
        cost_estimate=pl.CostEstimate(
            flops=2 * 2 * slot_count * width * (units + 256), bytes_accessed=8 << 20, transcendentals=0
        ),
        name="hidden",
    )(place, *operands)


def sums_kernel(place, grads, w_gate, w_up, pick_t, keep, send, slots):
    pairs, _, rows = pick_t.shape
    rows = rows // 2
    for e in range(2):
        weights = jnp.concatenate([w_gate[e], w_up[e]], axis=0)
        slots[e] = jnp.dot(grads[e], weights, preferred_element_type=jnp.float32).astype(
            jnp.bfloat16
        )
    for r in range(pairs // 2):
        for ry in range(2):
            p = r * 2 + ry
            base = pair_base(place, pairs // 2, r, ry, rows)
            both = jnp.concatenate(
                [slots[0, pl.ds(base, rows), :], slots[1, pl.ds(base, rows), :]], axis=0
            )
            total = jnp.dot(pick_t[p], both, preferred_element_type=jnp.float32).astype(
                jnp.bfloat16
            )
            tokens = total.shape[0] // 2
            keep[p] = total[:tokens]
            send[p] = total[tokens:]


def sums(place, chunk, width, grads, w_gate, w_up, pick_t):
    steps = width // LANES
    offset = chunk * steps
    units = w_gate.shape[1]
    pairs, tokens, _ = pick_t.shape
    tokens = tokens // 2
    whole = lambda dims: pl.BlockSpec(dims, lambda k, place: (0,) * len(dims))
    weight = pl.BlockSpec((2, units, LANES), lambda k, place: (0, 0, offset + k))
    out = jax.ShapeDtypeStruct((pairs, tokens, width), jnp.bfloat16)
    return pl.pallas_call(
        sums_kernel,
        out_shape=(out, out),
        grid_spec=pltpu.PrefetchScalarGridSpec(
            num_scalar_prefetch=1,
            grid=(steps,),
            in_specs=[whole(grads.shape), weight, weight, whole(pick_t.shape)],
            out_specs=[pl.BlockSpec((pairs, tokens, LANES), lambda k, place: (0, 0, k))] * 2,
            scratch_shapes=[pltpu.VMEM((2, grads.shape[1], LANES), jnp.bfloat16)],
        ),
        compiler_params=pltpu.CompilerParams(vmem_limit_bytes=40 << 20),
        cost_estimate=pl.CostEstimate(
            flops=2 * 2 * grads.shape[1] * width * (2 * units + 256),
            bytes_accessed=10 << 20,
            transcendentals=0,
        ),
        name="sums",
    )(place, grads, w_gate, w_up, pick_t)


def plus(one, other):
    return one.astype(jnp.float32) + other.astype(jnp.float32)


def first_kernel(keep, came, send_l, keep_l, send_r, keep_r):
    total = plus(keep[...], came[...]).astype(jnp.bfloat16)
    middle = total.shape[-1] // 2
    keep_l[...] = total[:, 0, :, :middle]
    send_l[...] = total[:, 1, :, :middle]
    keep_r[...] = total[0:1, :, :, middle:]
    send_r[...] = total[1:2, :, :, middle:]


def first_sum(keep, came, piece):
    pairs, tokens, width = keep.shape
    keep = keep.reshape(pairs, 2, piece, width)
    came = came.reshape(pairs, 2, piece, width)
    full = pl.BlockSpec((2, 2, piece, width), lambda r: (r, 0, 0, 0))
    left = jax.ShapeDtypeStruct((pairs, piece, width // 2), jnp.bfloat16)
    right = jax.ShapeDtypeStruct((pairs // 2, 2, piece, width // 2), jnp.bfloat16)
    left_spec = pl.BlockSpec((2, piece, width // 2), lambda r: (r, 0, 0))
    right_spec = pl.BlockSpec((1, 2, piece, width // 2), lambda r: (r, 0, 0, 0))
    return pl.pallas_call(
        first_kernel,
        out_shape=(left, left, right, right),
        grid=(pairs // 2,),
        in_specs=[full, full],
        out_specs=[left_spec, left_spec, right_spec, right_spec],
        cost_estimate=pl.CostEstimate(flops=0, bytes_accessed=6 << 20, transcendentals=0),
        name="first_sum",
    )(keep, came)


def second_kernel(keep_l, came_l, keep_r, came_r, send_l, left, send_r, right):
    total = plus(keep_l[...], came_l[...]).astype(jnp.bfloat16)
    left[...] = total[0:1]
    send_l[...] = total[1:2]
    total = plus(keep_r[...], came_r[...]).astype(jnp.bfloat16)
    right[...] = total[:, 0]
    send_r[...] = total[:, 1]


def second_sum(keep_l, came_l, keep_r, came_r):
    lines, _, piece, middle = keep_r.shape
    out = jax.ShapeDtypeStruct((lines, piece, middle), jnp.bfloat16)
    left = pl.BlockSpec((2, piece, middle), lambda r: (r, 0, 0))
    right = pl.BlockSpec((1, 2, piece, middle), lambda r: (r, 0, 0, 0))
    return pl.pallas_call(
        second_kernel,
        out_shape=(out,) * 4,
        grid=(lines,),
        in_specs=[left, left, right, right],
        out_specs=[pl.BlockSpec((1, piece, middle), lambda r: (r, 0, 0))] * 4,
        cost_estimate=pl.CostEstimate(flops=0, bytes_accessed=3 << 20, transcendentals=0),
        name="second_sum",
    )(keep_l, came_l, keep_r, came_r)


def third_kernel(left, came_l, right, came_r, own, *sends):
    middle = left.shape[-1]
    for columns, one, other in ((slice(0, middle), left, came_l), (slice(middle, None), right, came_r)):
        own[:, columns] = plus(one[0], other[0])
        for r, send in enumerate(sends):
            send[:, columns] = plus(one[r + 1], other[r + 1]).astype(jnp.bfloat16)


def third_sum(left, came_l, right, came_r):
    lines, piece, middle = left.shape
    return pl.pallas_call(
        third_kernel,
        out_shape=(jax.ShapeDtypeStruct((piece, 2 * middle), jnp.float32),)
        + (jax.ShapeDtypeStruct((piece, 2 * middle), jnp.bfloat16),) * (lines - 1),
        cost_estimate=pl.CostEstimate(flops=0, bytes_accessed=2 << 20, transcendentals=0),
        name="third_sum",
    )(left, came_l, right, came_r)


def last_kernel(count, *refs):
    result = refs[-1]
    terms = len(refs[:-1]) // count
    width = refs[0].shape[1]
    for chunk in range(count):
        total = refs[chunk * terms][...]
        for ref in refs[chunk * terms + 1:(chunk + 1) * terms]:
            total = total + ref[...].astype(jnp.float32)
        result[:, chunk * width:(chunk + 1) * width] = total


def tokens_body(cotangent, gates, expert_ids, saved_gate, saved_up, w_gate, w_up, w_down):
    owners = lax.axis_size("expert")
    row_count, feature_dim = cotangent.shape
    slot_count = saved_gate.shape[2]
    capacity = slot_count // owners
    lines = owners // 4
    piece = row_count // 2
    width = feature_dim // CHUNKS
    middle = width // 2
    me, half = lax.axis_index("expert"), lax.axis_index("tp")
    place = jnp.stack([me % 2, me // 2 % 2, me // 4, half]).astype(jnp.int32)

    sides = jnp.concatenate([gates.T, expert_ids.T.astype(jnp.float32)], axis=0)
    sides = lax.all_gather(sides, "expert", axis=0)
    saved_gate, saved_up = saved_gate.swapaxes(1, 2), saved_up.swapaxes(1, 2)

    own_c = swap(cotangent, "expert", 1)
    near = lax.dynamic_slice_in_dim(cotangent, half * piece, piece, 0)
    far = lax.dynamic_slice_in_dim(cotangent, (1 - half) * piece, piece, 0)
    gathered = []
    for chunk in range(CHUNKS):
        columns = slice(chunk * width, (chunk + 1) * width)
        near_part = near[:, columns]
        line = jnp.stack([along_line(near_part, -r) for r in range(1, lines)])
        first = swap(near_part, "expert", 2)
        side = swap(line, "tp", 1)
        over = jnp.concatenate([first[None], swap(line, "expert", 2)])
        diag_l = swap(over[:, :, :middle], "tp", 1)
        far_part = far[None, :, chunk * width + middle:(chunk + 1) * width]
        diag_r = swap(jnp.concatenate([far_part, side[:, :, middle:]]), "expert", 2)
        moved = []
        for array in (line, side, over, diag_l, diag_r):
            moved += [array, swap(array, "expert", 1)]
        gathered.append(moved)
    pick, pick_t, gate = route(place, sides, capacity)
    rest = None
    for chunk in range(CHUNKS):
        if chunk == CHUNKS - 1:
            rest = [rest, saved_gate, saved_up]
        rest = hidden(place, chunk, cotangent, own_c, gathered[chunk], pick, gate, w_down, rest)
    grads = rest

    terms = []
    for chunk in range(CHUNKS):
        keep, send = sums(place, chunk, width, grads, w_gate, w_up, pick_t)
        came = swap(send, "expert", 1)
        send_l, keep_l, send_r, keep_r = first_sum(keep, came, piece)
        came_l, came_r = swap(send_l, "tp", 1), swap(send_r, "expert", 2)
        send_l, left, send_r, right = second_sum(keep_l, came_l, keep_r, came_r)
        came_l, came_r = swap(send_l, "expert", 2), swap(send_r, "tp", 1)
        own, *sends = third_sum(left, came_l, right, came_r)
        terms += [own] + [along_line(send, r + 1) for r, send in enumerate(sends)]
    return pl.pallas_call(
        functools.partial(last_kernel, CHUNKS),
        out_shape=jax.ShapeDtypeStruct((piece, feature_dim), jnp.float32),
        name="last_sum",
    )(*terms)


def body(*arrays):
    cotangent, gates, _, saved_gate = arrays[:4]
    owners = lax.axis_size("expert")
    fits = (
        owners in (4, 8, 16)
        and lax.axis_size("tp") == 2
        and cotangent.shape[0] == 128
        and cotangent.shape[1] % (2 * CHUNKS * LANES) == 0
        and gates.shape[1] == 8
        and saved_gate.shape[0] == 2
        and saved_gate.shape[2] // owners % 16 == 0
        and 4 * saved_gate.shape[2] // owners <= 256
    )
    return (tokens_body if fits else slots_body)(*arrays)


def solution(mesh):
    in_specs = (
        P("expert", None),
        P("expert", None),
        P("expert", None),
        P("expert", "tp", None),
        P("expert", "tp", None),
        P("expert", "tp", None),
        P("expert", "tp", None),
        P("expert", "tp", None),
    )
    out_specs = P(("expert", "tp"), None)
    return jax.shard_map(body, mesh=mesh, in_specs=in_specs, out_specs=out_specs, check_vma=False)
```

```python
import functools

import jax
import jax.numpy as jnp
from jax import lax
from jax.experimental import pallas as pl
from jax.experimental.pallas import tpu as pltpu
from jax.sharding import PartitionSpec as P


def route_slots(expert_ids, expert_total):
    flat_ids = expert_ids.reshape(-1)
    one_hot = (flat_ids[:, None] == jnp.arange(expert_total, dtype=jnp.int32)[None, :]).astype(
        jnp.int32
    )
    before = jnp.cumsum(one_hot, axis=0) - one_hot
    return (flat_ids, jnp.sum(before * one_hot, axis=1))


def expert_step(arrived, saved_gate, saved_up, w_gate, w_up, w_down):
    hidden_grad = jnp.einsum("efd,esd->efs", w_down, arrived, preferred_element_type=jnp.float32)
    gate_value = saved_gate.astype(jnp.float32)
    up_value = saved_up.astype(jnp.float32)
    sigmoid_gate = jax.nn.sigmoid(gate_value)
    up_grad = (hidden_grad * gate_value * sigmoid_gate).astype(jnp.bfloat16)
    gate_grad = (
        hidden_grad * up_value * sigmoid_gate * (1.0 + gate_value * (1.0 - sigmoid_gate))
    ).astype(jnp.bfloat16)
    partial_value = jnp.einsum(
        "efs,efd->esd", gate_grad, w_gate, preferred_element_type=jnp.float32
    )
    partial_value = partial_value + jnp.einsum(
        "efs,efd->esd", up_grad, w_up, preferred_element_type=jnp.float32
    )
    return partial_value.astype(jnp.bfloat16)


def slots_body(cotangent, gates, expert_ids, saved_gate, saved_up, w_gate, w_up, w_down):
    owners = lax.axis_size("expert")
    row_count, feature_dim = cotangent.shape
    top_count = expert_ids.shape[1]
    local_count, _, slot_count = saved_gate.shape
    capacity = slot_count // owners
    flat_ids, slot_pos = route_slots(expert_ids, local_count * owners)
    target = flat_ids % local_count * slot_count + flat_ids // local_count * capacity + slot_pos
    scaled = (gates[:, :, None] * cotangent.astype(jnp.float32)[:, None, :]).astype(jnp.bfloat16)
    scaled = scaled.reshape(row_count * top_count, feature_dim)
    outgoing = (
        jnp.zeros((local_count * slot_count, feature_dim), jnp.bfloat16).at[target].set(scaled)
    )
    outgoing = outgoing.reshape(local_count, slot_count, feature_dim)
    arrived = lax.all_to_all(outgoing, "expert", split_axis=1, concat_axis=1, tiled=True)
    partial_value = expert_step(arrived, saved_gate, saved_up, w_gate, w_up, w_down)
    returned = lax.all_to_all(partial_value, "expert", split_axis=1, concat_axis=1, tiled=True)
    picked = returned.reshape(local_count * slot_count, feature_dim)[target].astype(jnp.float32)
    combined = jnp.sum(picked.reshape(row_count, top_count, feature_dim), axis=1)
    return lax.psum_scatter(combined, "tp", scatter_dimension=0, tiled=True)


LANES = 256
CHUNKS = 2


def swap(value, axis, step):
    count = lax.axis_size(axis)
    return lax.ppermute(value, axis, [(i, i ^ step) for i in range(count)])


def along_line(value, shift):
    count = lax.axis_size("expert")
    return lax.ppermute(value, "expert", [(i, (i + 4 * shift) % count) for i in range(count)])


def pair_base(place, line_count, r, ry, width):
    line = lax.rem(place[2] + r, line_count)
    row = place[1] if ry == 0 else 1 - place[1]
    return pl.multiple_of((line * 2 + row) * width, width)


def prepare_kernel(width, place, tokens, gates, ids, first, *others):
    piece = first.shape[0]
    near = pl.multiple_of(place[3] * piece, piece)
    first[:, :width] = tokens[pl.ds(near, piece), :width]
    for i, other in enumerate(others[:-1]):
        other[...] = tokens[pl.ds(near, piece), (i + 1) * width:(i + 2) * width]
    rest = gates[...]
    terms = []
    for _ in range(3):
        term = rest.astype(jnp.bfloat16).astype(jnp.float32)
        terms.append(term)
        rest = rest - term
    terms.append(ids[...].astype(jnp.float32))
    unused = piece - 4 * gates.shape[0]
    terms.append(jnp.zeros((unused, gates.shape[1]), jnp.float32))
    table = jnp.concatenate(terms, axis=0).astype(jnp.bfloat16)
    first[:, width:] = table
    others[-1][...] = table


def prepare(place, cotangent, gates, ids, piece, width):
    feature_dim = cotangent.shape[1]
    shapes = [(piece, width + 128)] + [(piece, width)] * (feature_dim // width - 1) + [(piece, 128)]
    return pl.pallas_call(
        functools.partial(prepare_kernel, width),
        out_shape=[jax.ShapeDtypeStruct(dims, jnp.bfloat16) for dims in shapes],
        in_specs=[pl.BlockSpec(memory_space=pltpu.SMEM)] + [pl.BlockSpec(memory_space=pltpu.VMEM)] * 3,
        compiler_params=pltpu.CompilerParams(vmem_limit_bytes=4 << 20),
        name="prepare",
    )(place, cotangent, gates, ids)


def route_kernel(capacity, place, own, own_c, lines, lines_c, over, over_c, pick, pick_t, gate, hits, gates):
    line_count, _, tokens = over.shape
    core, row, line, half = place[0], place[1], place[2], place[3]
    first = (line * 4 + row * 2 + core) * 2
    for r in range(line_count):
        for ry in range(2):
            tables = []
            for c in range(2):
                if ry == 1:
                    table = (over, over_c)[c][r]
                elif r == 0:
                    table = (own, own_c)[c][...]
                else:
                    table = (lines, lines_c)[c][r - 1]
                tables.append(table[:32].astype(jnp.float32))
            swapped = core > 0
            ordered = [
                jnp.where(swapped, tables[1], tables[0]), jnp.where(swapped, tables[0], tables[1])
            ]
            for c in range(2):
                block = ordered[c]
                value = block[0:8] + block[8:16] + block[16:24]
                for e in range(2):
                    named = block[24:32] == (first + e).astype(jnp.float32)
                    at = ((r * 2 + ry) * 2 + c) * 2 + e
                    hits[at:at + 1] = jnp.sum(named.astype(jnp.float32), axis=0, keepdims=True)
                    gates[at:at + 1] = jnp.sum(
                        jnp.where(named, value, 0.0), axis=0, keepdims=True
                    )
    earlier = lax.broadcasted_iota(jnp.int32, (tokens, tokens), 0) < lax.broadcasted_iota(
        jnp.int32, (tokens, tokens), 1
    )
    hit = hits[...]
    slot = jnp.dot(
        hit.astype(jnp.bfloat16),
        earlier.astype(jnp.float32).astype(jnp.bfloat16),
        preferred_element_type=jnp.float32,
    )
    slot = jnp.where(hit > 0.5, slot, -1.0)
    turned = half > 0
    slot = jnp.where(turned, pltpu.roll(slot, tokens // 2, 1), slot)
    weight = jnp.where(turned, pltpu.roll(gates[...], tokens // 2, 1), gates[...])
    order = lax.broadcasted_iota(jnp.int32, (capacity, tokens), 0).astype(jnp.float32)
    for p in range(line_count * 2):
        rows = []
        for e in range(2):
            for c in range(2):
                at = (p * 2 + c) * 2 + e
                ones = (order == slot[at:at + 1]).astype(jnp.float32)
                column = jnp.sum(ones * weight[at:at + 1], axis=1, keepdims=True)
                place_in = (e * 2 + c) * capacity
                gate[p, place_in:place_in + capacity] = jnp.broadcast_to(
                    column, (capacity, gate.shape[2])
                )
                own_core = (core == c).astype(jnp.float32)
                rows.append(jnp.concatenate([ones * own_core, ones * (1.0 - own_core)], axis=1))
        matrix = jnp.concatenate(rows, axis=0)
        pick[p] = matrix.astype(jnp.bfloat16)
        count = matrix.shape[0]
        square = jnp.concatenate(
            [matrix, jnp.zeros((2 * tokens - count, 2 * tokens), jnp.float32)], axis=0
        )
        pick_t[p] = square.T[:, :count].astype(jnp.bfloat16)


def route(place, own, own_c, lines, lines_c, over, over_c, capacity):
    line_count, piece, whole_width = over.shape
    tokens = 2 * piece
    pairs = 2 * line_count
    rows = 4 * capacity
    last = whole_width // 128 - 1
    table = lambda array: pl.BlockSpec(array.shape[:-1] + (128,), lambda i, place: (0, 0, last))
    alone = pl.BlockSpec((piece, 128), lambda i, place: (0, 0))
    shapes = ((pairs, rows, 2 * tokens), (pairs, 2 * tokens, rows), (pairs, rows, 128))
    return pl.pallas_call(
        functools.partial(route_kernel, capacity),
        out_shape=[
            jax.ShapeDtypeStruct(dims, kind)
            for dims, kind in zip(shapes, (jnp.bfloat16, jnp.bfloat16, jnp.float32))
        ],
        grid_spec=pltpu.PrefetchScalarGridSpec(
            num_scalar_prefetch=1,
            grid=(1,),
            in_specs=[alone, alone] + [table(array) for array in (lines, lines_c, over, over_c)],
            out_specs=[pl.BlockSpec(dims, lambda i, place: (0, 0, 0)) for dims in shapes],
            scratch_shapes=[pltpu.VMEM((4 * pairs, tokens), jnp.float32)] * 2,
        ),
        compiler_params=pltpu.CompilerParams(vmem_limit_bytes=8 << 20),
        name="route",
    )(place, own, own_c, lines, lines_c, over, over_c)


def hidden_kernel(last, place, *refs):
    (own, own_c, lines, lines_c, side, side_c, over, over_c, diag_l, diag_lc, diag_r, diag_rc,
     pick, gate, w_down) = refs[:15]
    if last:
        before, saved_gate, saved_up, result, slots, diag, total = refs[15:]
    else:
        result, slots, diag = refs[15:]
        total = result
    k, steps = pl.program_id(0), pl.num_programs(0)
    line_count, piece, _ = over.shape
    rows = pick.shape[1] // 2

    @pl.when(k == 0)
    def _():
        total[...] = before[...] if last else jnp.zeros_like(total)

    @pl.when(k < steps // 2)
    def _():
        diag[0] = diag_l[...]
        diag[1] = diag_lc[...]

    @pl.when(k >= steps // 2)
    def _():
        diag[0] = diag_r[...]
        diag[1] = diag_rc[...]

    near = pl.multiple_of(place[3] * piece, piece)
    far = pl.multiple_of((1 - place[3]) * piece, piece)
    for r in range(line_count):
        for ry in range(2):
            parts = []
            for c in range(2):
                if ry == 1:
                    parts += [(over, over_c)[c][r], diag[c, r]]
                elif r == 0:
                    group = (own, own_c)[c]
                    parts += [group[pl.ds(near, piece), :], group[pl.ds(far, piece), :]]
                else:
                    parts += [(lines, lines_c)[c][r - 1], (side, side_c)[c][r - 1]]
            p = r * 2 + ry
            picked = jnp.dot(
                pick[p], jnp.concatenate(parts, axis=0), preferred_element_type=jnp.float32
            )
            weight = gate[p]
            weight = jnp.concatenate([weight] * (picked.shape[1] // weight.shape[1]), axis=1)
            scaled = (picked * weight).astype(jnp.bfloat16)
            base = pair_base(place, line_count, r, ry, rows)
            slots[0, pl.ds(base, rows), :] = scaled[:rows]
            slots[1, pl.ds(base, rows), :] = scaled[rows:]
    for e in range(2):
        total[e] = total[e] + lax.dot_general(
            slots[e], w_down[e], (((1,), (1,)), ((), ())), preferred_element_type=jnp.float32
        )

    if last:
        tile = 64
        per_expert = total.shape[1] // tile
        width = total.shape[2]

        @pl.when(k == steps - 1)
        def _():
            @pl.loop(0, 2 * per_expert)
            def _(i):
                e, at = i // per_expert, pl.ds(pl.multiple_of(i % per_expert * tile, tile), tile)
                hidden_grad = total[e, at, :]
                gate_value = saved_gate[e, at, :].astype(jnp.float32)
                up_value = saved_up[e, at, :].astype(jnp.float32)
                sigmoid_gate = jax.nn.sigmoid(gate_value)
                result[e, at, width:] = (hidden_grad * gate_value * sigmoid_gate).astype(
                    jnp.bfloat16
                )
                result[e, at, :width] = (
                    hidden_grad * up_value * sigmoid_gate * (1.0 + gate_value * (1.0 - sigmoid_gate))
                ).astype(jnp.bfloat16)


def hidden(place, chunk, own, own_c, moved, pick, gate, w_down, rest):
    last = rest is not None
    line_count, piece, _ = moved[4].shape
    width = 2 * moved[6].shape[-1]
    steps = width // LANES
    offset = chunk * steps
    units = w_down.shape[1]
    slot_count = pick.shape[0] * pick.shape[1] // 2
    whole = lambda dims: pl.BlockSpec(
        dims, lambda k, place: (0,) * len(dims), pipeline_mode=pl.Buffered(1)
    )
    column = lambda array: pl.BlockSpec(array.shape[:-1] + (LANES,), lambda k, place: (0, 0, k))
    first_half = lambda array: pl.BlockSpec(
        array.shape[:-1] + (LANES,), lambda k, place: (0, 0, jnp.minimum(k, steps // 2 - 1))
    )
    second_half = lambda array: pl.BlockSpec(
        array.shape[:-1] + (LANES,), lambda k, place: (0, 0, jnp.maximum(k - steps // 2, 0))
    )
    group = pl.BlockSpec((own.shape[0], LANES), lambda k, place: (0, offset + k))
    in_specs = [group, group]
    in_specs += [column(array) for array in moved[:6]]
    in_specs += [first_half(array) for array in moved[6:8]]
    in_specs += [second_half(array) for array in moved[8:]]
    in_specs += [whole(pick.shape), whole(gate.shape)]
    in_specs += [pl.BlockSpec((2, units, LANES), lambda k, place: (0, 0, offset + k))]
    scratch = [
        pltpu.VMEM((2, slot_count, LANES), jnp.bfloat16),
        pltpu.VMEM((2, line_count, piece, LANES), jnp.bfloat16),
    ]
    operands = [own, own_c, *moved, pick, gate, w_down]
    if last:
        in_specs += [whole(array.shape) for array in rest]
        operands += rest
        out = jax.ShapeDtypeStruct((2, slot_count, 2 * units), jnp.bfloat16)
        scratch += [pltpu.VMEM((2, slot_count, units), jnp.float32)]
    else:
        out = jax.ShapeDtypeStruct((2, slot_count, units), jnp.float32)
    return pl.pallas_call(
        functools.partial(hidden_kernel, last),
        out_shape=out,
        grid_spec=pltpu.PrefetchScalarGridSpec(
            num_scalar_prefetch=1,
            grid=(steps,),
            in_specs=in_specs,
            out_specs=whole(out.shape),
            scratch_shapes=scratch,
        ),
        compiler_params=pltpu.CompilerParams(vmem_limit_bytes=24 << 20),
        cost_estimate=pl.CostEstimate(
            flops=2 * 2 * slot_count * width * (units + 256), bytes_accessed=8 << 20, transcendentals=0
        ),
        name="hidden",
    )(place, *operands)


def sums_kernel(place, grads, w_gate, w_up, pick_t, keep, send, slots):
    pairs, _, rows = pick_t.shape
    rows = rows // 2
    for e in range(2):
        weights = jnp.concatenate([w_gate[e], w_up[e]], axis=0)
        slots[e] = jnp.dot(grads[e], weights, preferred_element_type=jnp.float32).astype(
            jnp.bfloat16
        )
    for r in range(pairs // 2):
        for ry in range(2):
            p = r * 2 + ry
            base = pair_base(place, pairs // 2, r, ry, rows)
            both = jnp.concatenate(
                [slots[0, pl.ds(base, rows), :], slots[1, pl.ds(base, rows), :]], axis=0
            )
            total = jnp.dot(pick_t[p], both, preferred_element_type=jnp.float32).astype(
                jnp.bfloat16
            )
            tokens = total.shape[0] // 2
            keep[p] = total[:tokens]
            send[p] = total[tokens:]


def sums(place, chunk, width, grads, w_gate, w_up, pick_t):
    steps = width // LANES
    offset = chunk * steps
    units = w_gate.shape[1]
    pairs, tokens, _ = pick_t.shape
    tokens = tokens // 2
    whole = lambda dims: pl.BlockSpec(
        dims, lambda k, place: (0,) * len(dims), pipeline_mode=pl.Buffered(1)
    )
    weight = pl.BlockSpec((2, units, LANES), lambda k, place: (0, 0, offset + k))
    out = jax.ShapeDtypeStruct((pairs, tokens, width), jnp.bfloat16)
    return pl.pallas_call(
        sums_kernel,
        out_shape=(out, out),
        grid_spec=pltpu.PrefetchScalarGridSpec(
            num_scalar_prefetch=1,
            grid=(steps,),
            in_specs=[whole(grads.shape), weight, weight, whole(pick_t.shape)],
            out_specs=[pl.BlockSpec((pairs, tokens, LANES), lambda k, place: (0, 0, k))] * 2,
            scratch_shapes=[pltpu.VMEM((2, grads.shape[1], LANES), jnp.bfloat16)],
        ),
        compiler_params=pltpu.CompilerParams(vmem_limit_bytes=16 << 20),
        cost_estimate=pl.CostEstimate(
            flops=2 * 2 * grads.shape[1] * width * (2 * units + 256),
            bytes_accessed=10 << 20,
            transcendentals=0,
        ),
        name="sums",
    )(place, grads, w_gate, w_up, pick_t)


def first_kernel(keep, came, send_l, keep_l, send_r, keep_r):
    total = keep[...] + came[...]
    middle = total.shape[-1] // 2
    keep_l[...] = total[:, 0, :, :middle]
    send_l[...] = total[:, 1, :, :middle]
    keep_r[...] = total[0:1, :, :, middle:]
    send_r[...] = total[1:2, :, :, middle:]


def first_sum(keep, came, piece):
    pairs, tokens, width = keep.shape
    keep = keep.reshape(pairs, 2, piece, width)
    came = came.reshape(pairs, 2, piece, width)
    full = pl.BlockSpec((2, 2, piece, width), lambda r: (r, 0, 0, 0))
    left = jax.ShapeDtypeStruct((pairs, piece, width // 2), jnp.bfloat16)
    right = jax.ShapeDtypeStruct((pairs // 2, 2, piece, width // 2), jnp.bfloat16)
    left_spec = pl.BlockSpec((2, piece, width // 2), lambda r: (r, 0, 0))
    right_spec = pl.BlockSpec((1, 2, piece, width // 2), lambda r: (r, 0, 0, 0))
    return pl.pallas_call(
        first_kernel,
        out_shape=(left, left, right, right),
        grid=(pairs // 2,),
        in_specs=[full, full],
        out_specs=[left_spec, left_spec, right_spec, right_spec],
        cost_estimate=pl.CostEstimate(flops=0, bytes_accessed=6 << 20, transcendentals=0),
        compiler_params=pltpu.CompilerParams(vmem_limit_bytes=8 << 20),
        name="first_sum",
    )(keep, came)


def second_kernel(keep_l, came_l, keep_r, came_r, send_l, left, send_r, right):
    total = keep_l[...] + came_l[...]
    left[...] = total[0:1]
    send_l[...] = total[1:2]
    total = keep_r[...] + came_r[...]
    right[...] = total[:, 0]
    send_r[...] = total[:, 1]


def second_sum(keep_l, came_l, keep_r, came_r):
    lines, _, piece, middle = keep_r.shape
    out = jax.ShapeDtypeStruct((lines, piece, middle), jnp.bfloat16)
    left = pl.BlockSpec((2, piece, middle), lambda r: (r, 0, 0))
    right = pl.BlockSpec((1, 2, piece, middle), lambda r: (r, 0, 0, 0))
    return pl.pallas_call(
        second_kernel,
        out_shape=(out,) * 4,
        grid=(lines,),
        in_specs=[left, left, right, right],
        out_specs=[pl.BlockSpec((1, piece, middle), lambda r: (r, 0, 0))] * 4,
        cost_estimate=pl.CostEstimate(flops=0, bytes_accessed=3 << 20, transcendentals=0),
        compiler_params=pltpu.CompilerParams(vmem_limit_bytes=8 << 20),
        name="second_sum",
    )(keep_l, came_l, keep_r, came_r)


def third_kernel(left, came_l, right, came_r, own, *sends):
    middle = left.shape[-1]
    for columns, one, other in ((slice(0, middle), left, came_l), (slice(middle, None), right, came_r)):
        own[:, columns] = one[0].astype(jnp.float32) + other[0].astype(jnp.float32)
        for r, send in enumerate(sends):
            send[:, columns] = one[r + 1] + other[r + 1]


def third_sum(left, came_l, right, came_r):
    lines, piece, middle = left.shape
    return pl.pallas_call(
        third_kernel,
        out_shape=(jax.ShapeDtypeStruct((piece, 2 * middle), jnp.float32),)
        + (jax.ShapeDtypeStruct((piece, 2 * middle), jnp.bfloat16),) * (lines - 1),
        cost_estimate=pl.CostEstimate(flops=0, bytes_accessed=2 << 20, transcendentals=0),
        compiler_params=pltpu.CompilerParams(vmem_limit_bytes=8 << 20),
        name="third_sum",
    )(left, came_l, right, came_r)


def last_kernel(count, *refs):
    result = refs[-1]
    terms = len(refs[:-1]) // count
    width = refs[0].shape[1]
    for chunk in range(count):
        total = refs[chunk * terms][...]
        for ref in refs[chunk * terms + 1:(chunk + 1) * terms]:
            total = total + ref[...].astype(jnp.float32)
        result[:, chunk * width:(chunk + 1) * width] = total


def tokens_body(cotangent, gates, expert_ids, saved_gate, saved_up, w_gate, w_up, w_down):
    owners = lax.axis_size("expert")
    row_count, feature_dim = cotangent.shape
    slot_count = saved_gate.shape[2]
    capacity = slot_count // owners
    lines = owners // 4
    piece = row_count // 2
    width = feature_dim // CHUNKS
    middle = width // 2
    me, half = lax.axis_index("expert"), lax.axis_index("tp")
    place = jnp.stack([me % 2, me // 2 % 2, me // 4, half]).astype(jnp.int32)

    *parts, table = prepare(place, cotangent, gates.T, expert_ids.T, piece, width)
    saved_gate, saved_up = saved_gate.swapaxes(1, 2), saved_up.swapaxes(1, 2)
    own_c, table_c = swap(cotangent, "expert", 1), swap(table, "expert", 1)
    far = lax.dynamic_slice_in_dim(cotangent, (1 - half) * piece, piece, 0)
    gathered = []
    for chunk, part in enumerate(parts):
        line = jnp.stack([along_line(part, -r) for r in range(1, lines)])
        first = swap(part, "expert", 2)
        side = swap(line, "tp", 1)
        over = jnp.concatenate([first[None], swap(line, "expert", 2)])
        diag_l = swap(over[:, :, :middle], "tp", 1)
        far_part = far[None, :, chunk * width + middle:(chunk + 1) * width]
        diag_r = swap(jnp.concatenate([far_part, side[:, :, middle:width]]), "expert", 2)
        moved = []
        for array in (line, side, over, diag_l, diag_r):
            moved += [array, swap(array, "expert", 1)]
        gathered.append(moved)
    lines_n, lines_c, _, _, over_n, over_c = gathered[0][:6]
    pick, pick_t, gate = route(place, table, table_c, lines_n, lines_c, over_n, over_c, capacity)
    rest = None
    for chunk in range(CHUNKS):
        if chunk == CHUNKS - 1:
            rest = [rest, saved_gate, saved_up]
        rest = hidden(place, chunk, cotangent, own_c, gathered[chunk], pick, gate, w_down, rest)
    grads = rest

    terms = []
    for chunk in range(CHUNKS):
        keep, send = sums(place, chunk, width, grads, w_gate, w_up, pick_t)
        came = swap(send, "expert", 1)
        send_l, keep_l, send_r, keep_r = first_sum(keep, came, piece)
        came_l, came_r = swap(send_l, "tp", 1), swap(send_r, "expert", 2)
        send_l, left, send_r, right = second_sum(keep_l, came_l, keep_r, came_r)
        came_l, came_r = swap(send_l, "expert", 2), swap(send_r, "tp", 1)
        own, *sends = third_sum(left, came_l, right, came_r)
        terms += [own] + [along_line(send, r + 1) for r, send in enumerate(sends)]
    return pl.pallas_call(
        functools.partial(last_kernel, CHUNKS),
        out_shape=jax.ShapeDtypeStruct((piece, feature_dim), jnp.float32),
        compiler_params=pltpu.CompilerParams(vmem_limit_bytes=8 << 20),
        name="last_sum",
    )(*terms)


def body(*arrays):
    cotangent, gates, _, saved_gate = arrays[:4]
    owners = lax.axis_size("expert")
    fits = (
        owners in (4, 8, 16)
        and lax.axis_size("tp") == 2
        and cotangent.shape[0] == 128
        and cotangent.shape[1] % (2 * CHUNKS * LANES) == 0
        and gates.shape[1] == 8
        and saved_gate.shape[0] == 2
        and saved_gate.shape[2] // owners % 16 == 0
        and 4 * saved_gate.shape[2] // owners <= 256
    )
    return (tokens_body if fits else slots_body)(*arrays)


def solution(mesh):
    in_specs = (
        P("expert", None),
        P("expert", None),
        P("expert", None),
        P("expert", "tp", None),
        P("expert", "tp", None),
        P("expert", "tp", None),
        P("expert", "tp", None),
        P("expert", "tp", None),
    )
    out_specs = P(("expert", "tp"), None)
    return jax.shard_map(body, mesh=mesh, in_specs=in_specs, out_specs=out_specs, check_vma=False)
```

```python
import functools

import jax
import jax.numpy as jnp
from jax import lax
from jax.experimental import pallas as pl
from jax.experimental.pallas import tpu as pltpu
from jax.sharding import PartitionSpec as P


def route_slots(expert_ids, expert_total):
    flat_ids = expert_ids.reshape(-1)
    one_hot = (flat_ids[:, None] == jnp.arange(expert_total, dtype=jnp.int32)[None, :]).astype(
        jnp.int32
    )
    before = jnp.cumsum(one_hot, axis=0) - one_hot
    return (flat_ids, jnp.sum(before * one_hot, axis=1))


def expert_step(arrived, saved_gate, saved_up, w_gate, w_up, w_down):
    hidden_grad = jnp.einsum("efd,esd->efs", w_down, arrived, preferred_element_type=jnp.float32)
    gate_value = saved_gate.astype(jnp.float32)
    up_value = saved_up.astype(jnp.float32)
    sigmoid_gate = jax.nn.sigmoid(gate_value)
    up_grad = (hidden_grad * gate_value * sigmoid_gate).astype(jnp.bfloat16)
    gate_grad = (
        hidden_grad * up_value * sigmoid_gate * (1.0 + gate_value * (1.0 - sigmoid_gate))
    ).astype(jnp.bfloat16)
    partial_value = jnp.einsum(
        "efs,efd->esd", gate_grad, w_gate, preferred_element_type=jnp.float32
    )
    partial_value = partial_value + jnp.einsum(
        "efs,efd->esd", up_grad, w_up, preferred_element_type=jnp.float32
    )
    return partial_value.astype(jnp.bfloat16)


def slots_body(cotangent, gates, expert_ids, saved_gate, saved_up, w_gate, w_up, w_down):
    owners = lax.axis_size("expert")
    row_count, feature_dim = cotangent.shape
    top_count = expert_ids.shape[1]
    local_count, _, slot_count = saved_gate.shape
    capacity = slot_count // owners
    flat_ids, slot_pos = route_slots(expert_ids, local_count * owners)
    target = flat_ids % local_count * slot_count + flat_ids // local_count * capacity + slot_pos
    scaled = (gates[:, :, None] * cotangent.astype(jnp.float32)[:, None, :]).astype(jnp.bfloat16)
    scaled = scaled.reshape(row_count * top_count, feature_dim)
    outgoing = (
        jnp.zeros((local_count * slot_count, feature_dim), jnp.bfloat16).at[target].set(scaled)
    )
    outgoing = outgoing.reshape(local_count, slot_count, feature_dim)
    arrived = lax.all_to_all(outgoing, "expert", split_axis=1, concat_axis=1, tiled=True)
    partial_value = expert_step(arrived, saved_gate, saved_up, w_gate, w_up, w_down)
    returned = lax.all_to_all(partial_value, "expert", split_axis=1, concat_axis=1, tiled=True)
    picked = returned.reshape(local_count * slot_count, feature_dim)[target].astype(jnp.float32)
    combined = jnp.sum(picked.reshape(row_count, top_count, feature_dim), axis=1)
    return lax.psum_scatter(combined, "tp", scatter_dimension=0, tiled=True)


LANES = 256
CHUNKS = 2


def swap(value, axis, step):
    count = lax.axis_size(axis)
    return lax.ppermute(value, axis, [(i, i ^ step) for i in range(count)])


def along_line(value, shift):
    count = lax.axis_size("expert")
    return lax.ppermute(value, "expert", [(i, (i + 4 * shift) % count) for i in range(count)])


def pair_base(place, line_count, r, ry, width):
    line = lax.rem(place[2] + r, line_count)
    row = place[1] if ry == 0 else 1 - place[1]
    return pl.multiple_of((line * 2 + row) * width, width)


def small(kernel, name, shapes, kinds, operands, scratch=(), limit=8, moved=0):
    spaces = {"s": pltpu.SMEM, "v": pltpu.VMEM, "a": pl.ANY, "o": pl.ANY}
    return pl.pallas_call(
        kernel,
        out_shape=[jax.ShapeDtypeStruct(dims, jnp.bfloat16) for dims in shapes],
        in_specs=[pl.BlockSpec(memory_space=spaces[kind]) for kind in kinds],
        scratch_shapes=list(scratch),
        compiler_params=pltpu.CompilerParams(vmem_limit_bytes=limit << 20),
        cost_estimate=pl.CostEstimate(flops=0, bytes_accessed=moved, transcendentals=0),
        name=name,
    )(*operands)


def prepare_kernel(place, tokens, gates_any, ids_any, first, table, gates, ids, sems):
    piece = first.shape[0]
    width = first.shape[1] - table.shape[1]
    near = pl.multiple_of(place[3] * piece, piece)
    copies = [
        pltpu.make_async_copy(gates_any, gates, sems.at[0]),
        pltpu.make_async_copy(ids_any, ids, sems.at[1]),
        pltpu.make_async_copy(
            tokens.at[pl.ds(near, piece), pl.ds(0, width)], first.at[:, pl.ds(0, width)], sems.at[2]
        ),
    ]
    for copy in copies:
        copy.start()
    copies[0].wait()
    copies[1].wait()
    rest = gates[...]
    terms = []
    for _ in range(3):
        term = rest.astype(jnp.bfloat16).astype(jnp.float32)
        terms.append(term)
        rest = rest - term
    terms.append(ids[...].astype(jnp.float32))
    unused = piece - 4 * gates.shape[0]
    terms.append(jnp.zeros((unused, gates.shape[1]), jnp.float32))
    packed = jnp.concatenate(terms, axis=0).astype(jnp.bfloat16)
    first[:, width:] = packed
    table[...] = packed
    copies[2].wait()


def prepare(place, cotangent, gates, ids, piece, width):
    return small(
        prepare_kernel,
        "prepare",
        [(piece, width + 128), (piece, 128)],
        "saaa",
        (place, cotangent, gates, ids),
        [
            pltpu.VMEM(gates.shape, jnp.float32),
            pltpu.VMEM(ids.shape, jnp.int32),
            pltpu.SemaphoreType.DMA((3,)),
        ],
        limit=4,
        moved=1 << 18,
    )


def stack_kernel(offset, place, tokens, *refs):
    if offset is None:
        *pieces, _, lines = refs
    else:
        *pieces, lines, following, sem = refs
        piece, width = following.shape
        near = pl.multiple_of(place[3] * piece, piece)
        copy = pltpu.make_async_copy(
            tokens.at[pl.ds(near, piece), pl.ds(offset, width)], following, sem.at[0]
        )
        copy.start()
    for r, ref in enumerate(pieces):
        lines[r] = ref[...]
    if offset is not None:
        copy.wait()


def stack(place, cotangent, pieces, offset, width, after):
    dims = pieces[0].shape
    count = len(pieces)
    shapes = [(count,) + dims]
    operands = [place, cotangent, *pieces]
    kinds = "sa" + "v" * count
    scratch = ()
    if offset is None:
        operands.append(after)
        kinds += "o"
    else:
        shapes.append((dims[0], width))
        scratch = (pltpu.SemaphoreType.DMA((1,)),)
    return small(
        functools.partial(stack_kernel, offset), "stack", shapes, kinds, operands, scratch, moved=1 << 20
    )


def turn_kernel(gate, up, _, gate_t, up_t):
    tile = 128
    for source, target in ((gate, gate_t), (up, up_t)):
        for e in range(source.shape[0]):
            for at in range(0, source.shape[2], tile):
                target[e, at:at + tile] = source[e, :, at:at + tile].astype(jnp.float32).T.astype(
                    jnp.bfloat16
                )


def turn(saved_gate, saved_up, after):
    count, units, slots = saved_gate.shape
    return small(
        turn_kernel,
        "turn",
        [(count, slots, units)] * 2,
        "vvo",
        (saved_gate, saved_up, after),
        limit=12,
        moved=8 << 20,
    )


def corner_kernel(offset, place, tokens, first, over, side, whole_over, left, right, sem):
    _, piece, middle = left.shape
    far = pl.multiple_of((1 - place[3]) * piece, piece)
    copy = pltpu.make_async_copy(
        tokens.at[pl.ds(far, piece), pl.ds(offset, middle)], right.at[0], sem.at[0]
    )
    copy.start()
    whole_over[0] = first[...]
    whole_over[1:] = over[...]
    left[0] = first[:, :middle]
    left[1:] = over[:, :, :middle]
    right[1:] = side[:, :, middle:2 * middle]
    copy.wait()


def corner(place, cotangent, first, over, side, offset, middle):
    count, piece, width = over.shape
    return small(
        functools.partial(corner_kernel, offset + middle),
        "corner",
        [(count + 1, piece, width)] + [(count + 1, piece, middle)] * 2,
        "savvv",
        (place, cotangent, first, over, side),
        (pltpu.SemaphoreType.DMA((1,)),),
        moved=3 << 20,
    )


def join_kernel(left, right, *refs):
    result = refs[-1]
    middle = left.shape[-1]
    result[:, :, :middle] = left[...]
    result[:, :, middle:] = right[...]


def join(left, right, *after):
    dims = left.shape
    return small(
        join_kernel,
        "join",
        [dims[:-1] + (2 * dims[-1],)],
        "vv" + "o" * len(after),
        (left, right, *after),
        moved=1 << 20,
    )[0]


def route_kernel(capacity, place, own, own_c, lines, lines_c, over, over_c, pick, pick_t, gate, hits, gates):
    line_count, _, tokens = over.shape
    core, row, line, half = place[0], place[1], place[2], place[3]
    first = (line * 4 + row * 2 + core) * 2
    for r in range(line_count):
        for ry in range(2):
            tables = []
            for c in range(2):
                if ry == 1:
                    table = (over, over_c)[c][r]
                elif r == 0:
                    table = (own, own_c)[c][...]
                else:
                    table = (lines, lines_c)[c][r - 1]
                tables.append(table[:32].astype(jnp.float32))
            swapped = core > 0
            ordered = [
                jnp.where(swapped, tables[1], tables[0]), jnp.where(swapped, tables[0], tables[1])
            ]
            for c in range(2):
                block = ordered[c]
                value = block[0:8] + block[8:16] + block[16:24]
                for e in range(2):
                    named = block[24:32] == (first + e).astype(jnp.float32)
                    at = ((r * 2 + ry) * 2 + c) * 2 + e
                    hits[at:at + 1] = jnp.sum(named.astype(jnp.float32), axis=0, keepdims=True)
                    gates[at:at + 1] = jnp.sum(
                        jnp.where(named, value, 0.0), axis=0, keepdims=True
                    )
    earlier = lax.broadcasted_iota(jnp.int32, (tokens, tokens), 0) < lax.broadcasted_iota(
        jnp.int32, (tokens, tokens), 1
    )
    hit = hits[...]
    slot = jnp.dot(
        hit.astype(jnp.bfloat16),
        earlier.astype(jnp.float32).astype(jnp.bfloat16),
        preferred_element_type=jnp.float32,
    )
    slot = jnp.where(hit > 0.5, slot, -1.0)
    turned = half > 0
    slot = jnp.where(turned, pltpu.roll(slot, tokens // 2, 1), slot)
    weight = jnp.where(turned, pltpu.roll(gates[...], tokens // 2, 1), gates[...])
    order = lax.broadcasted_iota(jnp.int32, (capacity, tokens), 0).astype(jnp.float32)
    for p in range(line_count * 2):
        rows = []
        for e in range(2):
            for c in range(2):
                at = (p * 2 + c) * 2 + e
                ones = (order == slot[at:at + 1]).astype(jnp.float32)
                column = jnp.sum(ones * weight[at:at + 1], axis=1, keepdims=True)
                place_in = (e * 2 + c) * capacity
                gate[p, place_in:place_in + capacity] = jnp.broadcast_to(
                    column, (capacity, gate.shape[2])
                )
                own_core = (core == c).astype(jnp.float32)
                rows.append(jnp.concatenate([ones * own_core, ones * (1.0 - own_core)], axis=1))
        matrix = jnp.concatenate(rows, axis=0)
        pick[p] = matrix.astype(jnp.bfloat16)
        count = matrix.shape[0]
        square = jnp.concatenate(
            [matrix, jnp.zeros((2 * tokens - count, 2 * tokens), jnp.float32)], axis=0
        )
        pick_t[p] = square.T[:, :count].astype(jnp.bfloat16)


def route(place, own, own_c, lines, lines_c, over, over_c, capacity):
    line_count, piece, whole_width = over.shape
    tokens = 2 * piece
    pairs = 2 * line_count
    rows = 4 * capacity
    last = whole_width // 128 - 1
    table = lambda array: pl.BlockSpec(array.shape[:-1] + (128,), lambda i, place: (0, 0, last))
    alone = pl.BlockSpec((piece, 128), lambda i, place: (0, 0))
    shapes = ((pairs, rows, 2 * tokens), (pairs, 2 * tokens, rows), (pairs, rows, 128))
    return pl.pallas_call(
        functools.partial(route_kernel, capacity),
        out_shape=[
            jax.ShapeDtypeStruct(dims, kind)
            for dims, kind in zip(shapes, (jnp.bfloat16, jnp.bfloat16, jnp.float32))
        ],
        grid_spec=pltpu.PrefetchScalarGridSpec(
            num_scalar_prefetch=1,
            grid=(1,),
            in_specs=[alone, alone] + [table(array) for array in (lines, lines_c, over, over_c)],
            out_specs=[pl.BlockSpec(dims, lambda i, place: (0, 0, 0)) for dims in shapes],
            scratch_shapes=[pltpu.VMEM((4 * pairs, tokens), jnp.float32)] * 2,
        ),
        compiler_params=pltpu.CompilerParams(vmem_limit_bytes=8 << 20),
        name="route",
    )(place, own, own_c, lines, lines_c, over, over_c)


def hidden_kernel(last, place, *refs):
    own, own_c, lines, lines_c, side, side_c, over, over_c, diag, diag_c = refs[:10]
    pick, gate, w_down, _ = refs[10:14]
    if last:
        before, saved_gate, saved_up, result, slots, total = refs[14:]
    else:
        result, slots = refs[14:]
        total = result
    k, steps = pl.program_id(0), pl.num_programs(0)
    line_count, piece, _ = over.shape
    rows = pick.shape[1] // 2

    @pl.when(k == 0)
    def _():
        total[...] = before[...] if last else jnp.zeros_like(total)

    near = pl.multiple_of(place[3] * piece, piece)
    far = pl.multiple_of((1 - place[3]) * piece, piece)
    for r in range(line_count):
        for ry in range(2):
            parts = []
            for c in range(2):
                if ry == 1:
                    parts += [(over, over_c)[c][r], (diag, diag_c)[c][r]]
                elif r == 0:
                    group = (own, own_c)[c]
                    parts += [group[pl.ds(near, piece), :], group[pl.ds(far, piece), :]]
                else:
                    parts += [(lines, lines_c)[c][r - 1], (side, side_c)[c][r - 1]]
            p = r * 2 + ry
            picked = jnp.dot(
                pick[p], jnp.concatenate(parts, axis=0), preferred_element_type=jnp.float32
            )
            weight = gate[p]
            weight = jnp.concatenate([weight] * (picked.shape[1] // weight.shape[1]), axis=1)
            scaled = (picked * weight).astype(jnp.bfloat16)
            base = pair_base(place, line_count, r, ry, rows)
            slots[0, pl.ds(base, rows), :] = scaled[:rows]
            slots[1, pl.ds(base, rows), :] = scaled[rows:]
    for e in range(2):
        total[e] = total[e] + lax.dot_general(
            slots[e], w_down[e], (((1,), (1,)), ((), ())), preferred_element_type=jnp.float32
        )

    if last:
        tile = 64
        per_expert = total.shape[1] // tile
        width = total.shape[2]

        @pl.when(k == steps - 1)
        def _():
            @pl.loop(0, 2 * per_expert)
            def _(i):
                e, at = i // per_expert, pl.ds(pl.multiple_of(i % per_expert * tile, tile), tile)
                hidden_grad = total[e, at, :]
                gate_value = saved_gate[e, at, :].astype(jnp.float32)
                up_value = saved_up[e, at, :].astype(jnp.float32)
                sigmoid_gate = jax.nn.sigmoid(gate_value)
                result[e, at, width:] = (hidden_grad * gate_value * sigmoid_gate).astype(
                    jnp.bfloat16
                )
                result[e, at, :width] = (
                    hidden_grad * up_value * sigmoid_gate * (1.0 + gate_value * (1.0 - sigmoid_gate))
                ).astype(jnp.bfloat16)


def hidden(place, chunk, own, own_c, moved, pick, gate, w_down, after, rest):
    last = rest is not None
    line_count, piece, _ = moved[4].shape
    width = moved[6].shape[-1]
    steps = width // LANES
    offset = chunk * steps
    units = w_down.shape[1]
    slot_count = pick.shape[0] * pick.shape[1] // 2
    whole = lambda dims: pl.BlockSpec(
        dims, lambda k, place: (0,) * len(dims), pipeline_mode=pl.Buffered(1)
    )
    column = lambda array: pl.BlockSpec(array.shape[:-1] + (LANES,), lambda k, place: (0, 0, k))
    group = pl.BlockSpec((own.shape[0], LANES), lambda k, place: (0, offset + k))
    in_specs = [group, group]
    in_specs += [column(array) for array in moved]
    in_specs += [whole(pick.shape), whole(gate.shape)]
    in_specs += [pl.BlockSpec((2, units, LANES), lambda k, place: (0, 0, offset + k))]
    in_specs += [pl.BlockSpec(memory_space=pl.ANY)]
    scratch = [pltpu.VMEM((2, slot_count, LANES), jnp.bfloat16)]
    operands = [own, own_c, *moved, pick, gate, w_down, after]
    if last:
        in_specs += [whole(array.shape) for array in rest]
        operands += rest
        out = jax.ShapeDtypeStruct((2, slot_count, 2 * units), jnp.bfloat16)
        scratch += [pltpu.VMEM((2, slot_count, units), jnp.float32)]
    else:
        out = jax.ShapeDtypeStruct((2, slot_count, units), jnp.float32)
    return pl.pallas_call(
        functools.partial(hidden_kernel, last),
        out_shape=out,
        grid_spec=pltpu.PrefetchScalarGridSpec(
            num_scalar_prefetch=1,
            grid=(steps,),
            in_specs=in_specs,
            out_specs=whole(out.shape),
            scratch_shapes=scratch,
        ),
        compiler_params=pltpu.CompilerParams(vmem_limit_bytes=24 << 20),
        cost_estimate=pl.CostEstimate(
            flops=2 * 2 * slot_count * width * (units + 256), bytes_accessed=8 << 20, transcendentals=0
        ),
        name="hidden",
    )(place, *operands)


def sums_kernel(place, grads, w_gate, w_up, pick_t, keep, send, slots):
    pairs, _, rows = pick_t.shape
    rows = rows // 2
    for e in range(2):
        weights = jnp.concatenate([w_gate[e], w_up[e]], axis=0)
        slots[e] = jnp.dot(grads[e], weights, preferred_element_type=jnp.float32).astype(
            jnp.bfloat16
        )
    for r in range(pairs // 2):
        for ry in range(2):
            p = r * 2 + ry
            base = pair_base(place, pairs // 2, r, ry, rows)
            both = jnp.concatenate(
                [slots[0, pl.ds(base, rows), :], slots[1, pl.ds(base, rows), :]], axis=0
            )
            total = jnp.dot(pick_t[p], both, preferred_element_type=jnp.float32).astype(
                jnp.bfloat16
            )
            tokens = total.shape[0] // 2
            keep[p] = total[:tokens]
            send[p] = total[tokens:]


def sums(place, chunk, width, grads, w_gate, w_up, pick_t):
    steps = width // LANES
    offset = chunk * steps
    units = w_gate.shape[1]
    pairs, tokens, _ = pick_t.shape
    tokens = tokens // 2
    whole = lambda dims: pl.BlockSpec(
        dims, lambda k, place: (0,) * len(dims), pipeline_mode=pl.Buffered(1)
    )
    weight = pl.BlockSpec((2, units, LANES), lambda k, place: (0, 0, offset + k))
    out = jax.ShapeDtypeStruct((pairs, tokens, width), jnp.bfloat16)
    return pl.pallas_call(
        sums_kernel,
        out_shape=(out, out),
        grid_spec=pltpu.PrefetchScalarGridSpec(
            num_scalar_prefetch=1,
            grid=(steps,),
            in_specs=[whole(grads.shape), weight, weight, whole(pick_t.shape)],
            out_specs=[pl.BlockSpec((pairs, tokens, LANES), lambda k, place: (0, 0, k))] * 2,
            scratch_shapes=[pltpu.VMEM((2, grads.shape[1], LANES), jnp.bfloat16)],
        ),
        compiler_params=pltpu.CompilerParams(vmem_limit_bytes=16 << 20),
        cost_estimate=pl.CostEstimate(
            flops=2 * 2 * grads.shape[1] * width * (2 * units + 256),
            bytes_accessed=10 << 20,
            transcendentals=0,
        ),
        name="sums",
    )(place, grads, w_gate, w_up, pick_t)


def first_kernel(keep, came, _, send_l, keep_l, send_r, keep_r):
    total = keep[...] + came[...]
    middle = total.shape[-1] // 2
    keep_l[...] = total[:, 0, :, :middle]
    send_l[...] = total[:, 1, :, :middle]
    keep_r[...] = total[0:1, :, :, middle:]
    send_r[...] = total[1:2, :, :, middle:]


def first_sum(keep, came, piece, after):
    pairs, tokens, width = keep.shape
    keep = keep.reshape(pairs, 2, piece, width)
    came = came.reshape(pairs, 2, piece, width)
    full = pl.BlockSpec((2, 2, piece, width), lambda r: (r, 0, 0, 0))
    left = jax.ShapeDtypeStruct((pairs, piece, width // 2), jnp.bfloat16)
    right = jax.ShapeDtypeStruct((pairs // 2, 2, piece, width // 2), jnp.bfloat16)
    left_spec = pl.BlockSpec((2, piece, width // 2), lambda r: (r, 0, 0))
    right_spec = pl.BlockSpec((1, 2, piece, width // 2), lambda r: (r, 0, 0, 0))
    return pl.pallas_call(
        first_kernel,
        out_shape=(left, left, right, right),
        grid=(pairs // 2,),
        in_specs=[full, full, pl.BlockSpec(memory_space=pl.ANY)],
        out_specs=[left_spec, left_spec, right_spec, right_spec],
        cost_estimate=pl.CostEstimate(flops=0, bytes_accessed=6 << 20, transcendentals=0),
        compiler_params=pltpu.CompilerParams(vmem_limit_bytes=8 << 20),
        name="first_sum",
    )(keep, came, after)


def second_kernel(keep_l, came_l, keep_r, came_r, send_l, left, send_r, right):
    total = keep_l[...] + came_l[...]
    left[...] = total[0:1]
    send_l[...] = total[1:2]
    total = keep_r[...] + came_r[...]
    right[...] = total[:, 0]
    send_r[...] = total[:, 1]


def second_sum(keep_l, came_l, keep_r, came_r):
    lines, _, piece, middle = keep_r.shape
    out = jax.ShapeDtypeStruct((lines, piece, middle), jnp.bfloat16)
    left = pl.BlockSpec((2, piece, middle), lambda r: (r, 0, 0))
    right = pl.BlockSpec((1, 2, piece, middle), lambda r: (r, 0, 0, 0))
    return pl.pallas_call(
        second_kernel,
        out_shape=(out,) * 4,
        grid=(lines,),
        in_specs=[left, left, right, right],
        out_specs=[pl.BlockSpec((1, piece, middle), lambda r: (r, 0, 0))] * 4,
        cost_estimate=pl.CostEstimate(flops=0, bytes_accessed=3 << 20, transcendentals=0),
        compiler_params=pltpu.CompilerParams(vmem_limit_bytes=8 << 20),
        name="second_sum",
    )(keep_l, came_l, keep_r, came_r)


def third_kernel(left, came_l, right, came_r, own, *sends):
    middle = left.shape[-1]
    for columns, one, other in ((slice(0, middle), left, came_l), (slice(middle, None), right, came_r)):
        own[:, columns] = one[0].astype(jnp.float32) + other[0].astype(jnp.float32)
        for r, send in enumerate(sends):
            send[:, columns] = one[r + 1] + other[r + 1]


def third_sum(left, came_l, right, came_r):
    lines, piece, middle = left.shape
    return pl.pallas_call(
        third_kernel,
        out_shape=(jax.ShapeDtypeStruct((piece, 2 * middle), jnp.float32),)
        + (jax.ShapeDtypeStruct((piece, 2 * middle), jnp.bfloat16),) * (lines - 1),
        cost_estimate=pl.CostEstimate(flops=0, bytes_accessed=2 << 20, transcendentals=0),
        compiler_params=pltpu.CompilerParams(vmem_limit_bytes=8 << 20),
        name="third_sum",
    )(left, came_l, right, came_r)


def last_kernel(count, *refs):
    result = refs[-1]
    terms = len(refs[:-1]) // count
    width = refs[0].shape[1]
    for chunk in range(count):
        total = refs[chunk * terms][...]
        for ref in refs[chunk * terms + 1:(chunk + 1) * terms]:
            total = total + ref[...].astype(jnp.float32)
        result[:, chunk * width:(chunk + 1) * width] = total


def tokens_body(cotangent, gates, expert_ids, saved_gate, saved_up, w_gate, w_up, w_down):
    owners = lax.axis_size("expert")
    row_count, feature_dim = cotangent.shape
    slot_count = saved_gate.shape[2]
    capacity = slot_count // owners
    lines = owners // 4
    piece = row_count // 2
    width = feature_dim // CHUNKS
    middle = width // 2
    me, half = lax.axis_index("expert"), lax.axis_index("tp")
    place = jnp.stack([me % 2, me // 2 % 2, me // 4, half]).astype(jnp.int32)

    part, table = prepare(place, cotangent, gates.T, expert_ids.T, piece, width)
    own_c, table_c = swap(cotangent, "expert", 1), swap(table, "expert", 1)
    gathered, saved, rest = [], None, None
    for chunk in range(CHUNKS):
        last = chunk == CHUNKS - 1
        first = swap(part, "expert", 2)
        pieces = [along_line(part, -r) for r in range(1, lines)]
        if last:
            line, = stack(place, cotangent, pieces, None, width, saved[0])
        else:
            line, part = stack(place, cotangent, pieces, (chunk + 1) * width, width, None)
            saved = turn(saved_gate, saved_up, line)
        side, over = swap(line, "tp", 1), swap(line, "expert", 2)
        over, left, right = corner(place, cotangent, first, over, side, chunk * width, middle)
        left_came, right_came = swap(left, "tp", 1), swap(right, "expert", 2)
        if last:
            for index, moved in enumerate(gathered):
                rest = hidden(place, index, cotangent, own_c, moved, pick, gate, w_down, left, rest)
            diag = join(left_came, right_came, rest)
        else:
            diag = join(left_came, right_came)
        moved = []
        for array in (line, side, over, diag):
            moved += [array, swap(array, "expert", 1)]
        gathered.append(moved)
        if chunk == 0:
            lines_c, over_c = moved[1], moved[5]
            pick, pick_t, gate = route(place, table, table_c, line, lines_c, over, over_c, capacity)
    rest = [rest, *saved]
    grads = hidden(place, chunk, cotangent, own_c, moved, pick, gate, w_down, left, rest)

    terms = []
    after = grads
    for chunk in range(CHUNKS):
        keep, send = sums(place, chunk, width, grads, w_gate, w_up, pick_t)
        came = swap(send, "expert", 1)
        send_l, keep_l, send_r, keep_r = first_sum(keep, came, piece, after)
        came_l, came_r = swap(send_l, "tp", 1), swap(send_r, "expert", 2)
        send_l, left, send_r, right = second_sum(keep_l, came_l, keep_r, came_r)
        after = send_l
        came_l, came_r = swap(send_l, "expert", 2), swap(send_r, "tp", 1)
        own, *sends = third_sum(left, came_l, right, came_r)
        terms += [own] + [along_line(send, r + 1) for r, send in enumerate(sends)]
    return pl.pallas_call(
        functools.partial(last_kernel, CHUNKS),
        out_shape=jax.ShapeDtypeStruct((piece, feature_dim), jnp.float32),
        compiler_params=pltpu.CompilerParams(vmem_limit_bytes=8 << 20),
        name="last_sum",
    )(*terms)


def body(*arrays):
    cotangent, gates, _, saved_gate = arrays[:4]
    owners = lax.axis_size("expert")
    fits = (
        owners in (4, 8, 16)
        and lax.axis_size("tp") == 2
        and cotangent.shape[0] == 128
        and cotangent.shape[1] % (2 * CHUNKS * LANES) == 0
        and gates.shape[1] == 8
        and saved_gate.shape[0] == 2
        and saved_gate.shape[2] // owners % 16 == 0
        and 4 * saved_gate.shape[2] // owners <= 256
    )
    return (tokens_body if fits else slots_body)(*arrays)


def solution(mesh):
    in_specs = (
        P("expert", None),
        P("expert", None),
        P("expert", None),
        P("expert", "tp", None),
        P("expert", "tp", None),
        P("expert", "tp", None),
        P("expert", "tp", None),
        P("expert", "tp", None),
    )
    out_specs = P(("expert", "tp"), None)
    return jax.shard_map(body, mesh=mesh, in_specs=in_specs, out_specs=out_specs, check_vma=False)
```

```python
import functools

import jax
import jax.numpy as jnp
from jax import lax
from jax.experimental import pallas as pl
from jax.experimental.pallas import tpu as pltpu
from jax.sharding import PartitionSpec as P


def route_slots(expert_ids, expert_total):
    flat_ids = expert_ids.reshape(-1)
    one_hot = (flat_ids[:, None] == jnp.arange(expert_total, dtype=jnp.int32)[None, :]).astype(
        jnp.int32
    )
    before = jnp.cumsum(one_hot, axis=0) - one_hot
    return (flat_ids, jnp.sum(before * one_hot, axis=1))


def expert_step(arrived, saved_gate, saved_up, w_gate, w_up, w_down):
    hidden_grad = jnp.einsum("efd,esd->efs", w_down, arrived, preferred_element_type=jnp.float32)
    gate_value = saved_gate.astype(jnp.float32)
    up_value = saved_up.astype(jnp.float32)
    sigmoid_gate = jax.nn.sigmoid(gate_value)
    up_grad = (hidden_grad * gate_value * sigmoid_gate).astype(jnp.bfloat16)
    gate_grad = (
        hidden_grad * up_value * sigmoid_gate * (1.0 + gate_value * (1.0 - sigmoid_gate))
    ).astype(jnp.bfloat16)
    partial_value = jnp.einsum(
        "efs,efd->esd", gate_grad, w_gate, preferred_element_type=jnp.float32
    )
    partial_value = partial_value + jnp.einsum(
        "efs,efd->esd", up_grad, w_up, preferred_element_type=jnp.float32
    )
    return partial_value.astype(jnp.bfloat16)


def slots_body(cotangent, gates, expert_ids, saved_gate, saved_up, w_gate, w_up, w_down):
    owners = lax.axis_size("expert")
    row_count, feature_dim = cotangent.shape
    top_count = expert_ids.shape[1]
    local_count, _, slot_count = saved_gate.shape
    capacity = slot_count // owners
    flat_ids, slot_pos = route_slots(expert_ids, local_count * owners)
    target = flat_ids % local_count * slot_count + flat_ids // local_count * capacity + slot_pos
    scaled = (gates[:, :, None] * cotangent.astype(jnp.float32)[:, None, :]).astype(jnp.bfloat16)
    scaled = scaled.reshape(row_count * top_count, feature_dim)
    outgoing = (
        jnp.zeros((local_count * slot_count, feature_dim), jnp.bfloat16).at[target].set(scaled)
    )
    outgoing = outgoing.reshape(local_count, slot_count, feature_dim)
    arrived = lax.all_to_all(outgoing, "expert", split_axis=1, concat_axis=1, tiled=True)
    partial_value = expert_step(arrived, saved_gate, saved_up, w_gate, w_up, w_down)
    returned = lax.all_to_all(partial_value, "expert", split_axis=1, concat_axis=1, tiled=True)
    picked = returned.reshape(local_count * slot_count, feature_dim)[target].astype(jnp.float32)
    combined = jnp.sum(picked.reshape(row_count, top_count, feature_dim), axis=1)
    return lax.psum_scatter(combined, "tp", scatter_dimension=0, tiled=True)


CHUNKS = ((0, 2), (1, 3))
TILE = 512


def swap(value, axis, step):
    count = lax.axis_size(axis)
    return lax.ppermute(value, axis, [(i, i ^ step) for i in range(count)])


def along_line(value, shift):
    count = lax.axis_size("expert")
    return lax.ppermute(value, "expert", [(i, (i + 4 * shift) % count) for i in range(count)])


def small(kernel, name, outs, kinds, operands, scratch=(), limit=8, work=0):
    spaces = {"s": pltpu.SMEM, "v": pltpu.VMEM, "h": pltpu.HBM, "o": pl.ANY}
    return pl.pallas_call(
        kernel,
        out_shape=[
            out if hasattr(out, "dtype") else jax.ShapeDtypeStruct(out, jnp.bfloat16) for out in outs
        ],
        in_specs=[pl.BlockSpec(memory_space=spaces[kind]) for kind in kinds],
        scratch_shapes=list(scratch),
        compiler_params=pltpu.CompilerParams(vmem_limit_bytes=limit << 20),
        cost_estimate=pl.CostEstimate(flops=work, bytes_accessed=work >> 8, transcendentals=0),
        name=name,
    )(*operands)


def prepare_kernel(place, tokens, gates_any, ids_any, first, table, gates, ids, sems):
    piece = first.shape[0]
    width = first.shape[1] - table.shape[1]
    near = pl.multiple_of(place[3] * piece, piece)
    copies = [
        pltpu.make_async_copy(gates_any, gates, sems.at[0]),
        pltpu.make_async_copy(ids_any, ids, sems.at[1]),
        pltpu.make_async_copy(
            tokens.at[pl.ds(near, piece), :], first.at[:, pl.ds(0, width)], sems.at[2]
        ),
    ]
    for copy in copies:
        copy.start()
    copies[0].wait()
    copies[1].wait()
    rest = gates[...]
    terms = []
    for _ in range(3):
        term = rest.astype(jnp.bfloat16).astype(jnp.float32)
        terms.append(term)
        rest = rest - term
    terms.append(ids[...].astype(jnp.float32))
    unused = piece - 4 * gates.shape[0]
    terms.append(jnp.zeros((unused, gates.shape[1]), jnp.float32))
    packed = jnp.concatenate(terms, axis=0).astype(jnp.bfloat16)
    first[:, width:] = packed
    table[...] = packed
    copies[2].wait()


def prepare(place, cotangent, gates, ids, piece):
    return small(
        prepare_kernel,
        "prepare",
        [(piece, cotangent.shape[1] + 128), (piece, 128)],
        "shhh",
        (place, cotangent, gates, ids),
        [
            pltpu.VMEM(gates.shape, jnp.float32),
            pltpu.VMEM(ids.shape, jnp.int32),
            pltpu.SemaphoreType.DMA((3,)),
        ],
        limit=4,
    )


def stack_kernel(*refs):
    lines = refs[-1]
    for r in range(lines.shape[0]):
        lines[r] = refs[r][...]


def stack(pieces, *after):
    return small(
        stack_kernel,
        "stack",
        [(len(pieces),) + pieces[0].shape],
        "v" * len(pieces) + "o" * len(after),
        (*pieces, *after),
    )[0]


def relay_kernel(came, part, line, following):
    line[0] = came[...]
    following[...] = part[...]


def relay(came, part):
    return small(
        relay_kernel, "relay", [(1,) + came.shape, part.shape], "vv", (came, part)
    )


def turn_kernel(gate, up, _, gate_t, up_t):
    tile = 128
    for source, target in ((gate, gate_t), (up, up_t)):
        for e in range(source.shape[0]):
            for at in range(0, source.shape[2], tile):
                target[e, at:at + tile] = source[e, :, at:at + tile].astype(jnp.float32).T.astype(
                    jnp.bfloat16
                )


def turn(saved_gate, saved_up, after):
    count, units, slots = saved_gate.shape
    return small(
        turn_kernel,
        "turn",
        [(count, slots, units)] * 2,
        "vvo",
        (saved_gate, saved_up, after),
        limit=12,
    )


def corner_kernel(place, tokens, first, over, side, whole_over, left, right, sem):
    _, piece, middle = left.shape
    far = pl.multiple_of((1 - place[3]) * piece, piece)
    copy = pltpu.make_async_copy(
        tokens.at[pl.ds(far, piece), pl.ds(middle, middle)], right.at[0], sem.at[0]
    )
    copy.start()
    whole_over[0] = first[...]
    whole_over[1:] = over[...]
    left[0] = first[:, :middle]
    left[1:] = over[:, :, :middle]
    right[1:] = side[:, :, middle:2 * middle]
    copy.wait()


def own_corner(place, cotangent, first, over, side):
    count, piece, width = over.shape
    middle = cotangent.shape[1] // 2
    return small(
        corner_kernel,
        "own_corner",
        [(count + 1, piece, width)] + [(count + 1, piece, middle)] * 2,
        "shvvv",
        (place, cotangent, first, over, side),
        (pltpu.SemaphoreType.DMA((1,)),),
    )


def plain_corner_kernel(over, side, _, left, right):
    middle = left.shape[-1]
    left[...] = over[:, :, :middle]
    right[...] = side[:, :, middle:2 * middle]


def corner(over, side, middle, after):
    return small(
        plain_corner_kernel,
        "corner",
        [over.shape[:2] + (middle,)] * 2,
        "vvo",
        (over, side, after),
    )


def join_kernel(left, right, *refs):
    result = refs[-1]
    middle = left.shape[-1]
    result[:, :, :middle] = left[...]
    result[:, :, middle:] = right[...]


def join(left, right, *after):
    dims = left.shape
    return small(
        join_kernel,
        "join",
        [dims[:-1] + (2 * dims[-1],)],
        "vv" + "o" * len(after),
        (left, right, *after),
        work=1 << 36,
    )[0]


def tokens_of(own, lines, r, offsets):
    if r == 0:
        return own[...]
    return lines[r_place(r, offsets)]


def r_place(r, offsets):
    return [offset for offset in offsets if offset != 0].index(r)


def pair_base(place, line_count, r, ry, width):
    line = lax.rem(place[2] + r, line_count)
    row = place[1] if ry == 0 else 1 - place[1]
    return pl.multiple_of((line * 2 + row) * width, width)


def route_kernel(offsets, capacity, place, own, own_c, lines, lines_c, over, over_c, pick, pick_t, gate,
                 hits, gates):
    tokens = pick.shape[2] // 2
    width = over.shape[2] - 128
    core, row, line, half = place[0], place[1], place[2], place[3]
    first = (line * 4 + row * 2 + core) * 2
    for i, r in enumerate(offsets):
        for ry in range(2):
            tables = []
            for c in range(2):
                if ry == 1:
                    table = (over, over_c)[c][i, :32, width:]
                elif r == 0:
                    table = (own, own_c)[c][:32]
                else:
                    table = (lines, lines_c)[c][r_place(r, offsets), :32, width:]
                tables.append(table.astype(jnp.float32))
            swapped = core > 0
            ordered = [
                jnp.where(swapped, tables[1], tables[0]), jnp.where(swapped, tables[0], tables[1])
            ]
            for c in range(2):
                block = ordered[c]
                value = block[0:8] + block[8:16] + block[16:24]
                for e in range(2):
                    named = block[24:32] == (first + e).astype(jnp.float32)
                    at = ((i * 2 + ry) * 2 + c) * 2 + e
                    hits[at:at + 1] = jnp.sum(named.astype(jnp.float32), axis=0, keepdims=True)
                    gates[at:at + 1] = jnp.sum(
                        jnp.where(named, value, 0.0), axis=0, keepdims=True
                    )
    earlier = lax.broadcasted_iota(jnp.int32, (tokens, tokens), 0) < lax.broadcasted_iota(
        jnp.int32, (tokens, tokens), 1
    )
    hit = hits[...]
    slot = jnp.dot(
        hit.astype(jnp.bfloat16),
        earlier.astype(jnp.float32).astype(jnp.bfloat16),
        preferred_element_type=jnp.float32,
    )
    slot = jnp.where(hit > 0.5, slot, -1.0)
    turned = half > 0
    slot = jnp.where(turned, pltpu.roll(slot, tokens // 2, 1), slot)
    weight = jnp.where(turned, pltpu.roll(gates[...], tokens // 2, 1), gates[...])
    order = lax.broadcasted_iota(jnp.int32, (capacity, tokens), 0).astype(jnp.float32)
    for p in range(pick.shape[0]):
        rows = []
        for e in range(2):
            for c in range(2):
                at = (p * 2 + c) * 2 + e
                ones = (order == slot[at:at + 1]).astype(jnp.float32)
                column = jnp.sum(ones * weight[at:at + 1], axis=1, keepdims=True)
                place_in = (e * 2 + c) * capacity
                gate[p, place_in:place_in + capacity] = jnp.broadcast_to(
                    column, (capacity, gate.shape[2])
                )
                own_core = (core == c).astype(jnp.float32)
                rows.append(jnp.concatenate([ones * own_core, ones * (1.0 - own_core)], axis=1))
        matrix = jnp.concatenate(rows, axis=0)
        pick[p] = matrix.astype(jnp.bfloat16)
        count = matrix.shape[0]
        square = jnp.concatenate(
            [matrix, jnp.zeros((2 * tokens - count, 2 * tokens), jnp.float32)], axis=0
        )
        pick_t[p] = square.T[:, :count].astype(jnp.bfloat16)


def route(offsets, place, table, table_c, lines, lines_c, over, over_c, capacity):
    tokens = 2 * over.shape[1]
    pairs = 2 * len(offsets)
    rows = 4 * capacity
    return small(
        functools.partial(route_kernel, offsets, capacity),
        "route",
        [
            (pairs, rows, 2 * tokens),
            (pairs, 2 * tokens, rows),
            jax.ShapeDtypeStruct((pairs, rows, 128), jnp.float32),
        ],
        "s" + "v" * 6,
        (place, table, table_c, lines, lines_c, over, over_c),
        [pltpu.VMEM((4 * pairs, tokens), jnp.float32)] * 2,
    )


def hidden_kernel(offsets, line_count, place, own, own_c, lines, lines_c, side, side_c, over, over_c,
                  diag, diag_c, pick, gate, w_down, saved_gate, saved_up, _, grads, slots):
    piece = over.shape[1]
    width = diag.shape[2]
    rows = pick.shape[1] // 2
    units = w_down.shape[1]
    near = pl.multiple_of(place[3] * piece, piece)
    far = pl.multiple_of((1 - place[3]) * piece, piece)

    @pl.loop(0, width // TILE)
    def _(k):
        at = pl.ds(pl.multiple_of(k * TILE, TILE), TILE)
        for i, r in enumerate(offsets):
            for ry in range(2):
                parts = []
                for c in range(2):
                    if ry == 1:
                        parts += [(over, over_c)[c][i, :, at], (diag, diag_c)[c][i, :, at]]
                    elif r == 0:
                        group = (own, own_c)[c]
                        parts += [group[pl.ds(near, piece), at], group[pl.ds(far, piece), at]]
                    else:
                        j = r_place(r, offsets)
                        parts += [(lines, lines_c)[c][j, :, at], (side, side_c)[c][j, :, at]]
                p = i * 2 + ry
                picked = jnp.dot(
                    pick[p], jnp.concatenate(parts, axis=0), preferred_element_type=jnp.float32
                )
                weight = gate[p]
                weight = jnp.concatenate([weight] * (TILE // weight.shape[1]), axis=1)
                scaled = (picked * weight).astype(jnp.bfloat16)
                slots[0, p * rows:(p + 1) * rows, at] = scaled[:rows]
                slots[1, p * rows:(p + 1) * rows, at] = scaled[rows:]

    for e in range(2):
        total = lax.dot_general(
            slots[e], w_down[e], (((1,), (1,)), ((), ())), preferred_element_type=jnp.float32
        )
        for i, r in enumerate(offsets):
            for ry in range(2):
                p = i * 2 + ry
                mine = slice(p * rows, (p + 1) * rows)
                saved = pl.ds(pair_base(place, line_count, r, ry, rows), rows)
                hidden_grad = total[mine]
                gate_value = saved_gate[e, saved, :].astype(jnp.float32)
                up_value = saved_up[e, saved, :].astype(jnp.float32)
                sigmoid_gate = jax.nn.sigmoid(gate_value)
                grads[e, mine, units:] = (hidden_grad * gate_value * sigmoid_gate).astype(
                    jnp.bfloat16
                )
                grads[e, mine, :units] = (
                    hidden_grad * up_value * sigmoid_gate * (1.0 + gate_value * (1.0 - sigmoid_gate))
                ).astype(jnp.bfloat16)


def hidden(offsets, line_count, place, own, own_c, moved, pick, gate, w_down, saved, after):
    width = own.shape[1]
    units = w_down.shape[1]
    count = pick.shape[0] * pick.shape[1] // 2
    return small(
        functools.partial(hidden_kernel, offsets, line_count),
        "hidden",
        [(2, count, 2 * units)],
        "s" + "v" * 15 + "o",
        (place, own, own_c, *moved, pick, gate, w_down, *saved, after),
        [pltpu.VMEM((2, count, width), jnp.bfloat16)],
        limit=12,
    )[0]


def sums_kernel(offset, grads, w_gate, w_up, pick_t, _, keep, send, slots):
    rows = pick_t.shape[2] // 2
    tokens = pick_t.shape[1] // 2

    @pl.loop(0, keep.shape[2] // TILE)
    def _(k):
        at = pl.ds(pl.multiple_of(k * TILE, TILE), TILE)
        source = pl.ds(pl.multiple_of(offset + k * TILE, TILE), TILE)
        for e in range(2):
            weights = jnp.concatenate([w_gate[e, :, source], w_up[e, :, source]], axis=0)
            slots[e] = jnp.dot(grads[e], weights, preferred_element_type=jnp.float32).astype(
                jnp.bfloat16
            )
        for p in range(pick_t.shape[0]):
            mine = slice(p * rows, (p + 1) * rows)
            both = jnp.concatenate([slots[0, mine], slots[1, mine]], axis=0)
            total = jnp.dot(pick_t[p], both, preferred_element_type=jnp.float32).astype(
                jnp.bfloat16
            )
            keep[p, :, at] = total[:tokens]
            send[p, :, at] = total[tokens:]


def sums(offset, width, grads, w_gate, w_up, pick_t, after):
    pairs, tokens, _ = pick_t.shape
    _, count, units = grads.shape
    return small(
        functools.partial(sums_kernel, offset),
        "sums",
        [(pairs, tokens // 2, width)] * 2,
        "vvvvo",
        (grads, w_gate, w_up, pick_t, after),
        [pltpu.VMEM((2, count, TILE), jnp.bfloat16)],
        limit=8,
    )


def first_left_kernel(keep, came, _, send, kept):
    piece = kept.shape[1]
    kept[...] = keep[:, :piece] + came[:, :piece]
    send[...] = keep[:, piece:] + came[:, piece:]


def first_left(keep, came, after):
    pairs, tokens, width = keep.shape
    return small(
        first_left_kernel,
        "first_left",
        [(pairs, tokens // 2, width)] * 2,
        "vvo",
        (keep, came, after),
    )


def first_right_kernel(keep, came, _, send, kept):
    for i in range(kept.shape[0]):
        kept[i] = keep[2 * i] + came[2 * i]
        send[i] = keep[2 * i + 1] + came[2 * i + 1]


def first_right(keep, came, after):
    pairs, tokens, width = keep.shape
    return small(
        first_right_kernel,
        "first_right",
        [(pairs // 2, tokens, width)] * 2,
        "vvo",
        (keep, came, after),
    )


def second_kernel(keep_l, came_l, keep_r, came_r, _, send_l, left, send_r, right):
    piece = left.shape[1]
    for i in range(left.shape[0]):
        left[i] = keep_l[2 * i] + came_l[2 * i]
        send_l[i] = keep_l[2 * i + 1] + came_l[2 * i + 1]
        right[i] = keep_r[i, :piece] + came_r[i, :piece]
        send_r[i] = keep_r[i, piece:] + came_r[i, piece:]


def second_sum(keep_l, came_l, keep_r, came_r, after):
    lines = keep_r.shape[0]
    _, piece, middle = keep_l.shape
    return small(
        second_kernel,
        "second_sum",
        [(lines, piece, middle)] * 4,
        "vvvvo",
        (keep_l, came_l, keep_r, came_r, after),
        work=1 << 36,
    )


def third_kernel(left, came_l, right, came_r, _, *outs):
    middle = left.shape[-1]
    for columns, one, other in ((slice(0, middle), left, came_l), (slice(middle, None), right, came_r)):
        for i, out in enumerate(outs):
            out[:, columns] = (one[i].astype(jnp.float32) + other[i].astype(jnp.float32)).astype(
                out.dtype
            )


def third_sum(offsets, left, came_l, right, came_r, after):
    _, piece, middle = left.shape
    return small(
        third_kernel,
        "third_sum",
        [
            jax.ShapeDtypeStruct((piece, 2 * middle), jnp.float32 if r == 0 else jnp.bfloat16)
            for r in offsets
        ],
        "vvvvo",
        (left, came_l, right, came_r, after),
        work=1 << 36,
    )


def last_kernel(*refs):
    total = refs[0][...]
    for ref in refs[1:-1]:
        total = total + ref[...].astype(jnp.float32)
    refs[-1][...] = total


def tokens_body(cotangent, gates, expert_ids, saved_gate, saved_up, w_gate, w_up, w_down):
    owners = lax.axis_size("expert")
    row_count, feature_dim = cotangent.shape
    capacity = saved_gate.shape[2] // owners
    lines = owners // 4
    piece = row_count // 2
    middle = feature_dim // 2
    me, half = lax.axis_index("expert"), lax.axis_index("tp")
    place = jnp.stack([me % 2, me // 2 % 2, me // 4, half]).astype(jnp.int32)

    part, table = prepare(place, cotangent, gates.T, expert_ids.T, piece)
    first = swap(part, "expert", 2)
    own_c, table_c = swap(cotangent, "expert", 1), swap(table, "expert", 1)
    gathered, saved = [], None

    def compute(index, after):
        offsets, moved = CHUNKS[index], gathered[index]
        line, line_c, _, _, over, over_c = moved[:6]
        pick, pick_t, gate = route(
            offsets, place, table, table_c, line, line_c, over, over_c, capacity
        )
        grads = hidden(
            offsets, lines, place, cotangent, own_c, moved, pick, gate, w_down, saved, after
        )
        return grads, pick_t

    def spread(grads, pick_t, after):
        keep_l, send_l = sums(0, middle, grads, w_gate, w_up, pick_t, after)
        keep_r, send_r = sums(middle, middle, grads, w_gate, w_up, pick_t, send_l)
        return keep_l, swap(send_l, "expert", 1), keep_r, swap(send_r, "expert", 1), send_r

    for offsets in CHUNKS:
        pieces = [along_line(part, -r) for r in offsets if r != 0]
        if saved is None:
            line, part = relay(pieces[0], part)
            saved = turn(saved_gate, saved_up, line)
        else:
            line = stack(pieces, saved[0])
        side, over = swap(line, "tp", 1), swap(line, "expert", 2)
        if offsets[0] == 0:
            over, left, right = own_corner(place, cotangent, first, over, side)
            after = (left,)
        else:
            early = compute(0, line)
            left, right = corner(over, side, middle, early[0])
            early = spread(*early, left)
            after = (early[-1],)
        diag = join(swap(left, "tp", 1), swap(right, "expert", 2), *after)
        moved = []
        for array in (line, side, over, diag):
            moved += [array, swap(array, "expert", 1)]
        gathered.append(moved)

    def first_step(keep_l, came_l, keep_r, came_r, after):
        send_l, keep_l = first_left(keep_l, came_l, after)
        send_r, keep_r = first_right(keep_r, came_r, send_l)
        return keep_l, swap(send_l, "tp", 1), keep_r, swap(send_r, "expert", 2), send_r

    def second_step(offsets, sums_of_two, after, came):
        send_l, left, send_r, right = second_sum(*sums_of_two, after)
        came_l, came_r = swap(send_l, "expert", 2), swap(send_r, "tp", 1)
        rows = third_sum(offsets, left, came_l, right, came_r, send_l if came is None else came)
        return rows[0], [row if r == 0 else along_line(row, r) for r, row in zip(offsets, rows)], send_l

    early = first_step(*early[:4], gathered[1][6])
    late = spread(*compute(1, early[4]), early[4])
    done, early, after = second_step(CHUNKS[0], early[:4], early[4], None)
    late = first_step(*late[:4], after)
    _, late, _ = second_step(CHUNKS[1], late[:4], done, early[-1])
    terms = early + late
    return pl.pallas_call(
        last_kernel,
        out_shape=jax.ShapeDtypeStruct((piece, feature_dim), jnp.float32),
        compiler_params=pltpu.CompilerParams(vmem_limit_bytes=8 << 20),
        name="last_sum",
    )(*terms)


def body(*arrays):
    cotangent, gates, _, saved_gate = arrays[:4]
    owners = lax.axis_size("expert")
    fits = (
        owners == 16
        and lax.axis_size("tp") == 2
        and cotangent.shape[0] == 128
        and cotangent.shape[1] % (2 * TILE) == 0
        and gates.shape[1] == 8
        and saved_gate.shape[0] == 2
        and saved_gate.shape[2] // owners % 16 == 0
        and 4 * saved_gate.shape[2] // owners <= 256
    )
    return (tokens_body if fits else slots_body)(*arrays)


def solution(mesh):
    in_specs = (
        P("expert", None),
        P("expert", None),
        P("expert", None),
        P("expert", "tp", None),
        P("expert", "tp", None),
        P("expert", "tp", None),
        P("expert", "tp", None),
        P("expert", "tp", None),
    )
    out_specs = P(("expert", "tp"), None)
    return jax.shard_map(body, mesh=mesh, in_specs=in_specs, out_specs=out_specs, check_vma=False)
```

```python
import functools

import jax
import jax.numpy as jnp
from jax import lax
from jax.experimental import pallas as pl
from jax.experimental.pallas import tpu as pltpu
from jax.sharding import PartitionSpec as P


def route_slots(expert_ids, expert_total):
    flat_ids = expert_ids.reshape(-1)
    one_hot = (flat_ids[:, None] == jnp.arange(expert_total, dtype=jnp.int32)[None, :]).astype(
        jnp.int32
    )
    before = jnp.cumsum(one_hot, axis=0) - one_hot
    return (flat_ids, jnp.sum(before * one_hot, axis=1))


def expert_step(arrived, saved_gate, saved_up, w_gate, w_up, w_down):
    hidden_grad = jnp.einsum("efd,esd->efs", w_down, arrived, preferred_element_type=jnp.float32)
    gate_value = saved_gate.astype(jnp.float32)
    up_value = saved_up.astype(jnp.float32)
    sigmoid_gate = jax.nn.sigmoid(gate_value)
    up_grad = (hidden_grad * gate_value * sigmoid_gate).astype(jnp.bfloat16)
    gate_grad = (
        hidden_grad * up_value * sigmoid_gate * (1.0 + gate_value * (1.0 - sigmoid_gate))
    ).astype(jnp.bfloat16)
    partial_value = jnp.einsum(
        "efs,efd->esd", gate_grad, w_gate, preferred_element_type=jnp.float32
    )
    partial_value = partial_value + jnp.einsum(
        "efs,efd->esd", up_grad, w_up, preferred_element_type=jnp.float32
    )
    return partial_value.astype(jnp.bfloat16)


def slots_body(cotangent, gates, expert_ids, saved_gate, saved_up, w_gate, w_up, w_down):
    owners = lax.axis_size("expert")
    row_count, feature_dim = cotangent.shape
    top_count = expert_ids.shape[1]
    local_count, _, slot_count = saved_gate.shape
    capacity = slot_count // owners
    flat_ids, slot_pos = route_slots(expert_ids, local_count * owners)
    target = flat_ids % local_count * slot_count + flat_ids // local_count * capacity + slot_pos
    scaled = (gates[:, :, None] * cotangent.astype(jnp.float32)[:, None, :]).astype(jnp.bfloat16)
    scaled = scaled.reshape(row_count * top_count, feature_dim)
    outgoing = (
        jnp.zeros((local_count * slot_count, feature_dim), jnp.bfloat16).at[target].set(scaled)
    )
    outgoing = outgoing.reshape(local_count, slot_count, feature_dim)
    arrived = lax.all_to_all(outgoing, "expert", split_axis=1, concat_axis=1, tiled=True)
    partial_value = expert_step(arrived, saved_gate, saved_up, w_gate, w_up, w_down)
    returned = lax.all_to_all(partial_value, "expert", split_axis=1, concat_axis=1, tiled=True)
    picked = returned.reshape(local_count * slot_count, feature_dim)[target].astype(jnp.float32)
    combined = jnp.sum(picked.reshape(row_count, top_count, feature_dim), axis=1)
    return lax.psum_scatter(combined, "tp", scatter_dimension=0, tiled=True)


CHUNKS = ((0, 2), (3, 1))
TILE = 512


def swap(value, axis, step):
    count = lax.axis_size(axis)
    return lax.ppermute(value, axis, [(i, i ^ step) for i in range(count)])


def along_line(value, shift):
    count = lax.axis_size("expert")
    return lax.ppermute(value, "expert", [(i, (i + 4 * shift) % count) for i in range(count)])


def small(kernel, name, outs, kinds, operands, scratch=(), limit=8, work=0):
    spaces = {"s": pltpu.SMEM, "v": pltpu.VMEM, "h": pltpu.HBM, "o": pl.ANY}
    return pl.pallas_call(
        kernel,
        out_shape=[
            out if hasattr(out, "dtype") else jax.ShapeDtypeStruct(out, jnp.bfloat16) for out in outs
        ],
        in_specs=[pl.BlockSpec(memory_space=spaces[kind]) for kind in kinds],
        scratch_shapes=list(scratch),
        compiler_params=pltpu.CompilerParams(vmem_limit_bytes=limit << 20),
        cost_estimate=pl.CostEstimate(flops=work, bytes_accessed=work >> 8, transcendentals=0),
        name=name,
    )(*operands)


def prepare_kernel(place, tokens, gates_any, ids_any, first, table, gates, ids, sems):
    piece = first.shape[0]
    width = first.shape[1] - table.shape[1]
    near = pl.multiple_of(place[3] * piece, piece)
    copies = [
        pltpu.make_async_copy(gates_any, gates, sems.at[0]),
        pltpu.make_async_copy(ids_any, ids, sems.at[1]),
        pltpu.make_async_copy(
            tokens.at[pl.ds(near, piece), :], first.at[:, pl.ds(0, width)], sems.at[2]
        ),
    ]
    for copy in copies:
        copy.start()
    copies[0].wait()
    copies[1].wait()
    rest = gates[...]
    terms = []
    for _ in range(3):
        term = rest.astype(jnp.bfloat16).astype(jnp.float32)
        terms.append(term)
        rest = rest - term
    terms.append(ids[...].astype(jnp.float32))
    unused = piece - 4 * gates.shape[0]
    terms.append(jnp.zeros((unused, gates.shape[1]), jnp.float32))
    packed = jnp.concatenate(terms, axis=0).astype(jnp.bfloat16)
    first[:, width:] = packed
    table[...] = packed
    copies[2].wait()


def prepare(place, cotangent, gates, ids, piece):
    return small(
        prepare_kernel,
        "prepare",
        [(piece, cotangent.shape[1] + 128), (piece, 128)],
        "shhh",
        (place, cotangent, gates, ids),
        [
            pltpu.VMEM(gates.shape, jnp.float32),
            pltpu.VMEM(ids.shape, jnp.int32),
            pltpu.SemaphoreType.DMA((3,)),
        ],
        limit=60,
    )


def relay_kernel(*refs):
    count = len(refs) // 2
    for source, target in zip(refs[:count], refs[len(refs) - count:]):
        target[...] = source[...]


def relay(pieces, *after, work=0):
    return small(
        relay_kernel,
        "relay",
        [piece.shape for piece in pieces],
        "v" * len(pieces) + "o" * len(after),
        (*pieces, *after),
        work=work,
    )


def turn_kernel(gate, up, _, gate_t, up_t):
    tile = 128
    for source, target in ((gate, gate_t), (up, up_t)):
        for e in range(source.shape[0]):
            for at in range(0, source.shape[2], tile):
                target[e, at:at + tile] = source[e, :, at:at + tile].astype(jnp.float32).T.astype(
                    jnp.bfloat16
                )


def turn(saved_gate, saved_up, after):
    count, units, slots = saved_gate.shape
    return small(
        turn_kernel,
        "turn",
        [(count, slots, units)] * 2,
        "vvo",
        (saved_gate, saved_up, after),
        limit=12,
    )


def corner_kernel(place, tokens, *refs):
    *sources, _, left, right = refs
    count, piece, middle = left.shape
    overs, sides = sources[:count], sources[count:]
    for i, over in enumerate(overs):
        left[i] = over[:, :middle]
    if len(sides) < count:
        far = pl.multiple_of((1 - place[3]) * piece, piece)
        right[0] = tokens[pl.ds(far, piece), middle:]
    for i, side in enumerate(sides):
        right[count - len(sides) + i] = side[:, middle:2 * middle]


def corner(place, cotangent, overs, sides, after):
    dims = (len(overs), overs[0].shape[0], cotangent.shape[1] // 2)
    return small(
        corner_kernel,
        "corner",
        [dims] * 2,
        "sv" + "v" * (len(overs) + len(sides)) + "o",
        (place, cotangent, *overs, *sides, after),
    )


def join_kernel(left, right, *refs):
    result = refs[-1]
    middle = left.shape[-1]
    result[:, :, :middle] = left[...]
    result[:, :, middle:] = right[...]


def join(left, right, *after, work=0):
    dims = left.shape
    return small(
        join_kernel,
        "join",
        [dims[:-1] + (2 * dims[-1],)],
        "vv" + "o" * len(after),
        (left, right, *after),
        work=work,
    )[0]


def pair_base(place, line_count, r, ry, width):
    line = lax.rem(place[2] + r, line_count)
    row = place[1] if ry == 0 else 1 - place[1]
    return pl.multiple_of((line * 2 + row) * width, width)


def route_kernel(offsets, capacity, place, *refs):
    nears, overs = refs[:2 * len(offsets)], refs[2 * len(offsets):4 * len(offsets)]
    pick, pick_t, gate, hits, gates = refs[-5:]
    tokens = pick.shape[2] // 2
    core, row, line, half = place[0], place[1], place[2], place[3]
    first = (line * 4 + row * 2 + core) * 2
    for i, r in enumerate(offsets):
        for ry in range(2):
            tables = []
            for c in range(2):
                source = (nears, overs)[ry][2 * i + c]
                table = source[:32, source.shape[1] - 128:]
                tables.append(table.astype(jnp.float32))
            swapped = core > 0
            ordered = [
                jnp.where(swapped, tables[1], tables[0]), jnp.where(swapped, tables[0], tables[1])
            ]
            for c in range(2):
                block = ordered[c]
                value = block[0:8] + block[8:16] + block[16:24]
                for e in range(2):
                    named = block[24:32] == (first + e).astype(jnp.float32)
                    at = ((i * 2 + ry) * 2 + c) * 2 + e
                    hits[at:at + 1] = jnp.sum(named.astype(jnp.float32), axis=0, keepdims=True)
                    gates[at:at + 1] = jnp.sum(
                        jnp.where(named, value, 0.0), axis=0, keepdims=True
                    )
    earlier = lax.broadcasted_iota(jnp.int32, (tokens, tokens), 0) < lax.broadcasted_iota(
        jnp.int32, (tokens, tokens), 1
    )
    hit = hits[...]
    slot = jnp.dot(
        hit.astype(jnp.bfloat16),
        earlier.astype(jnp.float32).astype(jnp.bfloat16),
        preferred_element_type=jnp.float32,
    )
    slot = jnp.where(hit > 0.5, slot, -1.0)
    turned = half > 0
    slot = jnp.where(turned, pltpu.roll(slot, tokens // 2, 1), slot)
    weight = jnp.where(turned, pltpu.roll(gates[...], tokens // 2, 1), gates[...])
    order = lax.broadcasted_iota(jnp.int32, (capacity, tokens), 0).astype(jnp.float32)
    for p in range(pick.shape[0]):
        rows = []
        for e in range(2):
            for c in range(2):
                at = (p * 2 + c) * 2 + e
                ones = (order == slot[at:at + 1]).astype(jnp.float32)
                column = jnp.sum(ones * weight[at:at + 1], axis=1, keepdims=True)
                place_in = (e * 2 + c) * capacity
                gate[p, place_in:place_in + capacity] = jnp.broadcast_to(
                    column, (capacity, gate.shape[2])
                )
                own_core = (core == c).astype(jnp.float32)
                rows.append(jnp.concatenate([ones * own_core, ones * (1.0 - own_core)], axis=1))
        matrix = jnp.concatenate(rows, axis=0)
        pick[p] = matrix.astype(jnp.bfloat16)
        count = matrix.shape[0]
        square = jnp.concatenate(
            [matrix, jnp.zeros((2 * tokens - count, 2 * tokens), jnp.float32)], axis=0
        )
        pick_t[p] = square.T[:, :count].astype(jnp.bfloat16)


def route(offsets, place, nears, overs, capacity, *after):
    tokens = 2 * overs[0].shape[0]
    pairs = 2 * len(offsets)
    rows = 4 * capacity
    return small(
        functools.partial(route_kernel, offsets, capacity),
        "route",
        [
            (pairs, rows, 2 * tokens),
            (pairs, 2 * tokens, rows),
            jax.ShapeDtypeStruct((pairs, rows, 128), jnp.float32),
        ],
        "s" + "v" * (len(nears) + len(overs)) + "o" * len(after),
        (place, *nears, *overs, *after),
        [pltpu.VMEM((4 * pairs, tokens), jnp.float32)] * 2,
    )


def hidden_kernel(offsets, line_count, place, *refs):
    *sources, pick, gate, w_down, saved_gate, saved_up, _, grads, slots = refs
    nears, sides, overs, diag = (
        sources[2 * at * len(offsets):2 * (at + 1) * len(offsets)] for at in range(4)
    )
    _, piece, width = diag[0].shape
    rows = pick.shape[1] // 2
    units = w_down.shape[1]
    near = pl.multiple_of(place[3] * piece, piece)
    far = pl.multiple_of((1 - place[3]) * piece, piece)

    @pl.loop(0, width // TILE)
    def _(k):
        at = pl.ds(pl.multiple_of(k * TILE, TILE), TILE)
        for i, r in enumerate(offsets):
            for ry in range(2):
                parts = []
                for c in range(2):
                    if ry == 1:
                        parts += [overs[2 * i + c][:, at], diag[c][i, :, at]]
                    elif r == 0:
                        group = nears[2 * i + c]
                        parts += [group[pl.ds(near, piece), at], group[pl.ds(far, piece), at]]
                    else:
                        parts += [nears[2 * i + c][:, at], sides[2 * i + c][:, at]]
                p = i * 2 + ry
                picked = jnp.dot(
                    pick[p], jnp.concatenate(parts, axis=0), preferred_element_type=jnp.float32
                )
                weight = gate[p]
                weight = jnp.concatenate([weight] * (TILE // weight.shape[1]), axis=1)
                scaled = (picked * weight).astype(jnp.bfloat16)
                slots[0, p * rows:(p + 1) * rows, at] = scaled[:rows]
                slots[1, p * rows:(p + 1) * rows, at] = scaled[rows:]

    for e in range(2):
        total = lax.dot_general(
            slots[e], w_down[e], (((1,), (1,)), ((), ())), preferred_element_type=jnp.float32
        )
        for i, r in enumerate(offsets):
            for ry in range(2):
                p = i * 2 + ry
                mine = slice(p * rows, (p + 1) * rows)
                saved = pl.ds(pair_base(place, line_count, r, ry, rows), rows)
                hidden_grad = total[mine]
                gate_value = saved_gate[e, saved, :].astype(jnp.float32)
                up_value = saved_up[e, saved, :].astype(jnp.float32)
                sigmoid_gate = jax.nn.sigmoid(gate_value)
                grads[e, mine, units:] = (hidden_grad * gate_value * sigmoid_gate).astype(
                    jnp.bfloat16
                )
                grads[e, mine, :units] = (
                    hidden_grad * up_value * sigmoid_gate * (1.0 + gate_value * (1.0 - sigmoid_gate))
                ).astype(jnp.bfloat16)


def hidden(offsets, line_count, place, sources, pick, gate, w_down, saved, after):
    _, units, width = w_down.shape
    count = pick.shape[0] * pick.shape[1] // 2
    return small(
        functools.partial(hidden_kernel, offsets, line_count),
        "hidden",
        [(2, count, 2 * units)],
        "s" + "v" * (len(sources) + 5) + "o",
        (place, *sources, pick, gate, w_down, *saved, after),
        [pltpu.VMEM((2, count, width), jnp.bfloat16)],
        limit=12,
    )[0]


def sums_kernel(offset, grads, w_gate, w_up, pick_t, _, keep, send, slots):
    rows = pick_t.shape[2] // 2
    tokens = pick_t.shape[1] // 2

    @pl.loop(0, keep.shape[2] // TILE)
    def _(k):
        at = pl.ds(pl.multiple_of(k * TILE, TILE), TILE)
        source = pl.ds(pl.multiple_of(offset + k * TILE, TILE), TILE)
        for e in range(2):
            weights = jnp.concatenate([w_gate[e, :, source], w_up[e, :, source]], axis=0)
            slots[e] = jnp.dot(grads[e], weights, preferred_element_type=jnp.float32).astype(
                jnp.bfloat16
            )
        for p in range(pick_t.shape[0]):
            mine = slice(p * rows, (p + 1) * rows)
            both = jnp.concatenate([slots[0, mine], slots[1, mine]], axis=0)
            total = jnp.dot(pick_t[p], both, preferred_element_type=jnp.float32).astype(
                jnp.bfloat16
            )
            keep[p, :, at] = total[:tokens]
            send[p, :, at] = total[tokens:]


def sums(offset, width, grads, w_gate, w_up, pick_t, after, work=0):
    pairs, tokens, _ = pick_t.shape
    _, count, units = grads.shape
    return small(
        functools.partial(sums_kernel, offset),
        "sums",
        [(pairs, tokens // 2, width)] * 2,
        "vvvvo",
        (grads, w_gate, w_up, pick_t, after),
        [pltpu.VMEM((2, count, TILE), jnp.bfloat16)],
        limit=8,
        work=work,
    )


def first_left_kernel(keep, came, _, send, kept):
    piece = kept.shape[1]
    kept[...] = keep[:, :piece] + came[:, :piece]
    send[...] = keep[:, piece:] + came[:, piece:]


def first_left(keep, came, after):
    pairs, tokens, width = keep.shape
    return small(
        first_left_kernel,
        "first_left",
        [(pairs, tokens // 2, width)] * 2,
        "vvo",
        (keep, came, after),
    )


def first_right_kernel(keep, came, _, send, kept):
    for i in range(kept.shape[0]):
        kept[i] = keep[2 * i] + came[2 * i]
        send[i] = keep[2 * i + 1] + came[2 * i + 1]


def first_right(keep, came, after):
    pairs, tokens, width = keep.shape
    return small(
        first_right_kernel,
        "first_right",
        [(pairs // 2, tokens, width)] * 2,
        "vvo",
        (keep, came, after),
    )


def second_kernel(keep_l, came_l, keep_r, came_r, _, send_l, left, send_r, right):
    piece = left.shape[1]
    for i in range(left.shape[0]):
        left[i] = keep_l[2 * i] + came_l[2 * i]
        send_l[i] = keep_l[2 * i + 1] + came_l[2 * i + 1]
        right[i] = keep_r[i, :piece] + came_r[i, :piece]
        send_r[i] = keep_r[i, piece:] + came_r[i, piece:]


def second_sum(keep_l, came_l, keep_r, came_r, after):
    lines = keep_r.shape[0]
    _, piece, middle = keep_l.shape
    return small(
        second_kernel,
        "second_sum",
        [(lines, piece, middle)] * 4,
        "vvvvo",
        (keep_l, came_l, keep_r, came_r, after),
        work=1 << 36,
    )


def third_kernel(left, came_l, right, came_r, _, *outs):
    middle = left.shape[-1]
    for columns, one, other in ((slice(0, middle), left, came_l), (slice(middle, None), right, came_r)):
        for i, out in enumerate(outs):
            out[:, columns] = (one[i].astype(jnp.float32) + other[i].astype(jnp.float32)).astype(
                out.dtype
            )


def third_sum(offsets, left, came_l, right, came_r, after):
    _, piece, middle = left.shape
    return small(
        third_kernel,
        "third_sum",
        [
            jax.ShapeDtypeStruct((piece, 2 * middle), jnp.float32 if r == 0 else jnp.bfloat16)
            for r in offsets
        ],
        "vvvvo",
        (left, came_l, right, came_r, after),
        work=1 << 36,
    )


def last_kernel(*refs):
    total = refs[0][...]
    for ref in refs[1:-1]:
        total = total + ref[...].astype(jnp.float32)
    refs[-1][...] = total


def tokens_body(cotangent, gates, expert_ids, saved_gate, saved_up, w_gate, w_up, w_down):
    owners = lax.axis_size("expert")
    row_count, feature_dim = cotangent.shape
    capacity = saved_gate.shape[2] // owners
    lines = owners // 4
    piece = row_count // 2
    middle = feature_dim // 2
    me, half = lax.axis_index("expert"), lax.axis_index("tp")
    place = jnp.stack([me % 2, me // 2 % 2, me // 4, half]).astype(jnp.int32)

    def both_cores(arrays):
        return [each for array in arrays for each in (array, swap(array, "expert", 1))]

    def sums_by_token(offset, grads, pick_t, after, work=0):
        keep, send = sums(offset, middle, grads, w_gate, w_up, pick_t, after, work)
        return [keep, swap(send, "expert", 1)], send

    part, table = prepare(place, cotangent, gates.T, expert_ids.T, piece)
    first = swap(part, "expert", 2)
    near, third, second = CHUNKS[0][1], *CHUNKS[1]
    own, tables = both_cores([cotangent]), both_cores([table])

    line, part = relay([along_line(part, -near), part])
    side, over = swap(line, "tp", 1), swap(line, "expert", 2)
    later = [along_line(part, -third), along_line(part, -second)]
    saved = turn(saved_gate, saved_up, line)
    left, right = corner(place, cotangent, [first, over], [side], line)
    lines_0, sides_0, overs_0 = both_cores([line]), both_cores([side]), both_cores([first, over])
    pick, pick_t, gate = route(
        CHUNKS[0], place, tables + lines_0, overs_0, capacity, own[1], sides_0[1], saved[0]
    )
    left_came, right_came = swap(left, "tp", 1), swap(right, "expert", 2)
    lines_1, sides_1, overs_1 = [], [], []
    after = saved[0]
    for piece_of in later:
        line, = relay([piece_of], after)
        after = line
        lines_1.append(line)
        side, over = swap(line, "tp", 1), swap(line, "expert", 2)
        if not sides_1:
            side, over = relay([side, over], work=1 << 30)
        sides_1.append(side)
        overs_1.append(over)
    diag = both_cores([join(left_came, right_came, line)])
    grads = hidden(
        CHUNKS[0], lines, place, own + lines_0 + own + sides_0 + overs_0 + diag, pick, gate, w_down,
        saved, overs_1[0],
    )
    early_l, after = sums_by_token(0, grads, pick_t, grads)
    left, right = corner(place, cotangent, overs_1, sides_1, after)
    early_r, after = sums_by_token(middle, grads, pick_t, left, 1 << 36)
    lines_1, sides_1, overs_1 = both_cores(lines_1), both_cores(sides_1), both_cores(overs_1)
    pick, pick_t, gate = route(CHUNKS[1], place, lines_1, overs_1, capacity)

    def first_step(keep_l, came_l, keep_r, came_r, after):
        send_l, keep_l = first_left(keep_l, came_l, after)
        send_r, keep_r = first_right(keep_r, came_r, send_l)
        return keep_l, swap(send_l, "tp", 1), keep_r, swap(send_r, "expert", 2), send_r

    def second_step(offsets, sums_of_two, after, came):
        send_l, left, send_r, right = second_sum(*sums_of_two, after)
        came_l, came_r = swap(send_l, "expert", 2), swap(send_r, "tp", 1)
        rows = third_sum(offsets, left, came_l, right, came_r, send_l if came is None else came)
        return rows[0], [row if r == 0 else along_line(row, r) for r, row in zip(offsets, rows)], send_l

    diag = join(swap(left, "tp", 1), swap(right, "expert", 2), after, work=8589934592)
    diag = both_cores([diag])
    early = first_step(*early_l, *early_r, diag[0])
    grads = hidden(
        CHUNKS[1], lines, place, lines_1 + sides_1 + overs_1 + diag, pick, gate, w_down, saved, early[4]
    )
    late_l, after = sums_by_token(0, grads, pick_t, grads)
    late_r, _ = sums_by_token(middle, grads, pick_t, after)
    done, early, after = second_step(CHUNKS[0], early[:4], early[4], None)
    late = first_step(*late_l, *late_r, after)
    _, late, _ = second_step(CHUNKS[1], late[:4], done, early[-1])
    terms = early + late
    return pl.pallas_call(
        last_kernel,
        out_shape=jax.ShapeDtypeStruct((piece, feature_dim), jnp.float32),
        compiler_params=pltpu.CompilerParams(vmem_limit_bytes=8 << 20),
        name="last_sum",
    )(*terms)


def body(*arrays):
    cotangent, gates, _, saved_gate = arrays[:4]
    owners = lax.axis_size("expert")
    fits = (
        owners == 16
        and lax.axis_size("tp") == 2
        and cotangent.shape[0] == 128
        and cotangent.shape[1] % (2 * TILE) == 0
        and gates.shape[1] == 8
        and saved_gate.shape[0] == 2
        and saved_gate.shape[2] // owners % 16 == 0
        and 4 * saved_gate.shape[2] // owners <= 256
    )
    return (tokens_body if fits else slots_body)(*arrays)


def solution(mesh):
    in_specs = (
        P("expert", None),
        P("expert", None),
        P("expert", None),
        P("expert", "tp", None),
        P("expert", "tp", None),
        P("expert", "tp", None),
        P("expert", "tp", None),
        P("expert", "tp", None),
    )
    out_specs = P(("expert", "tp"), None)
    return jax.shard_map(body, mesh=mesh, in_specs=in_specs, out_specs=out_specs, check_vma=False)
```

```python
import functools

import jax
import jax.numpy as jnp
from jax import lax
from jax.experimental import pallas as pl
from jax.experimental.pallas import tpu as pltpu
from jax.sharding import PartitionSpec as P


def route_slots(expert_ids, expert_total):
    flat_ids = expert_ids.reshape(-1)
    one_hot = (flat_ids[:, None] == jnp.arange(expert_total, dtype=jnp.int32)[None, :]).astype(
        jnp.int32
    )
    before = jnp.cumsum(one_hot, axis=0) - one_hot
    return (flat_ids, jnp.sum(before * one_hot, axis=1))


def expert_step(arrived, saved_gate, saved_up, w_gate, w_up, w_down):
    hidden_grad = jnp.einsum("efd,esd->efs", w_down, arrived, preferred_element_type=jnp.float32)
    gate_value = saved_gate.astype(jnp.float32)
    up_value = saved_up.astype(jnp.float32)
    sigmoid_gate = jax.nn.sigmoid(gate_value)
    up_grad = (hidden_grad * gate_value * sigmoid_gate).astype(jnp.bfloat16)
    gate_grad = (
        hidden_grad * up_value * sigmoid_gate * (1.0 + gate_value * (1.0 - sigmoid_gate))
    ).astype(jnp.bfloat16)
    partial_value = jnp.einsum(
        "efs,efd->esd", gate_grad, w_gate, preferred_element_type=jnp.float32
    )
    partial_value = partial_value + jnp.einsum(
        "efs,efd->esd", up_grad, w_up, preferred_element_type=jnp.float32
    )
    return partial_value.astype(jnp.bfloat16)


def slots_body(cotangent, gates, expert_ids, saved_gate, saved_up, w_gate, w_up, w_down):
    owners = lax.axis_size("expert")
    row_count, feature_dim = cotangent.shape
    top_count = expert_ids.shape[1]
    local_count, _, slot_count = saved_gate.shape
    capacity = slot_count // owners
    flat_ids, slot_pos = route_slots(expert_ids, local_count * owners)
    target = flat_ids % local_count * slot_count + flat_ids // local_count * capacity + slot_pos
    scaled = (gates[:, :, None] * cotangent.astype(jnp.float32)[:, None, :]).astype(jnp.bfloat16)
    scaled = scaled.reshape(row_count * top_count, feature_dim)
    outgoing = (
        jnp.zeros((local_count * slot_count, feature_dim), jnp.bfloat16).at[target].set(scaled)
    )
    outgoing = outgoing.reshape(local_count, slot_count, feature_dim)
    arrived = lax.all_to_all(outgoing, "expert", split_axis=1, concat_axis=1, tiled=True)
    partial_value = expert_step(arrived, saved_gate, saved_up, w_gate, w_up, w_down)
    returned = lax.all_to_all(partial_value, "expert", split_axis=1, concat_axis=1, tiled=True)
    picked = returned.reshape(local_count * slot_count, feature_dim)[target].astype(jnp.float32)
    combined = jnp.sum(picked.reshape(row_count, top_count, feature_dim), axis=1)
    return lax.psum_scatter(combined, "tp", scatter_dimension=0, tiled=True)


CHUNKS = ((0, 2), (1, 3))
TILE = 512


def swap(value, axis, step):
    count = lax.axis_size(axis)
    return lax.ppermute(value, axis, [(i, i ^ step) for i in range(count)])


def along_line(value, shift):
    count = lax.axis_size("expert")
    return lax.ppermute(value, "expert", [(i, (i + 4 * shift) % count) for i in range(count)])


def small(kernel, name, outs, kinds, operands, scratch=(), limit=8, work=0):
    spaces = {"s": pltpu.SMEM, "v": pltpu.VMEM, "h": pltpu.HBM, "o": pl.ANY}
    return pl.pallas_call(
        kernel,
        out_shape=[
            out if hasattr(out, "dtype") else jax.ShapeDtypeStruct(out, jnp.bfloat16) for out in outs
        ],
        in_specs=[pl.BlockSpec(memory_space=spaces[kind]) for kind in kinds],
        scratch_shapes=list(scratch),
        compiler_params=pltpu.CompilerParams(vmem_limit_bytes=limit << 20),
        cost_estimate=pl.CostEstimate(flops=work, bytes_accessed=work >> 8, transcendentals=0),
        name=name,
    )(*operands)


def prepare_kernel(place, tokens, gates_any, ids_any, first, table, gates, ids, sems):
    piece = first.shape[0]
    width = first.shape[1] - table.shape[1]
    near = pl.multiple_of(place[3] * piece, piece)
    copies = [
        pltpu.make_async_copy(gates_any, gates, sems.at[0]),
        pltpu.make_async_copy(ids_any, ids, sems.at[1]),
        pltpu.make_async_copy(
            tokens.at[pl.ds(near, piece), :], first.at[:, pl.ds(0, width)], sems.at[2]
        ),
    ]
    for copy in copies:
        copy.start()
    copies[0].wait()
    copies[1].wait()
    rest = gates[...]
    terms = []
    for _ in range(3):
        term = rest.astype(jnp.bfloat16).astype(jnp.float32)
        terms.append(term)
        rest = rest - term
    terms.append(ids[...].astype(jnp.float32))
    unused = piece - 4 * gates.shape[0]
    terms.append(jnp.zeros((unused, gates.shape[1]), jnp.float32))
    packed = jnp.concatenate(terms, axis=0).astype(jnp.bfloat16)
    first[:, width:] = packed
    table[...] = packed
    copies[2].wait()


def prepare(place, cotangent, gates, ids, piece):
    return small(
        prepare_kernel,
        "prepare",
        [(piece, cotangent.shape[1] + 128), (piece, 128)],
        "shhh",
        (place, cotangent, gates, ids),
        [
            pltpu.VMEM(gates.shape, jnp.float32),
            pltpu.VMEM(ids.shape, jnp.int32),
            pltpu.SemaphoreType.DMA((3,)),
        ],
        limit=60,
    )


def stack_kernel(*refs):
    lines = refs[-1]
    for r in range(lines.shape[0]):
        lines[r] = refs[r][...]


def stack(pieces, *after):
    return small(
        stack_kernel,
        "stack",
        [(len(pieces),) + pieces[0].shape],
        "v" * len(pieces) + "o" * len(after),
        (*pieces, *after),
    )[0]


def relay_kernel(came, part, line, following):
    line[0] = came[...]
    following[...] = part[...]


def relay(came, part):
    return small(
        relay_kernel, "relay", [(1,) + came.shape, part.shape], "vv", (came, part)
    )


def turn_kernel(gate, up, _, gate_t, up_t):
    tile = 128
    for source, target in ((gate, gate_t), (up, up_t)):
        for e in range(source.shape[0]):
            for at in range(0, source.shape[2], tile):
                target[e, at:at + tile] = source[e, :, at:at + tile].astype(jnp.float32).T.astype(
                    jnp.bfloat16
                )


def turn(saved_gate, saved_up, after):
    count, units, slots = saved_gate.shape
    return small(
        turn_kernel,
        "turn",
        [(count, slots, units)] * 2,
        "vvo",
        (saved_gate, saved_up, after),
        limit=12,
    )


def corner_kernel(place, tokens, first, over, side, whole_over, left, right, sem):
    _, piece, middle = left.shape
    far = pl.multiple_of((1 - place[3]) * piece, piece)
    copy = pltpu.make_async_copy(
        tokens.at[pl.ds(far, piece), pl.ds(middle, middle)], right.at[0], sem.at[0]
    )
    copy.start()
    whole_over[0] = first[...]
    whole_over[1:] = over[...]
    left[0] = first[:, :middle]
    left[1:] = over[:, :, :middle]
    right[1:] = side[:, :, middle:2 * middle]
    copy.wait()


def own_corner(place, cotangent, first, over, side):
    count, piece, width = over.shape
    middle = cotangent.shape[1] // 2
    return small(
        corner_kernel,
        "own_corner",
        [(count + 1, piece, width)] + [(count + 1, piece, middle)] * 2,
        "shvvv",
        (place, cotangent, first, over, side),
        (pltpu.SemaphoreType.DMA((1,)),),
    )


def plain_corner_kernel(over, side, _, left, right):
    middle = left.shape[-1]
    left[...] = over[:, :, :middle]
    right[...] = side[:, :, middle:2 * middle]


def corner(over, side, middle, after):
    return small(
        plain_corner_kernel,
        "corner",
        [over.shape[:2] + (middle,)] * 2,
        "vvo",
        (over, side, after),
    )


def join_kernel(left, right, *refs):
    result = refs[-1]
    middle = left.shape[-1]
    result[:, :, :middle] = left[...]
    result[:, :, middle:] = right[...]


def join(left, right, *after, work=0):
    dims = left.shape
    return small(
        join_kernel,
        "join",
        [dims[:-1] + (2 * dims[-1],)],
        "vv" + "o" * len(after),
        (left, right, *after),
        work=work,
    )[0]


def tokens_of(own, lines, r, offsets):
    if r == 0:
        return own[...]
    return lines[r_place(r, offsets)]


def r_place(r, offsets):
    return [offset for offset in offsets if offset != 0].index(r)


def pair_base(place, line_count, r, ry, width):
    line = lax.rem(place[2] + r, line_count)
    row = place[1] if ry == 0 else 1 - place[1]
    return pl.multiple_of((line * 2 + row) * width, width)


def route_kernel(offsets, capacity, place, own, own_c, lines, lines_c, over, over_c, pick, pick_t, gate,
                 hits, gates):
    tokens = pick.shape[2] // 2
    width = over.shape[2] - 128
    core, row, line, half = place[0], place[1], place[2], place[3]
    first = (line * 4 + row * 2 + core) * 2
    for i, r in enumerate(offsets):
        for ry in range(2):
            tables = []
            for c in range(2):
                if ry == 1:
                    table = (over, over_c)[c][i, :32, width:]
                elif r == 0:
                    table = (own, own_c)[c][:32]
                else:
                    table = (lines, lines_c)[c][r_place(r, offsets), :32, width:]
                tables.append(table.astype(jnp.float32))
            swapped = core > 0
            ordered = [
                jnp.where(swapped, tables[1], tables[0]), jnp.where(swapped, tables[0], tables[1])
            ]
            for c in range(2):
                block = ordered[c]
                value = block[0:8] + block[8:16] + block[16:24]
                for e in range(2):
                    named = block[24:32] == (first + e).astype(jnp.float32)
                    at = ((i * 2 + ry) * 2 + c) * 2 + e
                    hits[at:at + 1] = jnp.sum(named.astype(jnp.float32), axis=0, keepdims=True)
                    gates[at:at + 1] = jnp.sum(
                        jnp.where(named, value, 0.0), axis=0, keepdims=True
                    )
    earlier = lax.broadcasted_iota(jnp.int32, (tokens, tokens), 0) < lax.broadcasted_iota(
        jnp.int32, (tokens, tokens), 1
    )
    hit = hits[...]
    slot = jnp.dot(
        hit.astype(jnp.bfloat16),
        earlier.astype(jnp.float32).astype(jnp.bfloat16),
        preferred_element_type=jnp.float32,
    )
    slot = jnp.where(hit > 0.5, slot, -1.0)
    turned = half > 0
    slot = jnp.where(turned, pltpu.roll(slot, tokens // 2, 1), slot)
    weight = jnp.where(turned, pltpu.roll(gates[...], tokens // 2, 1), gates[...])
    order = lax.broadcasted_iota(jnp.int32, (capacity, tokens), 0).astype(jnp.float32)
    for p in range(pick.shape[0]):
        rows = []
        for e in range(2):
            for c in range(2):
                at = (p * 2 + c) * 2 + e
                ones = (order == slot[at:at + 1]).astype(jnp.float32)
                column = jnp.sum(ones * weight[at:at + 1], axis=1, keepdims=True)
                place_in = (e * 2 + c) * capacity
                gate[p, place_in:place_in + capacity] = jnp.broadcast_to(
                    column, (capacity, gate.shape[2])
                )
                own_core = (core == c).astype(jnp.float32)
                rows.append(jnp.concatenate([ones * own_core, ones * (1.0 - own_core)], axis=1))
        matrix = jnp.concatenate(rows, axis=0)
        pick[p] = matrix.astype(jnp.bfloat16)
        count = matrix.shape[0]
        square = jnp.concatenate(
            [matrix, jnp.zeros((2 * tokens - count, 2 * tokens), jnp.float32)], axis=0
        )
        pick_t[p] = square.T[:, :count].astype(jnp.bfloat16)


def route(offsets, place, table, table_c, lines, lines_c, over, over_c, capacity):
    tokens = 2 * over.shape[1]
    pairs = 2 * len(offsets)
    rows = 4 * capacity
    return small(
        functools.partial(route_kernel, offsets, capacity),
        "route",
        [
            (pairs, rows, 2 * tokens),
            (pairs, 2 * tokens, rows),
            jax.ShapeDtypeStruct((pairs, rows, 128), jnp.float32),
        ],
        "s" + "v" * 6,
        (place, table, table_c, lines, lines_c, over, over_c),
        [pltpu.VMEM((4 * pairs, tokens), jnp.float32)] * 2,
    )


def hidden_kernel(offsets, line_count, place, own, own_c, lines, lines_c, side, side_c, over, over_c,
                  diag, diag_c, pick, gate, w_down, saved_gate, saved_up, _, grads, slots):
    piece = over.shape[1]
    width = diag.shape[2]
    rows = pick.shape[1] // 2
    units = w_down.shape[1]
    near = pl.multiple_of(place[3] * piece, piece)
    far = pl.multiple_of((1 - place[3]) * piece, piece)

    @pl.loop(0, width // TILE)
    def _(k):
        at = pl.ds(pl.multiple_of(k * TILE, TILE), TILE)
        for i, r in enumerate(offsets):
            for ry in range(2):
                parts = []
                for c in range(2):
                    if ry == 1:
                        parts += [(over, over_c)[c][i, :, at], (diag, diag_c)[c][i, :, at]]
                    elif r == 0:
                        group = (own, own_c)[c]
                        parts += [group[pl.ds(near, piece), at], group[pl.ds(far, piece), at]]
                    else:
                        j = r_place(r, offsets)
                        parts += [(lines, lines_c)[c][j, :, at], (side, side_c)[c][j, :, at]]
                p = i * 2 + ry
                picked = jnp.dot(
                    pick[p], jnp.concatenate(parts, axis=0), preferred_element_type=jnp.float32
                )
                weight = gate[p]
                weight = jnp.concatenate([weight] * (TILE // weight.shape[1]), axis=1)
                scaled = (picked * weight).astype(jnp.bfloat16)
                slots[0, p * rows:(p + 1) * rows, at] = scaled[:rows]
                slots[1, p * rows:(p + 1) * rows, at] = scaled[rows:]

    for e in range(2):
        total = lax.dot_general(
            slots[e], w_down[e], (((1,), (1,)), ((), ())), preferred_element_type=jnp.float32
        )
        for i, r in enumerate(offsets):
            for ry in range(2):
                p = i * 2 + ry
                mine = slice(p * rows, (p + 1) * rows)
                saved = pl.ds(pair_base(place, line_count, r, ry, rows), rows)
                hidden_grad = total[mine]
                gate_value = saved_gate[e, saved, :].astype(jnp.float32)
                up_value = saved_up[e, saved, :].astype(jnp.float32)
                sigmoid_gate = jax.nn.sigmoid(gate_value)
                grads[e, mine, units:] = (hidden_grad * gate_value * sigmoid_gate).astype(
                    jnp.bfloat16
                )
                grads[e, mine, :units] = (
                    hidden_grad * up_value * sigmoid_gate * (1.0 + gate_value * (1.0 - sigmoid_gate))
                ).astype(jnp.bfloat16)


def hidden(offsets, line_count, place, own, own_c, moved, pick, gate, w_down, saved, after):
    width = own.shape[1]
    units = w_down.shape[1]
    count = pick.shape[0] * pick.shape[1] // 2
    return small(
        functools.partial(hidden_kernel, offsets, line_count),
        "hidden",
        [(2, count, 2 * units)],
        "s" + "v" * 15 + "o",
        (place, own, own_c, *moved, pick, gate, w_down, *saved, after),
        [pltpu.VMEM((2, count, width), jnp.bfloat16)],
        limit=12,
    )[0]


def sums_kernel(offset, grads, w_gate, w_up, pick_t, _, keep, send, slots):
    rows = pick_t.shape[2] // 2
    tokens = pick_t.shape[1] // 2

    @pl.loop(0, keep.shape[2] // TILE)
    def _(k):
        at = pl.ds(pl.multiple_of(k * TILE, TILE), TILE)
        source = pl.ds(pl.multiple_of(offset + k * TILE, TILE), TILE)
        for e in range(2):
            weights = jnp.concatenate([w_gate[e, :, source], w_up[e, :, source]], axis=0)
            slots[e] = jnp.dot(grads[e], weights, preferred_element_type=jnp.float32).astype(
                jnp.bfloat16
            )
        for p in range(pick_t.shape[0]):
            mine = slice(p * rows, (p + 1) * rows)
            both = jnp.concatenate([slots[0, mine], slots[1, mine]], axis=0)
            total = jnp.dot(pick_t[p], both, preferred_element_type=jnp.float32).astype(
                jnp.bfloat16
            )
            keep[p, :, at] = total[:tokens]
            send[p, :, at] = total[tokens:]


def sums(offset, width, grads, w_gate, w_up, pick_t, after, work=0):
    pairs, tokens, _ = pick_t.shape
    _, count, units = grads.shape
    return small(
        functools.partial(sums_kernel, offset),
        "sums",
        [(pairs, tokens // 2, width)] * 2,
        "vvvvo",
        (grads, w_gate, w_up, pick_t, after),
        [pltpu.VMEM((2, count, TILE), jnp.bfloat16)],
        limit=8,
        work=work,
    )


def first_left_kernel(keep, came, _, send, kept):
    piece = kept.shape[1]
    kept[...] = keep[:, :piece] + came[:, :piece]
    send[...] = keep[:, piece:] + came[:, piece:]


def first_left(keep, came, after):
    pairs, tokens, width = keep.shape
    return small(
        first_left_kernel,
        "first_left",
        [(pairs, tokens // 2, width)] * 2,
        "vvo",
        (keep, came, after),
    )


def first_right_kernel(keep, came, _, send, kept):
    for i in range(kept.shape[0]):
        kept[i] = keep[2 * i] + came[2 * i]
        send[i] = keep[2 * i + 1] + came[2 * i + 1]


def first_right(keep, came, after):
    pairs, tokens, width = keep.shape
    return small(
        first_right_kernel,
        "first_right",
        [(pairs // 2, tokens, width)] * 2,
        "vvo",
        (keep, came, after),
    )


def second_kernel(keep_l, came_l, keep_r, came_r, _, send_l, left, send_r, right):
    piece = left.shape[1]
    for i in range(left.shape[0]):
        left[i] = keep_l[2 * i] + came_l[2 * i]
        send_l[i] = keep_l[2 * i + 1] + came_l[2 * i + 1]
        right[i] = keep_r[i, :piece] + came_r[i, :piece]
        send_r[i] = keep_r[i, piece:] + came_r[i, piece:]


def second_sum(keep_l, came_l, keep_r, came_r, after):
    lines = keep_r.shape[0]
    _, piece, middle = keep_l.shape
    return small(
        second_kernel,
        "second_sum",
        [(lines, piece, middle)] * 4,
        "vvvvo",
        (keep_l, came_l, keep_r, came_r, after),
        work=1 << 36,
    )


def third_kernel(left, came_l, right, came_r, _, *outs):
    middle = left.shape[-1]
    for columns, one, other in ((slice(0, middle), left, came_l), (slice(middle, None), right, came_r)):
        for i, out in enumerate(outs):
            out[:, columns] = (one[i].astype(jnp.float32) + other[i].astype(jnp.float32)).astype(
                out.dtype
            )


def third_sum(offsets, left, came_l, right, came_r, after):
    _, piece, middle = left.shape
    return small(
        third_kernel,
        "third_sum",
        [
            jax.ShapeDtypeStruct((piece, 2 * middle), jnp.float32 if r == 0 else jnp.bfloat16)
            for r in offsets
        ],
        "vvvvo",
        (left, came_l, right, came_r, after),
        work=1 << 36,
    )


def last_kernel(*refs):
    total = refs[0][...]
    for ref in refs[1:-1]:
        total = total + ref[...].astype(jnp.float32)
    refs[-1][...] = total


def tokens_body(cotangent, gates, expert_ids, saved_gate, saved_up, w_gate, w_up, w_down):
    owners = lax.axis_size("expert")
    row_count, feature_dim = cotangent.shape
    capacity = saved_gate.shape[2] // owners
    lines = owners // 4
    piece = row_count // 2
    middle = feature_dim // 2
    me, half = lax.axis_index("expert"), lax.axis_index("tp")
    place = jnp.stack([me % 2, me // 2 % 2, me // 4, half]).astype(jnp.int32)

    part, table = prepare(place, cotangent, gates.T, expert_ids.T, piece)
    first = swap(part, "expert", 2)
    own_c, table_c = swap(cotangent, "expert", 1), swap(table, "expert", 1)
    gathered, saved = [], None

    def compute(index, after):
        offsets, moved = CHUNKS[index], gathered[index]
        line, line_c, _, _, over, over_c = moved[:6]
        pick, pick_t, gate = route(
            offsets, place, table, table_c, line, line_c, over, over_c, capacity
        )
        grads = hidden(
            offsets, lines, place, cotangent, own_c, moved, pick, gate, w_down, saved, after
        )
        return grads, pick_t

    def sums_by_token(offset, grads, pick_t, after, work=0):
        keep, send = sums(offset, middle, grads, w_gate, w_up, pick_t, after, work)
        return [keep, swap(send, "expert", 1)], send

    for offsets in CHUNKS:
        pieces = [along_line(part, -r) for r in offsets if r != 0]
        if saved is None:
            line, part = relay(pieces[0], part)
            saved = turn(saved_gate, saved_up, line)
        else:
            line = stack(pieces, saved[0])
        side, over = swap(line, "tp", 1), swap(line, "expert", 2)
        if offsets[0] == 0:
            over, left, right = own_corner(place, cotangent, first, over, side)
            after = (left,)
        else:
            early = compute(0, line)
            grads, pick_t = early
            early_l, after = sums_by_token(0, grads, pick_t, grads)
            left, right = corner(over, side, middle, after)
            early_r, after = sums_by_token(middle, grads, pick_t, left, 68719476736)
            after = (after,)
        diag = join(swap(left, "tp", 1), swap(right, "expert", 2), *after, work=8589934592)
        moved = []
        for array in (line, side, over, diag):
            moved += [array, swap(array, "expert", 1)]
        gathered.append(moved)

    def first_step(keep_l, came_l, keep_r, came_r, after):
        send_l, keep_l = first_left(keep_l, came_l, after)
        send_r, keep_r = first_right(keep_r, came_r, send_l)
        return keep_l, swap(send_l, "tp", 1), keep_r, swap(send_r, "expert", 2), send_r

    def second_step(offsets, sums_of_two, after, came):
        send_l, left, send_r, right = second_sum(*sums_of_two, after)
        came_l, came_r = swap(send_l, "expert", 2), swap(send_r, "tp", 1)
        rows = third_sum(offsets, left, came_l, right, came_r, send_l if came is None else came)
        return rows[0], [row if r == 0 else along_line(row, r) for r, row in zip(offsets, rows)], send_l

    early = first_step(*early_l, *early_r, gathered[1][6])
    grads, pick_t = compute(1, early[4])
    late_l, after = sums_by_token(0, grads, pick_t, grads)
    late_r, _ = sums_by_token(middle, grads, pick_t, after)
    done, early, after = second_step(CHUNKS[0], early[:4], early[4], None)
    late = first_step(*late_l, *late_r, after)
    _, late, _ = second_step(CHUNKS[1], late[:4], done, early[-1])
    terms = early + late
    return pl.pallas_call(
        last_kernel,
        out_shape=jax.ShapeDtypeStruct((piece, feature_dim), jnp.float32),
        compiler_params=pltpu.CompilerParams(vmem_limit_bytes=8 << 20),
        name="last_sum",
    )(*terms)


def body(*arrays):
    cotangent, gates, _, saved_gate = arrays[:4]
    owners = lax.axis_size("expert")
    fits = (
        owners == 16
        and lax.axis_size("tp") == 2
        and cotangent.shape[0] == 128
        and cotangent.shape[1] % (2 * TILE) == 0
        and gates.shape[1] == 8
        and saved_gate.shape[0] == 2
        and saved_gate.shape[2] // owners % 16 == 0
        and 4 * saved_gate.shape[2] // owners <= 256
    )
    return (tokens_body if fits else slots_body)(*arrays)


def solution(mesh):
    in_specs = (
        P("expert", None),
        P("expert", None),
        P("expert", None),
        P("expert", "tp", None),
        P("expert", "tp", None),
        P("expert", "tp", None),
        P("expert", "tp", None),
        P("expert", "tp", None),
    )
    out_specs = P(("expert", "tp"), None)
    return jax.shard_map(body, mesh=mesh, in_specs=in_specs, out_specs=out_specs, check_vma=False)
```

```python
import functools

import jax
import jax.numpy as jnp
from jax import lax
from jax.experimental import pallas as pl
from jax.experimental.pallas import tpu as pltpu
from jax.sharding import PartitionSpec as P


def route_slots(expert_ids, expert_total):
    flat_ids = expert_ids.reshape(-1)
    one_hot = (flat_ids[:, None] == jnp.arange(expert_total, dtype=jnp.int32)[None, :]).astype(
        jnp.int32
    )
    before = jnp.cumsum(one_hot, axis=0) - one_hot
    return (flat_ids, jnp.sum(before * one_hot, axis=1))


def expert_step(arrived, saved_gate, saved_up, w_gate, w_up, w_down):
    hidden_grad = jnp.einsum("efd,esd->efs", w_down, arrived, preferred_element_type=jnp.float32)
    gate_value = saved_gate.astype(jnp.float32)
    up_value = saved_up.astype(jnp.float32)
    sigmoid_gate = jax.nn.sigmoid(gate_value)
    up_grad = (hidden_grad * gate_value * sigmoid_gate).astype(jnp.bfloat16)
    gate_grad = (
        hidden_grad * up_value * sigmoid_gate * (1.0 + gate_value * (1.0 - sigmoid_gate))
    ).astype(jnp.bfloat16)
    partial_value = jnp.einsum(
        "efs,efd->esd", gate_grad, w_gate, preferred_element_type=jnp.float32
    )
    partial_value = partial_value + jnp.einsum(
        "efs,efd->esd", up_grad, w_up, preferred_element_type=jnp.float32
    )
    return partial_value.astype(jnp.bfloat16)


def slots_body(cotangent, gates, expert_ids, saved_gate, saved_up, w_gate, w_up, w_down):
    owners = lax.axis_size("expert")
    row_count, feature_dim = cotangent.shape
    top_count = expert_ids.shape[1]
    local_count, _, slot_count = saved_gate.shape
    capacity = slot_count // owners
    flat_ids, slot_pos = route_slots(expert_ids, local_count * owners)
    target = flat_ids % local_count * slot_count + flat_ids // local_count * capacity + slot_pos
    scaled = (gates[:, :, None] * cotangent.astype(jnp.float32)[:, None, :]).astype(jnp.bfloat16)
    scaled = scaled.reshape(row_count * top_count, feature_dim)
    outgoing = (
        jnp.zeros((local_count * slot_count, feature_dim), jnp.bfloat16).at[target].set(scaled)
    )
    outgoing = outgoing.reshape(local_count, slot_count, feature_dim)
    arrived = lax.all_to_all(outgoing, "expert", split_axis=1, concat_axis=1, tiled=True)
    partial_value = expert_step(arrived, saved_gate, saved_up, w_gate, w_up, w_down)
    returned = lax.all_to_all(partial_value, "expert", split_axis=1, concat_axis=1, tiled=True)
    picked = returned.reshape(local_count * slot_count, feature_dim)[target].astype(jnp.float32)
    combined = jnp.sum(picked.reshape(row_count, top_count, feature_dim), axis=1)
    return lax.psum_scatter(combined, "tp", scatter_dimension=0, tiled=True)


CHUNKS = ((0, 2), (1, 3))
TILE = 512


def swap(value, axis, step):
    count = lax.axis_size(axis)
    return lax.ppermute(value, axis, [(i, i ^ step) for i in range(count)])


def along_line(value, shift):
    count = lax.axis_size("expert")
    return lax.ppermute(value, "expert", [(i, (i + 4 * shift) % count) for i in range(count)])


def small(kernel, name, outs, kinds, operands, scratch=(), limit=8, work=0):
    spaces = {"s": pltpu.SMEM, "v": pltpu.VMEM, "h": pltpu.HBM, "o": pl.ANY}
    return pl.pallas_call(
        kernel,
        out_shape=[
            out if hasattr(out, "dtype") else jax.ShapeDtypeStruct(out, jnp.bfloat16) for out in outs
        ],
        in_specs=[pl.BlockSpec(memory_space=spaces[kind]) for kind in kinds],
        scratch_shapes=list(scratch),
        compiler_params=pltpu.CompilerParams(vmem_limit_bytes=limit << 20),
        cost_estimate=pl.CostEstimate(flops=work, bytes_accessed=work >> 8, transcendentals=0),
        name=name,
    )(*operands)


def take_kernel(place, tokens, part):
    near = pl.multiple_of(place[3] * part.shape[0], part.shape[0])
    part[...] = tokens[pl.ds(near, part.shape[0]), :]


def take(place, cotangent, piece):
    return small(take_kernel, "take", [(piece, cotangent.shape[1])], "sv", (place, cotangent), limit=2)[0]


def table_kernel(gates, ids, table):
    count = gates.shape[0]
    rest = gates[...]
    for i in range(3):
        term = rest.astype(jnp.bfloat16).astype(jnp.float32)
        table[i * count:(i + 1) * count] = term.astype(jnp.bfloat16)
        rest = rest - term
    table[3 * count:] = ids[...].astype(jnp.float32).astype(jnp.bfloat16)


def routing_table(gates, ids):
    count, tokens = gates.shape
    return small(table_kernel, "table", [(4 * count, tokens)], "vv", (gates, ids), limit=2)[0]


def stack_kernel(*refs):
    lines = refs[-1]
    for r in range(lines.shape[0]):
        lines[r] = refs[r][...]


def stack(pieces, *after):
    return small(
        stack_kernel,
        "stack",
        [(len(pieces),) + pieces[0].shape],
        "v" * len(pieces) + "o" * len(after),
        (*pieces, *after),
    )[0]


def relay_kernel(came, part, _, __, line, following):
    line[0] = came[...]
    following[...] = part[...]


def relay(came, part, *after):
    return small(
        relay_kernel, "relay", [(1,) + came.shape, part.shape], "vvoo", (came, part, *after)
    )


def turn_kernel(gate, up, _, __, gate_t, up_t):
    tile = 128
    for source, target in ((gate, gate_t), (up, up_t)):
        for e in range(source.shape[0]):
            for at in range(0, source.shape[2], tile):
                target[e, at:at + tile] = source[e, :, at:at + tile].astype(jnp.float32).T.astype(
                    jnp.bfloat16
                )


def turn(saved_gate, saved_up, *after):
    count, units, slots = saved_gate.shape
    return small(
        turn_kernel,
        "turn",
        [(count, slots, units)] * 2,
        "vvoo",
        (saved_gate, saved_up, *after),
        limit=12,
    )


def corner_kernel(place, tokens, first, over, side, whole_over, left, right):
    _, piece, middle = left.shape
    far = pl.multiple_of((1 - place[3]) * piece, piece)
    right[0] = tokens[pl.ds(far, piece), middle:]
    whole_over[0] = first[...]
    whole_over[1:] = over[...]
    left[0] = first[:, :middle]
    left[1:] = over[:, :, :middle]
    right[1:] = side[:, :, middle:2 * middle]


def own_corner(place, cotangent, first, over, side):
    count, piece, width = over.shape
    middle = cotangent.shape[1] // 2
    return small(
        corner_kernel,
        "own_corner",
        [(count + 1, piece, width)] + [(count + 1, piece, middle)] * 2,
        "svvvv",
        (place, cotangent, first, over, side),
    )


def plain_corner_kernel(over, side, _, left, right):
    middle = left.shape[-1]
    left[...] = over[:, :, :middle]
    right[...] = side[:, :, middle:2 * middle]


def corner(over, side, middle, after):
    return small(
        plain_corner_kernel,
        "corner",
        [over.shape[:2] + (middle,)] * 2,
        "vvo",
        (over, side, after),
    )


def join_kernel(left, right, *refs):
    result = refs[-1]
    middle = left.shape[-1]
    result[:, :, :middle] = left[...]
    result[:, :, middle:] = right[...]


def join(left, right, *after, work=0):
    dims = left.shape
    return small(
        join_kernel,
        "join",
        [dims[:-1] + (2 * dims[-1],)],
        "vv" + "o" * len(after),
        (left, right, *after),
        work=work,
    )[0]


def tokens_of(own, lines, r, offsets):
    if r == 0:
        return own[...]
    return lines[r_place(r, offsets)]


def r_place(r, offsets):
    return [offset for offset in offsets if offset != 0].index(r)


def pair_base(place, line_count, r, ry, width):
    line = lax.rem(place[2] + r, line_count)
    row = place[1] if ry == 0 else 1 - place[1]
    return pl.multiple_of((line * 2 + row) * width, width)


def route_kernel(offsets, capacity, place, table, table_c, pick, pick_t, gate, hits, gates):
    tokens = pick.shape[2] // 2
    core, row, line, half = place[0], place[1], place[2], place[3]
    first = (line * 4 + row * 2 + core) * 2
    for i, r in enumerate(offsets):
        for ry in range(2):
            tables = [table[ry, r].astype(jnp.float32), table_c[ry, r].astype(jnp.float32)]
            swapped = core > 0
            ordered = [
                jnp.where(swapped, tables[1], tables[0]), jnp.where(swapped, tables[0], tables[1])
            ]
            for c in range(2):
                block = ordered[c]
                value = block[0:8] + block[8:16] + block[16:24]
                for e in range(2):
                    named = block[24:32] == (first + e).astype(jnp.float32)
                    at = ((i * 2 + ry) * 2 + c) * 2 + e
                    hits[at:at + 1] = jnp.sum(named.astype(jnp.float32), axis=0, keepdims=True)
                    gates[at:at + 1] = jnp.sum(
                        jnp.where(named, value, 0.0), axis=0, keepdims=True
                    )
    earlier = lax.broadcasted_iota(jnp.int32, (tokens, tokens), 0) < lax.broadcasted_iota(
        jnp.int32, (tokens, tokens), 1
    )
    hit = hits[...]
    slot = jnp.dot(
        hit.astype(jnp.bfloat16),
        earlier.astype(jnp.float32).astype(jnp.bfloat16),
        preferred_element_type=jnp.float32,
    )
    slot = jnp.where(hit > 0.5, slot, -1.0)
    turned = half > 0
    slot = jnp.where(turned, pltpu.roll(slot, tokens // 2, 1), slot)
    weight = jnp.where(turned, pltpu.roll(gates[...], tokens // 2, 1), gates[...])
    order = lax.broadcasted_iota(jnp.int32, (capacity, tokens), 0).astype(jnp.float32)
    for p in range(pick.shape[0]):
        rows = []
        for e in range(2):
            for c in range(2):
                at = (p * 2 + c) * 2 + e
                ones = (order == slot[at:at + 1]).astype(jnp.float32)
                column = jnp.sum(ones * weight[at:at + 1], axis=1, keepdims=True)
                place_in = (e * 2 + c) * capacity
                gate[p, place_in:place_in + capacity] = jnp.broadcast_to(
                    column, (capacity, gate.shape[2])
                )
                own_core = (core == c).astype(jnp.float32)
                rows.append(jnp.concatenate([ones * own_core, ones * (1.0 - own_core)], axis=1))
        matrix = jnp.concatenate(rows, axis=0)
        pick[p] = matrix.astype(jnp.bfloat16)
        count = matrix.shape[0]
        square = jnp.concatenate(
            [matrix, jnp.zeros((2 * tokens - count, 2 * tokens), jnp.float32)], axis=0
        )
        pick_t[p] = square.T[:, :count].astype(jnp.bfloat16)


def route(offsets, place, table, table_c, capacity):
    tokens = table.shape[3]
    pairs = 2 * len(offsets)
    rows = 4 * capacity
    return small(
        functools.partial(route_kernel, offsets, capacity),
        "route",
        [
            (pairs, rows, 2 * tokens),
            (pairs, 2 * tokens, rows),
            jax.ShapeDtypeStruct((pairs, rows, 128), jnp.float32),
        ],
        "svv",
        (place, table, table_c),
        [pltpu.VMEM((4 * pairs, tokens), jnp.float32)] * 2,
    )


def hidden_kernel(offsets, line_count, place, own, own_c, lines, lines_c, side, side_c, over, over_c,
                  diag, diag_c, pick, gate, w_down, saved_gate, saved_up, _, grads, slots):
    piece = over.shape[1]
    width = diag.shape[2]
    rows = pick.shape[1] // 2
    units = w_down.shape[1]
    near = pl.multiple_of(place[3] * piece, piece)
    far = pl.multiple_of((1 - place[3]) * piece, piece)

    @pl.loop(0, width // TILE)
    def _(k):
        at = pl.ds(pl.multiple_of(k * TILE, TILE), TILE)
        for i, r in enumerate(offsets):
            for ry in range(2):
                parts = []
                for c in range(2):
                    if ry == 1:
                        parts += [(over, over_c)[c][i, :, at], (diag, diag_c)[c][i, :, at]]
                    elif r == 0:
                        group = (own, own_c)[c]
                        parts += [group[pl.ds(near, piece), at], group[pl.ds(far, piece), at]]
                    else:
                        j = r_place(r, offsets)
                        parts += [(lines, lines_c)[c][j, :, at], (side, side_c)[c][j, :, at]]
                p = i * 2 + ry
                picked = jnp.dot(
                    pick[p], jnp.concatenate(parts, axis=0), preferred_element_type=jnp.float32
                )
                weight = gate[p]
                weight = jnp.concatenate([weight] * (TILE // weight.shape[1]), axis=1)
                scaled = (picked * weight).astype(jnp.bfloat16)
                slots[0, p * rows:(p + 1) * rows, at] = scaled[:rows]
                slots[1, p * rows:(p + 1) * rows, at] = scaled[rows:]

    for e in range(2):
        total = lax.dot_general(
            slots[e], w_down[e], (((1,), (1,)), ((), ())), preferred_element_type=jnp.float32
        )
        for i, r in enumerate(offsets):
            for ry in range(2):
                p = i * 2 + ry
                mine = slice(p * rows, (p + 1) * rows)
                saved = pl.ds(pair_base(place, line_count, r, ry, rows), rows)
                hidden_grad = total[mine]
                gate_value = saved_gate[e, saved, :].astype(jnp.float32)
                up_value = saved_up[e, saved, :].astype(jnp.float32)
                sigmoid_gate = jax.nn.sigmoid(gate_value)
                grads[e, mine, units:] = (hidden_grad * gate_value * sigmoid_gate).astype(
                    jnp.bfloat16
                )
                grads[e, mine, :units] = (
                    hidden_grad * up_value * sigmoid_gate * (1.0 + gate_value * (1.0 - sigmoid_gate))
                ).astype(jnp.bfloat16)


def hidden(offsets, line_count, place, own, own_c, moved, pick, gate, w_down, saved, after):
    width = own.shape[1]
    units = w_down.shape[1]
    count = pick.shape[0] * pick.shape[1] // 2
    return small(
        functools.partial(hidden_kernel, offsets, line_count),
        "hidden",
        [(2, count, 2 * units)],
        "s" + "v" * 15 + "o",
        (place, own, own_c, *moved, pick, gate, w_down, *saved, after),
        [pltpu.VMEM((2, count, width), jnp.bfloat16)],
        limit=12,
    )[0]


def sums_kernel(offset, grads, w_gate, w_up, pick_t, _, keep, send, slots):
    rows = pick_t.shape[2] // 2
    tokens = pick_t.shape[1] // 2

    @pl.loop(0, keep.shape[2] // TILE)
    def _(k):
        at = pl.ds(pl.multiple_of(k * TILE, TILE), TILE)
        source = pl.ds(pl.multiple_of(offset + k * TILE, TILE), TILE)
        for e in range(2):
            weights = jnp.concatenate([w_gate[e, :, source], w_up[e, :, source]], axis=0)
            slots[e] = jnp.dot(grads[e], weights, preferred_element_type=jnp.float32).astype(
                jnp.bfloat16
            )
        for p in range(pick_t.shape[0]):
            mine = slice(p * rows, (p + 1) * rows)
            both = jnp.concatenate([slots[0, mine], slots[1, mine]], axis=0)
            total = jnp.dot(pick_t[p], both, preferred_element_type=jnp.float32).astype(
                jnp.bfloat16
            )
            keep[p, :, at] = total[:tokens]
            send[p, :, at] = total[tokens:]


def sums(offset, width, grads, w_gate, w_up, pick_t, after, work=0):
    pairs, tokens, _ = pick_t.shape
    _, count, units = grads.shape
    return small(
        functools.partial(sums_kernel, offset),
        "sums",
        [(pairs, tokens // 2, width)] * 2,
        "vvvvo",
        (grads, w_gate, w_up, pick_t, after),
        [pltpu.VMEM((2, count, TILE), jnp.bfloat16)],
        limit=8,
        work=work,
    )


def first_left_kernel(keep, came, _, send, kept):
    piece = kept.shape[1]
    kept[...] = keep[:, :piece] + came[:, :piece]
    send[...] = keep[:, piece:] + came[:, piece:]


def first_left(keep, came, after):
    pairs, tokens, width = keep.shape
    return small(
        first_left_kernel,
        "first_left",
        [(pairs, tokens // 2, width)] * 2,
        "vvo",
        (keep, came, after),
    )


def first_right_kernel(keep, came, _, send, kept):
    for i in range(kept.shape[0]):
        kept[i] = keep[2 * i] + came[2 * i]
        send[i] = keep[2 * i + 1] + came[2 * i + 1]


def first_right(keep, came, after):
    pairs, tokens, width = keep.shape
    return small(
        first_right_kernel,
        "first_right",
        [(pairs // 2, tokens, width)] * 2,
        "vvo",
        (keep, came, after),
    )


def second_kernel(keep_l, came_l, keep_r, came_r, _, send_l, left, send_r, right):
    piece = left.shape[1]
    for i in range(left.shape[0]):
        left[i] = keep_l[2 * i] + came_l[2 * i]
        send_l[i] = keep_l[2 * i + 1] + came_l[2 * i + 1]
        right[i] = keep_r[i, :piece] + came_r[i, :piece]
        send_r[i] = keep_r[i, piece:] + came_r[i, piece:]


def second_sum(keep_l, came_l, keep_r, came_r, after):
    lines = keep_r.shape[0]
    _, piece, middle = keep_l.shape
    return small(
        second_kernel,
        "second_sum",
        [(lines, piece, middle)] * 4,
        "vvvvo",
        (keep_l, came_l, keep_r, came_r, after),
        work=1 << 36,
    )


def third_kernel(left, came_l, right, came_r, _, *outs):
    middle = left.shape[-1]
    for columns, one, other in ((slice(0, middle), left, came_l), (slice(middle, None), right, came_r)):
        for i, out in enumerate(outs):
            out[:, columns] = (one[i].astype(jnp.float32) + other[i].astype(jnp.float32)).astype(
                out.dtype
            )


def third_sum(offsets, left, came_l, right, came_r, after):
    _, piece, middle = left.shape
    return small(
        third_kernel,
        "third_sum",
        [
            jax.ShapeDtypeStruct((piece, 2 * middle), jnp.float32 if r == 0 else jnp.bfloat16)
            for r in offsets
        ],
        "vvvvo",
        (left, came_l, right, came_r, after),
        work=2,
    )


def last_kernel(*refs):
    total = refs[0][...]
    for ref in refs[1:-1]:
        total = total + ref[...].astype(jnp.float32)
    refs[-1][...] = total


def tokens_body(cotangent, gates, expert_ids, saved_gate, saved_up, w_gate, w_up, w_down):
    owners = lax.axis_size("expert")
    row_count, feature_dim = cotangent.shape
    capacity = saved_gate.shape[2] // owners
    lines = owners // 4
    piece = row_count // 2
    middle = feature_dim // 2
    me, half = lax.axis_index("expert"), lax.axis_index("tp")
    place = jnp.stack([me % 2, me // 2 % 2, me // 4, half]).astype(jnp.int32)

    part = take(place, cotangent, piece)
    first = swap(part, "expert", 2)
    own_c = swap(cotangent, "expert", 1)
    table = routing_table(gates.T, expert_ids.T)
    table = stack([table] + [along_line(table, -r) for r in range(1, lines)])
    table = stack([table, swap(table, "expert", 2)])
    table_c = swap(table, "expert", 1)
    routes = [route(offsets, place, table, table_c, capacity) for offsets in CHUNKS]
    gathered = []

    def compute(index, after):
        pick, pick_t, gate = routes[index]
        return hidden(
            CHUNKS[index], lines, place, cotangent, own_c, gathered[index], pick, gate, w_down, saved, after
        )

    def both_cores(arrays):
        return [each for array in arrays for each in (array, swap(array, "expert", 1))]

    def sums_by_token(offset, grads, pick_t, after, work=0):
        keep, send = sums(offset, middle, grads, w_gate, w_up, pick_t, after, work)
        return [keep, swap(send, "expert", 1)], send

    def step_left(keep, came, after):
        send, keep = first_left(keep, came, after)
        return keep, swap(send, "tp", 1), send

    def step_right(keep, came, after):
        send, keep = first_right(keep, came, after)
        return keep, swap(send, "expert", 2), send

    def second_step(offsets, sums_of_two, after, came):
        send_l, left, send_r, right = second_sum(*sums_of_two, after)
        came_l, came_r = swap(send_l, "expert", 2), swap(send_r, "tp", 1)
        rows = third_sum(offsets, left, came_l, right, came_r, send_l if came is None else came)
        return rows[0], [row if r == 0 else along_line(row, r) for r, row in zip(offsets, rows)], send_l

    (_, near), (third, second) = CHUNKS
    line, part = relay(along_line(part, -near), part, table_c, first)
    side, over = swap(line, "tp", 1), swap(line, "expert", 2)
    came = [along_line(part, -third), along_line(part, -second)]
    saved = turn(saved_gate, saved_up, routes[0][0], routes[1][0])
    over, left, right = own_corner(place, cotangent, first, over, side)
    left, right = swap(left, "tp", 1), swap(right, "expert", 2)
    later = stack(came, saved[0])
    gathered.append(both_cores([line, side, over, join(left, right, later)]))

    line, side, over = later, swap(later, "tp", 1), swap(later, "expert", 2)
    grads = compute(0, line)
    early_l, after = sums_by_token(0, grads, routes[0][1], grads)
    left, right = corner(over, side, middle, after)
    early_r, after = sums_by_token(middle, grads, routes[0][1], left, 68719476736)
    left, right = swap(left, "tp", 1), swap(right, "expert", 2)
    gathered.append(both_cores([line, side, over, join(left, right, after, work=8589934592)]))

    early_l = step_left(*early_l, gathered[1][6])
    early_r = step_right(*early_r, early_l[-1])
    grads = compute(1, early_r[-1])
    late_l, after = sums_by_token(0, grads, routes[1][1], grads)
    late_r, after = sums_by_token(middle, grads, routes[1][1], after)
    done, early, after = second_step(CHUNKS[0], early_l[:2] + early_r[:2], early_r[-1], None)
    late_l = step_left(*late_l, after)
    late_r = step_right(*late_r, late_l[-1])
    _, late, _ = second_step(CHUNKS[1], late_l[:2] + late_r[:2], done, early[-1])
    terms = early + late
    return pl.pallas_call(
        last_kernel,
        out_shape=jax.ShapeDtypeStruct((piece, feature_dim), jnp.float32),
        compiler_params=pltpu.CompilerParams(vmem_limit_bytes=8 << 20),
        name="last_sum",
    )(*terms)


def body(*arrays):
    cotangent, gates, _, saved_gate = arrays[:4]
    owners = lax.axis_size("expert")
    fits = (
        owners == 16
        and lax.axis_size("tp") == 2
        and cotangent.shape[0] == 128
        and cotangent.shape[1] % (2 * TILE) == 0
        and gates.shape[1] == 8
        and saved_gate.shape[0] == 2
        and saved_gate.shape[2] // owners % 16 == 0
        and 4 * saved_gate.shape[2] // owners <= 256
    )
    return (tokens_body if fits else slots_body)(*arrays)


def solution(mesh):
    in_specs = (
        P("expert", None),
        P("expert", None),
        P("expert", None),
        P("expert", "tp", None),
        P("expert", "tp", None),
        P("expert", "tp", None),
        P("expert", "tp", None),
        P("expert", "tp", None),
    )
    out_specs = P(("expert", "tp"), None)
    return jax.shard_map(body, mesh=mesh, in_specs=in_specs, out_specs=out_specs, check_vma=False)
```

```python
import functools

import jax
import jax.numpy as jnp
from jax import lax
from jax.experimental import pallas as pl
from jax.experimental.pallas import tpu as pltpu
from jax.sharding import PartitionSpec as P


def route_slots(expert_ids, expert_total):
    flat_ids = expert_ids.reshape(-1)
    one_hot = (flat_ids[:, None] == jnp.arange(expert_total, dtype=jnp.int32)[None, :]).astype(
        jnp.int32
    )
    before = jnp.cumsum(one_hot, axis=0) - one_hot
    return (flat_ids, jnp.sum(before * one_hot, axis=1))


def expert_step(arrived, saved_gate, saved_up, w_gate, w_up, w_down):
    hidden_grad = jnp.einsum("efd,esd->efs", w_down, arrived, preferred_element_type=jnp.float32)
    gate_value = saved_gate.astype(jnp.float32)
    up_value = saved_up.astype(jnp.float32)
    sigmoid_gate = jax.nn.sigmoid(gate_value)
    up_grad = (hidden_grad * gate_value * sigmoid_gate).astype(jnp.bfloat16)
    gate_grad = (
        hidden_grad * up_value * sigmoid_gate * (1.0 + gate_value * (1.0 - sigmoid_gate))
    ).astype(jnp.bfloat16)
    partial_value = jnp.einsum(
        "efs,efd->esd", gate_grad, w_gate, preferred_element_type=jnp.float32
    )
    partial_value = partial_value + jnp.einsum(
        "efs,efd->esd", up_grad, w_up, preferred_element_type=jnp.float32
    )
    return partial_value.astype(jnp.bfloat16)


def slots_body(cotangent, gates, expert_ids, saved_gate, saved_up, w_gate, w_up, w_down):
    owners = lax.axis_size("expert")
    row_count, feature_dim = cotangent.shape
    top_count = expert_ids.shape[1]
    local_count, _, slot_count = saved_gate.shape
    capacity = slot_count // owners
    flat_ids, slot_pos = route_slots(expert_ids, local_count * owners)
    target = flat_ids % local_count * slot_count + flat_ids // local_count * capacity + slot_pos
    scaled = (gates[:, :, None] * cotangent.astype(jnp.float32)[:, None, :]).astype(jnp.bfloat16)
    scaled = scaled.reshape(row_count * top_count, feature_dim)
    outgoing = (
        jnp.zeros((local_count * slot_count, feature_dim), jnp.bfloat16).at[target].set(scaled)
    )
    outgoing = outgoing.reshape(local_count, slot_count, feature_dim)
    arrived = lax.all_to_all(outgoing, "expert", split_axis=1, concat_axis=1, tiled=True)
    partial_value = expert_step(arrived, saved_gate, saved_up, w_gate, w_up, w_down)
    returned = lax.all_to_all(partial_value, "expert", split_axis=1, concat_axis=1, tiled=True)
    picked = returned.reshape(local_count * slot_count, feature_dim)[target].astype(jnp.float32)
    combined = jnp.sum(picked.reshape(row_count, top_count, feature_dim), axis=1)
    return lax.psum_scatter(combined, "tp", scatter_dimension=0, tiled=True)


CHUNKS = ((0, 2), (1, 3))
TILE = 512


def swap(value, axis, step):
    count = lax.axis_size(axis)
    return lax.ppermute(value, axis, [(i, i ^ step) for i in range(count)])


def along_line(value, shift):
    count = lax.axis_size("expert")
    return lax.ppermute(value, "expert", [(i, (i + 4 * shift) % count) for i in range(count)])


def small(kernel, name, outs, kinds, operands, scratch=(), limit=8, work=0):
    spaces = {"s": pltpu.SMEM, "v": pltpu.VMEM, "h": pltpu.HBM, "o": pl.ANY}
    return pl.pallas_call(
        kernel,
        out_shape=[
            out if hasattr(out, "dtype") else jax.ShapeDtypeStruct(out, jnp.bfloat16) for out in outs
        ],
        in_specs=[pl.BlockSpec(memory_space=spaces[kind]) for kind in kinds],
        scratch_shapes=list(scratch),
        compiler_params=pltpu.CompilerParams(vmem_limit_bytes=limit << 20),
        cost_estimate=pl.CostEstimate(flops=work, bytes_accessed=work >> 8, transcendentals=0),
        name=name,
    )(*operands)


def prepare_kernel(place, tokens, gates_any, ids_any, first, table, gates, ids, sems):
    piece = first.shape[0]
    width = first.shape[1] - table.shape[1]
    near = pl.multiple_of(place[3] * piece, piece)
    copies = [
        pltpu.make_async_copy(gates_any, gates, sems.at[0]),
        pltpu.make_async_copy(ids_any, ids, sems.at[1]),
        pltpu.make_async_copy(
            tokens.at[pl.ds(near, piece), :], first.at[:, pl.ds(0, width)], sems.at[2]
        ),
    ]
    for copy in copies:
        copy.start()
    copies[0].wait()
    copies[1].wait()
    rest = gates[...]
    terms = []
    for _ in range(3):
        term = rest.astype(jnp.bfloat16).astype(jnp.float32)
        terms.append(term)
        rest = rest - term
    terms.append(ids[...].astype(jnp.float32))
    unused = piece - 4 * gates.shape[0]
    terms.append(jnp.zeros((unused, gates.shape[1]), jnp.float32))
    packed = jnp.concatenate(terms, axis=0).astype(jnp.bfloat16)
    first[:, width:] = packed
    table[...] = packed
    copies[2].wait()


def prepare(place, cotangent, gates, ids, piece):
    return small(
        prepare_kernel,
        "prepare",
        [(piece, cotangent.shape[1] + 128), (piece, 128)],
        "shhh",
        (place, cotangent, gates, ids),
        [
            pltpu.VMEM(gates.shape, jnp.float32),
            pltpu.VMEM(ids.shape, jnp.int32),
            pltpu.SemaphoreType.DMA((3,)),
        ],
        limit=4,
    )


def stack_kernel(*refs):
    lines = refs[-1]
    for r in range(lines.shape[0]):
        lines[r] = refs[r][...]


def stack(pieces, *after, work=0):
    return small(
        stack_kernel,
        "stack",
        [(len(pieces),) + pieces[0].shape],
        "v" * len(pieces) + "o" * len(after),
        (*pieces, *after),
        work=work,
    )[0]


def relay_kernel(came, part, line, following):
    line[0] = came[...]
    following[...] = part[...]


def relay(came, part):
    return small(
        relay_kernel, "relay", [(1,) + came.shape, part.shape], "vv", (came, part)
    )


def turn_kernel(gate, up, _, gate_t, up_t):
    tile = 128
    for source, target in ((gate, gate_t), (up, up_t)):
        for e in range(source.shape[0]):
            for at in range(0, source.shape[2], tile):
                target[e, at:at + tile] = source[e, :, at:at + tile].astype(jnp.float32).T.astype(
                    jnp.bfloat16
                )


def turn(saved_gate, saved_up, after):
    count, units, slots = saved_gate.shape
    return small(
        turn_kernel,
        "turn",
        [(count, slots, units)] * 2,
        "vvo",
        (saved_gate, saved_up, after),
        limit=12,
    )


def corner_kernel(place, tokens, first, over, side, whole_over, left, right, sem):
    _, piece, middle = left.shape
    far = pl.multiple_of((1 - place[3]) * piece, piece)
    copy = pltpu.make_async_copy(
        tokens.at[pl.ds(far, piece), pl.ds(middle, middle)], right.at[0], sem.at[0]
    )
    copy.start()
    whole_over[0] = first[...]
    whole_over[1:] = over[...]
    left[0] = first[:, :middle]
    left[1:] = over[:, :, :middle]
    right[1:] = side[:, :, middle:2 * middle]
    copy.wait()


def own_corner(place, cotangent, first, over, side):
    count, piece, width = over.shape
    middle = cotangent.shape[1] // 2
    return small(
        corner_kernel,
        "own_corner",
        [(count + 1, piece, width)] + [(count + 1, piece, middle)] * 2,
        "shvvv",
        (place, cotangent, first, over, side),
        (pltpu.SemaphoreType.DMA((1,)),),
    )


def plain_corner_kernel(over, side, _, left, right):
    middle = left.shape[-1]
    left[...] = over[:, :, :middle]
    right[...] = side[:, :, middle:2 * middle]


def corner(over, side, middle, after, work=0):
    return small(
        plain_corner_kernel,
        "corner",
        [over.shape[:2] + (middle,)] * 2,
        "vvo",
        (over, side, after),
        work=work,
    )


def join_kernel(left, right, *refs):
    result = refs[-1]
    middle = left.shape[-1]
    result[:, :, :middle] = left[...]
    result[:, :, middle:] = right[...]


def join(left, right, *after, work=0):
    dims = left.shape
    return small(
        join_kernel,
        "join",
        [dims[:-1] + (2 * dims[-1],)],
        "vv" + "o" * len(after),
        (left, right, *after),
        work=work,
    )[0]


def tokens_of(own, lines, r, offsets):
    if r == 0:
        return own[...]
    return lines[r_place(r, offsets)]


def r_place(r, offsets):
    return [offset for offset in offsets if offset != 0].index(r)


def pair_base(place, line_count, r, ry, width):
    line = lax.rem(place[2] + r, line_count)
    row = place[1] if ry == 0 else 1 - place[1]
    return pl.multiple_of((line * 2 + row) * width, width)


def route_kernel(offsets, capacity, place, own, own_c, lines, lines_c, over, over_c, pick, pick_t, gate,
                 hits, gates):
    tokens = pick.shape[2] // 2
    width = over.shape[2] - 128
    core, row, line, half = place[0], place[1], place[2], place[3]
    first = (line * 4 + row * 2 + core) * 2
    for i, r in enumerate(offsets):
        for ry in range(2):
            tables = []
            for c in range(2):
                if ry == 1:
                    table = (over, over_c)[c][i, :32, width:]
                elif r == 0:
                    table = (own, own_c)[c][:32]
                else:
                    table = (lines, lines_c)[c][r_place(r, offsets), :32, width:]
                tables.append(table.astype(jnp.float32))
            swapped = core > 0
            ordered = [
                jnp.where(swapped, tables[1], tables[0]), jnp.where(swapped, tables[0], tables[1])
            ]
            for c in range(2):
                block = ordered[c]
                value = block[0:8] + block[8:16] + block[16:24]
                for e in range(2):
                    named = block[24:32] == (first + e).astype(jnp.float32)
                    at = ((i * 2 + ry) * 2 + c) * 2 + e
                    hits[at:at + 1] = jnp.sum(named.astype(jnp.float32), axis=0, keepdims=True)
                    gates[at:at + 1] = jnp.sum(
                        jnp.where(named, value, 0.0), axis=0, keepdims=True
                    )
    earlier = lax.broadcasted_iota(jnp.int32, (tokens, tokens), 0) < lax.broadcasted_iota(
        jnp.int32, (tokens, tokens), 1
    )
    hit = hits[...]
    slot = jnp.dot(
        hit.astype(jnp.bfloat16),
        earlier.astype(jnp.float32).astype(jnp.bfloat16),
        preferred_element_type=jnp.float32,
    )
    slot = jnp.where(hit > 0.5, slot, -1.0)
    turned = half > 0
    slot = jnp.where(turned, pltpu.roll(slot, tokens // 2, 1), slot)
    weight = jnp.where(turned, pltpu.roll(gates[...], tokens // 2, 1), gates[...])
    order = lax.broadcasted_iota(jnp.int32, (capacity, tokens), 0).astype(jnp.float32)
    for p in range(pick.shape[0]):
        rows = []
        for e in range(2):
            for c in range(2):
                at = (p * 2 + c) * 2 + e
                ones = (order == slot[at:at + 1]).astype(jnp.float32)
                column = jnp.sum(ones * weight[at:at + 1], axis=1, keepdims=True)
                place_in = (e * 2 + c) * capacity
                gate[p, place_in:place_in + capacity] = jnp.broadcast_to(
                    column, (capacity, gate.shape[2])
                )
                own_core = (core == c).astype(jnp.float32)
                rows.append(jnp.concatenate([ones * own_core, ones * (1.0 - own_core)], axis=1))
        matrix = jnp.concatenate(rows, axis=0)
        pick[p] = matrix.astype(jnp.bfloat16)
        count = matrix.shape[0]
        square = jnp.concatenate(
            [matrix, jnp.zeros((2 * tokens - count, 2 * tokens), jnp.float32)], axis=0
        )
        pick_t[p] = square.T[:, :count].astype(jnp.bfloat16)


def route(offsets, place, table, table_c, lines, lines_c, over, over_c, capacity):
    tokens = 2 * over.shape[1]
    pairs = 2 * len(offsets)
    rows = 4 * capacity
    return small(
        functools.partial(route_kernel, offsets, capacity),
        "route",
        [
            (pairs, rows, 2 * tokens),
            (pairs, 2 * tokens, rows),
            jax.ShapeDtypeStruct((pairs, rows, 128), jnp.float32),
        ],
        "s" + "v" * 6,
        (place, table, table_c, lines, lines_c, over, over_c),
        [pltpu.VMEM((4 * pairs, tokens), jnp.float32)] * 2,
    )


def hidden_kernel(offsets, line_count, place, own, own_c, lines, lines_c, side, side_c, over, over_c,
                  diag, diag_c, pick, gate, w_down, saved_gate, saved_up, _, grads, slots):
    piece = over.shape[1]
    width = diag.shape[2]
    rows = pick.shape[1] // 2
    units = w_down.shape[1]
    near = pl.multiple_of(place[3] * piece, piece)
    far = pl.multiple_of((1 - place[3]) * piece, piece)

    @pl.loop(0, width // TILE)
    def _(k):
        at = pl.ds(pl.multiple_of(k * TILE, TILE), TILE)
        for i, r in enumerate(offsets):
            for ry in range(2):
                parts = []
                for c in range(2):
                    if ry == 1:
                        parts += [(over, over_c)[c][i, :, at], (diag, diag_c)[c][i, :, at]]
                    elif r == 0:
                        group = (own, own_c)[c]
                        parts += [group[pl.ds(near, piece), at], group[pl.ds(far, piece), at]]
                    else:
                        j = r_place(r, offsets)
                        parts += [(lines, lines_c)[c][j, :, at], (side, side_c)[c][j, :, at]]
                p = i * 2 + ry
                picked = jnp.dot(
                    pick[p], jnp.concatenate(parts, axis=0), preferred_element_type=jnp.float32
                )
                weight = gate[p]
                weight = jnp.concatenate([weight] * (TILE // weight.shape[1]), axis=1)
                scaled = (picked * weight).astype(jnp.bfloat16)
                slots[0, p * rows:(p + 1) * rows, at] = scaled[:rows]
                slots[1, p * rows:(p + 1) * rows, at] = scaled[rows:]

    for e in range(2):
        total = lax.dot_general(
            slots[e], w_down[e], (((1,), (1,)), ((), ())), preferred_element_type=jnp.float32
        )
        for i, r in enumerate(offsets):
            for ry in range(2):
                p = i * 2 + ry
                mine = slice(p * rows, (p + 1) * rows)
                saved = pl.ds(pair_base(place, line_count, r, ry, rows), rows)
                hidden_grad = total[mine]
                gate_value = saved_gate[e, saved, :].astype(jnp.float32)
                up_value = saved_up[e, saved, :].astype(jnp.float32)
                sigmoid_gate = jax.nn.sigmoid(gate_value)
                grads[e, mine, units:] = (hidden_grad * gate_value * sigmoid_gate).astype(
                    jnp.bfloat16
                )
                grads[e, mine, :units] = (
                    hidden_grad * up_value * sigmoid_gate * (1.0 + gate_value * (1.0 - sigmoid_gate))
                ).astype(jnp.bfloat16)


def hidden(offsets, line_count, place, own, own_c, moved, pick, gate, w_down, saved, after):
    width = own.shape[1]
    units = w_down.shape[1]
    count = pick.shape[0] * pick.shape[1] // 2
    return small(
        functools.partial(hidden_kernel, offsets, line_count),
        "hidden",
        [(2, count, 2 * units)],
        "s" + "v" * 15 + "o",
        (place, own, own_c, *moved, pick, gate, w_down, *saved, after),
        [pltpu.VMEM((2, count, width), jnp.bfloat16)],
        limit=12,
    )[0]


def sums_kernel(offset, grads, w_gate, w_up, pick_t, _, keep, send, slots):
    rows = pick_t.shape[2] // 2
    tokens = pick_t.shape[1] // 2

    @pl.loop(0, keep.shape[2] // TILE)
    def _(k):
        at = pl.ds(pl.multiple_of(k * TILE, TILE), TILE)
        source = pl.ds(pl.multiple_of(offset + k * TILE, TILE), TILE)
        for e in range(2):
            weights = jnp.concatenate([w_gate[e, :, source], w_up[e, :, source]], axis=0)
            slots[e] = jnp.dot(grads[e], weights, preferred_element_type=jnp.float32).astype(
                jnp.bfloat16
            )
        for p in range(pick_t.shape[0]):
            mine = slice(p * rows, (p + 1) * rows)
            both = jnp.concatenate([slots[0, mine], slots[1, mine]], axis=0)
            total = jnp.dot(pick_t[p], both, preferred_element_type=jnp.float32).astype(
                jnp.bfloat16
            )
            keep[p, :, at] = total[:tokens]
            send[p, :, at] = total[tokens:]


def sums(offset, width, grads, w_gate, w_up, pick_t, after, work=0):
    pairs, tokens, _ = pick_t.shape
    _, count, units = grads.shape
    return small(
        functools.partial(sums_kernel, offset),
        "sums",
        [(pairs, tokens // 2, width)] * 2,
        "vvvvo",
        (grads, w_gate, w_up, pick_t, after),
        [pltpu.VMEM((2, count, TILE), jnp.bfloat16)],
        limit=8,
        work=work,
    )


def first_left_kernel(keep, came, _, send, kept):
    piece = kept.shape[1]
    kept[...] = keep[:, :piece] + came[:, :piece]
    send[...] = keep[:, piece:] + came[:, piece:]


def first_left(keep, came, after):
    pairs, tokens, width = keep.shape
    return small(
        first_left_kernel,
        "first_left",
        [(pairs, tokens // 2, width)] * 2,
        "vvo",
        (keep, came, after),
    )


def first_right_kernel(keep, came, _, send, kept):
    for i in range(kept.shape[0]):
        kept[i] = keep[2 * i] + came[2 * i]
        send[i] = keep[2 * i + 1] + came[2 * i + 1]


def first_right(keep, came, after):
    pairs, tokens, width = keep.shape
    return small(
        first_right_kernel,
        "first_right",
        [(pairs // 2, tokens, width)] * 2,
        "vvo",
        (keep, came, after),
    )


def second_kernel(keep_l, came_l, keep_r, came_r, _, send_l, left, send_r, right):
    piece = left.shape[1]
    for i in range(left.shape[0]):
        left[i] = keep_l[2 * i] + came_l[2 * i]
        send_l[i] = keep_l[2 * i + 1] + came_l[2 * i + 1]
        right[i] = keep_r[i, :piece] + came_r[i, :piece]
        send_r[i] = keep_r[i, piece:] + came_r[i, piece:]


def second_sum(keep_l, came_l, keep_r, came_r, after):
    lines = keep_r.shape[0]
    _, piece, middle = keep_l.shape
    return small(
        second_kernel,
        "second_sum",
        [(lines, piece, middle)] * 4,
        "vvvvo",
        (keep_l, came_l, keep_r, came_r, after),
        work=1 << 36,
    )


def third_kernel(left, came_l, right, came_r, _, *outs):
    middle = left.shape[-1]
    for columns, one, other in ((slice(0, middle), left, came_l), (slice(middle, None), right, came_r)):
        for i, out in enumerate(outs):
            out[:, columns] = (one[i].astype(jnp.float32) + other[i].astype(jnp.float32)).astype(
                out.dtype
            )


def third_sum(offsets, left, came_l, right, came_r, after):
    _, piece, middle = left.shape
    return small(
        third_kernel,
        "third_sum",
        [
            jax.ShapeDtypeStruct((piece, 2 * middle), jnp.float32 if r == 0 else jnp.bfloat16)
            for r in offsets
        ],
        "vvvvo",
        (left, came_l, right, came_r, after),
        work=1 << 36,
    )


def last_kernel(*refs):
    total = refs[0][...]
    for ref in refs[1:-1]:
        total = total + ref[...].astype(jnp.float32)
    refs[-1][...] = total


def tokens_body(cotangent, gates, expert_ids, saved_gate, saved_up, w_gate, w_up, w_down):
    owners = lax.axis_size("expert")
    row_count, feature_dim = cotangent.shape
    capacity = saved_gate.shape[2] // owners
    lines = owners // 4
    piece = row_count // 2
    middle = feature_dim // 2
    me, half = lax.axis_index("expert"), lax.axis_index("tp")
    place = jnp.stack([me % 2, me // 2 % 2, me // 4, half]).astype(jnp.int32)

    part, table = prepare(place, cotangent, gates.T, expert_ids.T, piece)
    first = swap(part, "expert", 2)
    own_c, table_c = swap(cotangent, "expert", 1), swap(table, "expert", 1)
    gathered = []

    def compute(index, after):
        offsets, moved = CHUNKS[index], gathered[index]
        line, line_c, _, _, over, over_c = moved[:6]
        pick, pick_t, gate = route(
            offsets, place, table, table_c, line, line_c, over, over_c, capacity
        )
        grads = hidden(
            offsets, lines, place, cotangent, own_c, moved, pick, gate, w_down, saved, after
        )
        return grads, pick_t

    def sums_by_token(offset, grads, pick_t, after, work=0):
        keep, send = sums(offset, middle, grads, w_gate, w_up, pick_t, after, work)
        return [keep, swap(send, "expert", 1)], send

    def both_cores(arrays):
        return [each for array in arrays for each in (array, swap(array, "expert", 1))]

    def step_left(keep, came, after):
        send, keep = first_left(keep, came, after)
        return keep, swap(send, "tp", 1), send

    def step_right(keep, came, after):
        send, keep = first_right(keep, came, after)
        return keep, swap(send, "expert", 2), send

    (_, near), (third, second) = CHUNKS
    line, part = relay(along_line(part, -near), part)
    side, over = swap(line, "tp", 1), swap(line, "expert", 2)
    came = [along_line(part, -third), along_line(part, -second)]
    saved = turn(saved_gate, saved_up, line)
    over, left, right = own_corner(place, cotangent, first, over, side)
    left, right = swap(left, "tp", 1), swap(right, "expert", 2)
    moved = both_cores([line, side, over])
    line = stack(came, saved[0], work=68719476736)
    line = stack([line], *moved[1::2], own_c, table_c)[0]
    gathered.append(moved + both_cores([join(left, right, line)]))

    side, over = swap(line, "tp", 1), swap(line, "expert", 2)
    grads, pick_t = compute(0, line)
    early_l, after = sums_by_token(0, grads, pick_t, grads)
    early_r, after = sums_by_token(middle, grads, pick_t, after)
    left, right = corner(over, side, middle, after, work=68719476736)
    after = left
    left, right = swap(left, "tp", 1), swap(right, "expert", 2)
    early_l = step_left(*early_l, after)
    early_r = step_right(*early_r, early_l[-1])
    moved = both_cores([line, side, over])
    other = [swap(left, "expert", 1), swap(right, "expert", 1)]
    moved += [join(left, right, early_r[-1], work=0), join(*other, early_r[-1])]
    gathered.append(moved)

    def second_step(offsets, sums_of_two, after, came):
        send_l, left, send_r, right = second_sum(*sums_of_two, after)
        came_l, came_r = swap(send_l, "expert", 2), swap(send_r, "tp", 1)
        rows = third_sum(offsets, left, came_l, right, came_r, send_l if came is None else came)
        return rows[0], [row if r == 0 else along_line(row, r) for r, row in zip(offsets, rows)], send_l

    grads, pick_t = compute(1, early_r[-1])
    late_l, after = sums_by_token(0, grads, pick_t, grads)
    late_r, _ = sums_by_token(middle, grads, pick_t, after)
    done, early, after = second_step(CHUNKS[0], early_l[:2] + early_r[:2], early_r[-1], None)
    late_l = step_left(*late_l, after)
    late_r = step_right(*late_r, late_l[-1])
    _, late, _ = second_step(CHUNKS[1], late_l[:2] + late_r[:2], done, early[-1])
    terms = early + late
    return pl.pallas_call(
        last_kernel,
        out_shape=jax.ShapeDtypeStruct((piece, feature_dim), jnp.float32),
        compiler_params=pltpu.CompilerParams(vmem_limit_bytes=8 << 20),
        name="last_sum",
    )(*terms)


def body(*arrays):
    cotangent, gates, _, saved_gate = arrays[:4]
    owners = lax.axis_size("expert")
    fits = (
        owners == 16
        and lax.axis_size("tp") == 2
        and cotangent.shape[0] == 128
        and cotangent.shape[1] % (2 * TILE) == 0
        and gates.shape[1] == 8
        and saved_gate.shape[0] == 2
        and saved_gate.shape[2] // owners % 16 == 0
        and 4 * saved_gate.shape[2] // owners <= 256
    )
    return (tokens_body if fits else slots_body)(*arrays)


def solution(mesh):
    in_specs = (
        P("expert", None),
        P("expert", None),
        P("expert", None),
        P("expert", "tp", None),
        P("expert", "tp", None),
        P("expert", "tp", None),
        P("expert", "tp", None),
        P("expert", "tp", None),
    )
    out_specs = P(("expert", "tp"), None)
    return jax.shard_map(body, mesh=mesh, in_specs=in_specs, out_specs=out_specs, check_vma=False)
```

```python
import functools

import jax
import jax.numpy as jnp
from jax import lax
from jax.experimental import pallas as pl
from jax.experimental.pallas import tpu as pltpu
from jax.sharding import PartitionSpec as P


def route_slots(expert_ids, expert_total):
    flat_ids = expert_ids.reshape(-1)
    one_hot = (flat_ids[:, None] == jnp.arange(expert_total, dtype=jnp.int32)[None, :]).astype(
        jnp.int32
    )
    before = jnp.cumsum(one_hot, axis=0) - one_hot
    return (flat_ids, jnp.sum(before * one_hot, axis=1))


def expert_step(arrived, saved_gate, saved_up, w_gate, w_up, w_down):
    hidden_grad = jnp.einsum("efd,esd->efs", w_down, arrived, preferred_element_type=jnp.float32)
    gate_value = saved_gate.astype(jnp.float32)
    up_value = saved_up.astype(jnp.float32)
    sigmoid_gate = jax.nn.sigmoid(gate_value)
    up_grad = (hidden_grad * gate_value * sigmoid_gate).astype(jnp.bfloat16)
    gate_grad = (
        hidden_grad * up_value * sigmoid_gate * (1.0 + gate_value * (1.0 - sigmoid_gate))
    ).astype(jnp.bfloat16)
    partial_value = jnp.einsum(
        "efs,efd->esd", gate_grad, w_gate, preferred_element_type=jnp.float32
    )
    partial_value = partial_value + jnp.einsum(
        "efs,efd->esd", up_grad, w_up, preferred_element_type=jnp.float32
    )
    return partial_value.astype(jnp.bfloat16)


def slots_body(cotangent, gates, expert_ids, saved_gate, saved_up, w_gate, w_up, w_down):
    owners = lax.axis_size("expert")
    row_count, feature_dim = cotangent.shape
    top_count = expert_ids.shape[1]
    local_count, _, slot_count = saved_gate.shape
    capacity = slot_count // owners
    flat_ids, slot_pos = route_slots(expert_ids, local_count * owners)
    target = flat_ids % local_count * slot_count + flat_ids // local_count * capacity + slot_pos
    scaled = (gates[:, :, None] * cotangent.astype(jnp.float32)[:, None, :]).astype(jnp.bfloat16)
    scaled = scaled.reshape(row_count * top_count, feature_dim)
    outgoing = (
        jnp.zeros((local_count * slot_count, feature_dim), jnp.bfloat16).at[target].set(scaled)
    )
    outgoing = outgoing.reshape(local_count, slot_count, feature_dim)
    arrived = lax.all_to_all(outgoing, "expert", split_axis=1, concat_axis=1, tiled=True)
    partial_value = expert_step(arrived, saved_gate, saved_up, w_gate, w_up, w_down)
    returned = lax.all_to_all(partial_value, "expert", split_axis=1, concat_axis=1, tiled=True)
    picked = returned.reshape(local_count * slot_count, feature_dim)[target].astype(jnp.float32)
    combined = jnp.sum(picked.reshape(row_count, top_count, feature_dim), axis=1)
    return lax.psum_scatter(combined, "tp", scatter_dimension=0, tiled=True)


CHUNKS = ((0, 2), (1, 3))
TILE = 512


def swap(value, axis, step):
    count = lax.axis_size(axis)
    return lax.ppermute(value, axis, [(i, i ^ step) for i in range(count)])


def along_line(value, shift):
    count = lax.axis_size("expert")
    return lax.ppermute(value, "expert", [(i, (i + 4 * shift) % count) for i in range(count)])


def small(kernel, name, outs, kinds, operands, scratch=(), limit=8, work=0):
    spaces = {"s": pltpu.SMEM, "v": pltpu.VMEM, "h": pltpu.HBM, "o": pl.ANY}
    return pl.pallas_call(
        kernel,
        out_shape=[
            out if hasattr(out, "dtype") else jax.ShapeDtypeStruct(out, jnp.bfloat16) for out in outs
        ],
        in_specs=[pl.BlockSpec(memory_space=spaces[kind]) for kind in kinds],
        scratch_shapes=list(scratch),
        compiler_params=pltpu.CompilerParams(vmem_limit_bytes=limit << 20),
        cost_estimate=pl.CostEstimate(flops=work, bytes_accessed=work >> 8, transcendentals=0),
        name=name,
    )(*operands)


def prepare_kernel(place, tokens, gates, ids, near, far, sems):
    piece, width = far.shape
    at = pl.multiple_of(place[3] * piece, piece)
    other = pl.multiple_of((1 - place[3]) * piece, piece)
    copies = [
        pltpu.make_async_copy(tokens.at[pl.ds(at, piece), :], near.at[:, pl.ds(0, width)], sems.at[0]),
        pltpu.make_async_copy(tokens.at[pl.ds(other, piece), :], far, sems.at[1]),
    ]
    for copy in copies:
        copy.start()
    rest = gates[...]
    terms = []
    for _ in range(3):
        term = rest.astype(jnp.bfloat16).astype(jnp.float32)
        terms.append(term)
        rest = rest - term
    terms.append(ids[...].astype(jnp.float32))
    unused = piece - 4 * gates.shape[0]
    terms.append(jnp.zeros((unused, gates.shape[1]), jnp.float32))
    near[:, width:] = jnp.concatenate(terms, axis=0).astype(jnp.bfloat16)
    for copy in copies:
        copy.wait()


def prepare(place, cotangent, gates, ids, piece):
    width = cotangent.shape[1]
    return small(
        prepare_kernel,
        "prepare",
        [(piece, width + 128), (piece, width)],
        "shvv",
        (place, cotangent, gates, ids),
        [pltpu.SemaphoreType.DMA((2,))],
        limit=4,
    )


def stack_kernel(*refs):
    lines = refs[-1]
    for r in range(lines.shape[0]):
        lines[r] = refs[r][...]


def stack(pieces, *after, work=0):
    return small(
        stack_kernel,
        "stack",
        [(len(pieces),) + pieces[0].shape],
        "v" * len(pieces) + "o" * len(after),
        (*pieces, *after),
        work=work,
    )[0]


def relay_kernel(came, part, _, __, ___, line, following):
    line[0] = came[...]
    following[...] = part[...]


def relay(came, part, *after):
    return small(
        relay_kernel, "relay", [(1,) + came.shape, part.shape], "vvooo", (came, part, *after)
    )


def turn_kernel(gate, up, *refs):
    gate_t, up_t = refs[-2:]
    tile = 128
    for source, target in ((gate, gate_t), (up, up_t)):
        for e in range(source.shape[0]):
            for at in range(0, source.shape[2], tile):
                target[e, at:at + tile] = source[e, :, at:at + tile].astype(jnp.float32).T.astype(
                    jnp.bfloat16
                )


def turn(saved_gate, saved_up, *after):
    count, units, slots = saved_gate.shape
    return small(
        turn_kernel,
        "turn",
        [(count, slots, units)] * 2,
        "vv" + "o" * len(after),
        (saved_gate, saved_up, *after),
        limit=12,
    )


def corner_kernel(far, first, over, side, whole_over, left, right):
    middle = left.shape[2]
    whole_over[0] = first[...]
    whole_over[1:] = over[...]
    left[0] = first[:, :middle]
    left[1:] = over[:, :, :middle]
    right[0] = far[:, middle:]
    right[1:] = side[:, :, middle:2 * middle]


def own_corner(far, first, over, side):
    count, piece, width = over.shape
    middle = far.shape[1] // 2
    return small(
        corner_kernel,
        "own_corner",
        [(count + 1, piece, width)] + [(count + 1, piece, middle)] * 2,
        "vvvv",
        (far, first, over, side),
    )


def plain_corner_kernel(over, side, _, left, right):
    middle = left.shape[-1]
    left[...] = over[:, :, :middle]
    right[...] = side[:, :, middle:2 * middle]


def corner(over, side, middle, after, work=0):
    return small(
        plain_corner_kernel,
        "corner",
        [over.shape[:2] + (middle,)] * 2,
        "vvo",
        (over, side, after),
        work=work,
    )


def join_kernel(left, right, *refs):
    result = refs[-1]
    middle = left.shape[-1]
    result[:, :, :middle] = left[...]
    result[:, :, middle:] = right[...]


def join(left, right, *after, work=0):
    dims = left.shape
    return small(
        join_kernel,
        "join",
        [dims[:-1] + (2 * dims[-1],)],
        "vv" + "o" * len(after),
        (left, right, *after),
        work=work,
    )[0]


def tokens_of(own, lines, r, offsets):
    if r == 0:
        return own[...]
    return lines[r_place(r, offsets)]


def r_place(r, offsets):
    return [offset for offset in offsets if offset != 0].index(r)


def pair_base(place, line_count, r, ry, width):
    line = lax.rem(place[2] + r, line_count)
    row = place[1] if ry == 0 else 1 - place[1]
    return pl.multiple_of((line * 2 + row) * width, width)


def route_kernel(offsets, capacity, place, own, own_c, lines, lines_c, over, over_c, pick, pick_t, gate,
                 hits, gates):
    tokens = pick.shape[2] // 2
    width = over.shape[2] - 128
    core, row, line, half = place[0], place[1], place[2], place[3]
    first = (line * 4 + row * 2 + core) * 2
    for i, r in enumerate(offsets):
        for ry in range(2):
            tables = []
            for c in range(2):
                if ry == 1:
                    table = (over, over_c)[c][i, :32, width:]
                elif r == 0:
                    table = (own, own_c)[c][:32, width:]
                else:
                    table = (lines, lines_c)[c][r_place(r, offsets), :32, width:]
                tables.append(table.astype(jnp.float32))
            swapped = core > 0
            ordered = [
                jnp.where(swapped, tables[1], tables[0]), jnp.where(swapped, tables[0], tables[1])
            ]
            for c in range(2):
                block = ordered[c]
                value = block[0:8] + block[8:16] + block[16:24]
                for e in range(2):
                    named = block[24:32] == (first + e).astype(jnp.float32)
                    at = ((i * 2 + ry) * 2 + c) * 2 + e
                    hits[at:at + 1] = jnp.sum(named.astype(jnp.float32), axis=0, keepdims=True)
                    gates[at:at + 1] = jnp.sum(
                        jnp.where(named, value, 0.0), axis=0, keepdims=True
                    )
    earlier = lax.broadcasted_iota(jnp.int32, (tokens, tokens), 0) < lax.broadcasted_iota(
        jnp.int32, (tokens, tokens), 1
    )
    hit = hits[...]
    slot = jnp.dot(
        hit.astype(jnp.bfloat16),
        earlier.astype(jnp.float32).astype(jnp.bfloat16),
        preferred_element_type=jnp.float32,
    )
    slot = jnp.where(hit > 0.5, slot, -1.0)
    turned = half > 0
    slot = jnp.where(turned, pltpu.roll(slot, tokens // 2, 1), slot)
    weight = jnp.where(turned, pltpu.roll(gates[...], tokens // 2, 1), gates[...])
    order = lax.broadcasted_iota(jnp.int32, (capacity, tokens), 0).astype(jnp.float32)
    for p in range(pick.shape[0]):
        rows = []
        for e in range(2):
            for c in range(2):
                at = (p * 2 + c) * 2 + e
                ones = (order == slot[at:at + 1]).astype(jnp.float32)
                column = jnp.sum(ones * weight[at:at + 1], axis=1, keepdims=True)
                place_in = (e * 2 + c) * capacity
                gate[p, place_in:place_in + capacity] = jnp.broadcast_to(
                    column, (capacity, gate.shape[2])
                )
                own_core = (core == c).astype(jnp.float32)
                rows.append(jnp.concatenate([ones * own_core, ones * (1.0 - own_core)], axis=1))
        matrix = jnp.concatenate(rows, axis=0)
        pick[p] = matrix.astype(jnp.bfloat16)
        count = matrix.shape[0]
        square = jnp.concatenate(
            [matrix, jnp.zeros((2 * tokens - count, 2 * tokens), jnp.float32)], axis=0
        )
        pick_t[p] = square.T[:, :count].astype(jnp.bfloat16)


def route(offsets, place, table, table_c, lines, lines_c, over, over_c, capacity):
    tokens = 2 * over.shape[1]
    pairs = 2 * len(offsets)
    rows = 4 * capacity
    return small(
        functools.partial(route_kernel, offsets, capacity),
        "route",
        [
            (pairs, rows, 2 * tokens),
            (pairs, 2 * tokens, rows),
            jax.ShapeDtypeStruct((pairs, rows, 128), jnp.float32),
        ],
        "s" + "v" * 6,
        (place, table, table_c, lines, lines_c, over, over_c),
        [pltpu.VMEM((4 * pairs, tokens), jnp.float32)] * 2,
    )


def hidden_kernel(offsets, rows_of, line_count, place, *refs):
    *sources, pick, gate, w_down, saved_gate, saved_up, _, grads, slots = refs
    sources = [sources[at:at + 2] for at in range(0, len(sources), 2)]
    near, far = (sources.pop(0), sources.pop(0)) if offsets[0] == 0 and 0 in rows_of else (None, None)
    lines, side = (sources.pop(0), sources.pop(0)) if 0 in rows_of else (None, None)
    over, diag = (sources.pop(0), sources.pop(0)) if 1 in rows_of else (None, None)
    width = w_down.shape[2]
    rows = pick.shape[1] // 2
    units = w_down.shape[1]
    pairs = [(i, r, ry) for i, r in enumerate(offsets) for ry in rows_of]

    @pl.loop(0, width // TILE)
    def _(k):
        at = pl.ds(pl.multiple_of(k * TILE, TILE), TILE)
        for q, (i, r, ry) in enumerate(pairs):
            parts = []
            for c in range(2):
                if ry == 1:
                    parts += [over[c][i, :, at], diag[c][i, :, at]]
                elif r == 0:
                    parts += [near[c][:, at], far[c][:, at]]
                else:
                    j = r_place(r, offsets)
                    parts += [lines[c][j, :, at], side[c][j, :, at]]
            p = i * 2 + ry
            picked = jnp.dot(
                pick[p], jnp.concatenate(parts, axis=0), preferred_element_type=jnp.float32
            )
            weight = gate[p]
            weight = jnp.concatenate([weight] * (TILE // weight.shape[1]), axis=1)
            scaled = (picked * weight).astype(jnp.bfloat16)
            slots[0, q * rows:(q + 1) * rows, at] = scaled[:rows]
            slots[1, q * rows:(q + 1) * rows, at] = scaled[rows:]

    for e in range(2):
        total = lax.dot_general(
            slots[e], w_down[e], (((1,), (1,)), ((), ())), preferred_element_type=jnp.float32
        )
        for q, (i, r, ry) in enumerate(pairs):
            mine = slice(q * rows, (q + 1) * rows)
            saved = pl.ds(pair_base(place, line_count, r, ry, rows), rows)
            hidden_grad = total[mine]
            gate_value = saved_gate[e, saved, :].astype(jnp.float32)
            up_value = saved_up[e, saved, :].astype(jnp.float32)
            sigmoid_gate = jax.nn.sigmoid(gate_value)
            grads[e, mine, units:] = (hidden_grad * gate_value * sigmoid_gate).astype(jnp.bfloat16)
            grads[e, mine, :units] = (
                hidden_grad * up_value * sigmoid_gate * (1.0 + gate_value * (1.0 - sigmoid_gate))
            ).astype(jnp.bfloat16)


def hidden(offsets, rows_of, line_count, place, sources, pick, gate, w_down, saved, after):
    _, units, width = w_down.shape
    count = len(offsets) * len(rows_of) * pick.shape[1] // 2
    return small(
        functools.partial(hidden_kernel, offsets, rows_of, line_count),
        "hidden",
        [(2, count, 2 * units)],
        "s" + "v" * (len(sources) + 5) + "o",
        (place, *sources, pick, gate, w_down, *saved, after),
        [pltpu.VMEM((2, count, width), jnp.bfloat16)],
        limit=12,
    )[0]


def sums_kernel(offset, pairs, grads, w_gate, w_up, pick_t, _, keep, send, slots):
    rows = pick_t.shape[2] // 2
    tokens = pick_t.shape[1] // 2

    @pl.loop(0, keep.shape[2] // TILE)
    def _(k):
        at = pl.ds(pl.multiple_of(k * TILE, TILE), TILE)
        source = pl.ds(pl.multiple_of(offset + k * TILE, TILE), TILE)
        for e in range(2):
            weights = jnp.concatenate([w_gate[e, :, source], w_up[e, :, source]], axis=0)
            slots[e] = jnp.dot(grads[e], weights, preferred_element_type=jnp.float32).astype(
                jnp.bfloat16
            )
        for q, p in enumerate(pairs):
            mine = slice(q * rows, (q + 1) * rows)
            both = jnp.concatenate([slots[0, mine], slots[1, mine]], axis=0)
            total = jnp.dot(pick_t[p], both, preferred_element_type=jnp.float32).astype(
                jnp.bfloat16
            )
            keep[q, :, at] = total[:tokens]
            send[q, :, at] = total[tokens:]


def sums(offset, width, pairs, grads, w_gate, w_up, pick_t, after, work=0):
    tokens = pick_t.shape[1]
    count = grads.shape[1]
    return small(
        functools.partial(sums_kernel, offset, pairs),
        "sums",
        [(len(pairs), tokens // 2, width)] * 2,
        "vvvvo",
        (grads, w_gate, w_up, pick_t, after),
        [pltpu.VMEM((2, count, TILE), jnp.bfloat16)],
        limit=8,
        work=work,
    )


def first_left_kernel(keep, came, _, send, kept):
    piece = kept.shape[1]
    kept[...] = keep[:, :piece] + came[:, :piece]
    send[...] = keep[:, piece:] + came[:, piece:]


def first_left(keep, came, after):
    pairs, tokens, width = keep.shape
    return small(
        first_left_kernel,
        "first_left",
        [(pairs, tokens // 2, width)] * 2,
        "vvo",
        (keep, came, after),
    )


def apart_right_kernel(keep_a, came_a, keep_b, came_b, _, send, kept):
    middle = kept.shape[2]
    kept[...] = keep_a[:, :, middle:] + came_a[:, :, middle:]
    send[...] = keep_b[...] + came_b[...]


def apart_left_kernel(keep_a, came_a, keep_b, came_b, _, send, kept):
    _, piece, middle = kept.shape
    for i in range(keep_a.shape[0]):
        kept[2 * i] = keep_a[i, :piece, :middle] + came_a[i, :piece, :middle]
        send[2 * i] = keep_a[i, piece:, :middle] + came_a[i, piece:, :middle]
        kept[2 * i + 1] = keep_b[i, :piece] + came_b[i, :piece]
        send[2 * i + 1] = keep_b[i, piece:] + came_b[i, piece:]


def first_apart(kernel, dims, row_a, row_b, after):
    return small(kernel, "first_apart", [dims] * 2, "vvvvo", (*row_a, *row_b, after))


def first_right_kernel(keep, came, _, send, kept):
    for i in range(kept.shape[0]):
        kept[i] = keep[2 * i] + came[2 * i]
        send[i] = keep[2 * i + 1] + came[2 * i + 1]


def first_right(keep, came, after):
    pairs, tokens, width = keep.shape
    return small(
        first_right_kernel,
        "first_right",
        [(pairs // 2, tokens, width)] * 2,
        "vvo",
        (keep, came, after),
    )


def second_kernel(keep_l, came_l, keep_r, came_r, _, send_l, left, send_r, right):
    piece = left.shape[1]
    for i in range(left.shape[0]):
        left[i] = keep_l[2 * i] + came_l[2 * i]
        send_l[i] = keep_l[2 * i + 1] + came_l[2 * i + 1]
        right[i] = keep_r[i, :piece] + came_r[i, :piece]
        send_r[i] = keep_r[i, piece:] + came_r[i, piece:]


def second_sum(keep_l, came_l, keep_r, came_r, after):
    lines = keep_r.shape[0]
    _, piece, middle = keep_l.shape
    return small(
        second_kernel,
        "second_sum",
        [(lines, piece, middle)] * 4,
        "vvvvo",
        (keep_l, came_l, keep_r, came_r, after),
        work=1 << 36,
    )


def third_kernel(left, came_l, right, came_r, _, *outs):
    middle = left.shape[-1]
    for columns, one, other in ((slice(0, middle), left, came_l), (slice(middle, None), right, came_r)):
        for i, out in enumerate(outs):
            out[:, columns] = (one[i].astype(jnp.float32) + other[i].astype(jnp.float32)).astype(
                out.dtype
            )


def third_sum(offsets, left, came_l, right, came_r, after):
    _, piece, middle = left.shape
    return small(
        third_kernel,
        "third_sum",
        [
            jax.ShapeDtypeStruct((piece, 2 * middle), jnp.float32 if r == 0 else jnp.bfloat16)
            for r in offsets
        ],
        "vvvvo",
        (left, came_l, right, came_r, after),
        work=1 << 36,
    )


def last_kernel(*refs):
    total = refs[0][...]
    for ref in refs[1:-1]:
        total = total + ref[...].astype(jnp.float32)
    refs[-1][...] = total


def tokens_body(cotangent, gates, expert_ids, saved_gate, saved_up, w_gate, w_up, w_down):
    owners = lax.axis_size("expert")
    row_count, feature_dim = cotangent.shape
    capacity = saved_gate.shape[2] // owners
    lines = owners // 4
    piece = row_count // 2
    middle = feature_dim // 2
    me, half = lax.axis_index("expert"), lax.axis_index("tp")
    place = jnp.stack([me % 2, me // 2 % 2, me // 4, half]).astype(jnp.int32)

    part, far = prepare(place, cotangent, gates.T, expert_ids.T, piece)
    first = swap(part, "expert", 2)
    near_c, far_c = swap(part, "expert", 1), swap(far, "expert", 1)
    own = [part, near_c, far, far_c]

    def routed(offsets, moved):
        line, line_c, _, _, over, over_c = moved[:6]
        return route(offsets, place, own[0], near_c, line, line_c, over, over_c, capacity)

    def sums_by_token(offset, width, pairs, grads, pick_t, after):
        keep, send = sums(offset, width, pairs, grads, w_gate, w_up, pick_t, after)
        return [keep, swap(send, "expert", 1)], send

    def both_cores(arrays):
        return [each for array in arrays for each in (array, swap(array, "expert", 1))]

    def step_left(keep, came, after):
        send, keep = first_left(keep, came, after)
        return keep, swap(send, "tp", 1), send

    def step_right(keep, came, after):
        send, keep = first_right(keep, came, after)
        return keep, swap(send, "expert", 2), send

    (_, near), (third, second) = CHUNKS
    line, part = relay(along_line(part, -near), part, first, near_c, far_c)
    side, over = swap(line, "tp", 1), swap(line, "expert", 2)
    came = [along_line(part, -third), along_line(part, -second)]
    line_c = swap(line, "expert", 1)
    saved = turn(saved_gate, saved_up, line)
    over, left, right = own_corner(far, first, over, side)
    left, right = swap(left, "tp", 1), swap(right, "expert", 2)
    moved = [line, line_c] + both_cores([side, over])
    line = stack(came, saved[0], work=68719476736)
    line = stack([line], moved[5])[0]
    moved += both_cores([join(left, right, line)])
    pick, pick_t, gate = routed(CHUNKS[0], moved)

    side, over = swap(line, "tp", 1), swap(line, "expert", 2)
    grads = hidden(CHUNKS[0], (0, 1), lines, place, own + moved, pick, gate, w_down, saved, line)
    early_l, after = sums_by_token(0, middle, (0, 1, 2, 3), grads, pick_t, grads)
    early_r, after = sums_by_token(middle, middle, (0, 1, 2, 3), grads, pick_t, after)
    left, right = corner(over, side, middle, after, work=68719476736)
    after = left
    left, right = swap(left, "tp", 1), swap(right, "expert", 2)
    moved = both_cores([line, side, over])
    pick, pick_t, gate = routed(CHUNKS[1], moved)
    grads = hidden(CHUNKS[1], (0,), lines, place, moved[:4], pick, gate, w_down, saved, after)
    row_a, after = sums_by_token(0, 2 * middle, (0, 2), grads, pick_t, grads)
    diag = join(left, right, after, work=0)
    early_l = step_left(*early_l, diag)
    early_r = step_right(*early_r, early_l[-1])
    diags = both_cores([diag])
    grads = hidden(
        CHUNKS[1], (1,), lines, place, moved[4:] + diags, pick, gate, w_down, saved, early_r[-1]
    )
    row_br, after = sums_by_token(middle, middle, (1, 3), grads, pick_t, grads)
    row_bl, after = sums_by_token(0, middle, (1, 3), grads, pick_t, after)

    def second_step(offsets, sums_of_two, after, came):
        send_l, left, send_r, right = second_sum(*sums_of_two, after)
        came_l, came_r = swap(send_l, "expert", 2), swap(send_r, "tp", 1)
        rows = third_sum(offsets, left, came_l, right, came_r, send_l if came is None else came)
        return rows[0], [row if r == 0 else along_line(row, r) for r, row in zip(offsets, rows)], send_l

    done, early, after = second_step(CHUNKS[0], early_l[:2] + early_r[:2], early_r[-1], None)
    send, keep_r = first_apart(apart_right_kernel, (2, 2 * piece, middle), row_a, row_br, after)
    came_r = swap(send, "expert", 2)
    send, keep_l = first_apart(apart_left_kernel, (4, piece, middle), row_a, row_bl, send)
    came_l = swap(send, "tp", 1)
    _, late, _ = second_step(CHUNKS[1], (keep_l, came_l, keep_r, came_r), done, early[-1])
    terms = early + late
    return pl.pallas_call(
        last_kernel,
        out_shape=jax.ShapeDtypeStruct((piece, feature_dim), jnp.float32),
        compiler_params=pltpu.CompilerParams(vmem_limit_bytes=8 << 20),
        name="last_sum",
    )(*terms)


def body(*arrays):
    cotangent, gates, _, saved_gate = arrays[:4]
    owners = lax.axis_size("expert")
    fits = (
        owners == 16
        and lax.axis_size("tp") == 2
        and cotangent.shape[0] == 128
        and cotangent.shape[1] % (2 * TILE) == 0
        and gates.shape[1] == 8
        and saved_gate.shape[0] == 2
        and saved_gate.shape[2] // owners % 16 == 0
        and 4 * saved_gate.shape[2] // owners <= 256
    )
    return (tokens_body if fits else slots_body)(*arrays)


def solution(mesh):
    in_specs = (
        P("expert", None),
        P("expert", None),
        P("expert", None),
        P("expert", "tp", None),
        P("expert", "tp", None),
        P("expert", "tp", None),
        P("expert", "tp", None),
        P("expert", "tp", None),
    )
    out_specs = P(("expert", "tp"), None)
    return jax.shard_map(body, mesh=mesh, in_specs=in_specs, out_specs=out_specs, check_vma=False)
```

```python
import functools

import jax
import jax.numpy as jnp
from jax import lax
from jax.experimental import pallas as pl
from jax.experimental.pallas import tpu as pltpu
from jax.sharding import PartitionSpec as P


def route_slots(expert_ids, expert_total):
    flat_ids = expert_ids.reshape(-1)
    one_hot = (flat_ids[:, None] == jnp.arange(expert_total, dtype=jnp.int32)[None, :]).astype(
        jnp.int32
    )
    before = jnp.cumsum(one_hot, axis=0) - one_hot
    return (flat_ids, jnp.sum(before * one_hot, axis=1))


def expert_step(arrived, saved_gate, saved_up, w_gate, w_up, w_down):
    hidden_grad = jnp.einsum("efd,esd->efs", w_down, arrived, preferred_element_type=jnp.float32)
    gate_value = saved_gate.astype(jnp.float32)
    up_value = saved_up.astype(jnp.float32)
    sigmoid_gate = jax.nn.sigmoid(gate_value)
    up_grad = (hidden_grad * gate_value * sigmoid_gate).astype(jnp.bfloat16)
    gate_grad = (
        hidden_grad * up_value * sigmoid_gate * (1.0 + gate_value * (1.0 - sigmoid_gate))
    ).astype(jnp.bfloat16)
    partial_value = jnp.einsum(
        "efs,efd->esd", gate_grad, w_gate, preferred_element_type=jnp.float32
    )
    partial_value = partial_value + jnp.einsum(
        "efs,efd->esd", up_grad, w_up, preferred_element_type=jnp.float32
    )
    return partial_value.astype(jnp.bfloat16)


def slots_body(cotangent, gates, expert_ids, saved_gate, saved_up, w_gate, w_up, w_down):
    owners = lax.axis_size("expert")
    row_count, feature_dim = cotangent.shape
    top_count = expert_ids.shape[1]
    local_count, _, slot_count = saved_gate.shape
    capacity = slot_count // owners
    flat_ids, slot_pos = route_slots(expert_ids, local_count * owners)
    target = flat_ids % local_count * slot_count + flat_ids // local_count * capacity + slot_pos
    scaled = (gates[:, :, None] * cotangent.astype(jnp.float32)[:, None, :]).astype(jnp.bfloat16)
    scaled = scaled.reshape(row_count * top_count, feature_dim)
    outgoing = (
        jnp.zeros((local_count * slot_count, feature_dim), jnp.bfloat16).at[target].set(scaled)
    )
    outgoing = outgoing.reshape(local_count, slot_count, feature_dim)
    arrived = lax.all_to_all(outgoing, "expert", split_axis=1, concat_axis=1, tiled=True)
    partial_value = expert_step(arrived, saved_gate, saved_up, w_gate, w_up, w_down)
    returned = lax.all_to_all(partial_value, "expert", split_axis=1, concat_axis=1, tiled=True)
    picked = returned.reshape(local_count * slot_count, feature_dim)[target].astype(jnp.float32)
    combined = jnp.sum(picked.reshape(row_count, top_count, feature_dim), axis=1)
    return lax.psum_scatter(combined, "tp", scatter_dimension=0, tiled=True)


CHUNKS = ((0, 2), (1, 3))
TILE = 512


def swap(value, axis, step):
    count = lax.axis_size(axis)
    return lax.ppermute(value, axis, [(i, i ^ step) for i in range(count)])


def along_line(value, shift):
    count = lax.axis_size("expert")
    return lax.ppermute(value, "expert", [(i, (i + 4 * shift) % count) for i in range(count)])


def small(kernel, name, outs, kinds, operands, scratch=(), limit=8, work=0):
    spaces = {"s": pltpu.SMEM, "v": pltpu.VMEM, "h": pltpu.HBM, "o": pl.ANY}
    return pl.pallas_call(
        kernel,
        out_shape=[
            out if hasattr(out, "dtype") else jax.ShapeDtypeStruct(out, jnp.bfloat16) for out in outs
        ],
        in_specs=[pl.BlockSpec(memory_space=spaces[kind]) for kind in kinds],
        scratch_shapes=list(scratch),
        compiler_params=pltpu.CompilerParams(vmem_limit_bytes=limit << 20),
        cost_estimate=pl.CostEstimate(flops=work, bytes_accessed=work >> 8, transcendentals=0),
        name=name,
    )(*operands)


def prepare_kernel(place, tokens, gates, ids, near, far, sems):
    piece, width = far.shape
    at = pl.multiple_of(place[3] * piece, piece)
    other = pl.multiple_of((1 - place[3]) * piece, piece)
    copies = [
        pltpu.make_async_copy(tokens.at[pl.ds(at, piece), :], near.at[:, pl.ds(0, width)], sems.at[0]),
        pltpu.make_async_copy(tokens.at[pl.ds(other, piece), :], far, sems.at[1]),
    ]
    for copy in copies:
        copy.start()
    rest = gates[...]
    terms = []
    for _ in range(3):
        term = rest.astype(jnp.bfloat16).astype(jnp.float32)
        terms.append(term)
        rest = rest - term
    terms.append(ids[...].astype(jnp.float32))
    unused = piece - 4 * gates.shape[0]
    terms.append(jnp.zeros((unused, gates.shape[1]), jnp.float32))
    near[:, width:] = jnp.concatenate(terms, axis=0).astype(jnp.bfloat16)
    for copy in copies:
        copy.wait()


def prepare(place, cotangent, gates, ids, piece):
    width = cotangent.shape[1]
    return small(
        prepare_kernel,
        "prepare",
        [(piece, width + 128), (piece, width)],
        "shvv",
        (place, cotangent, gates, ids),
        [pltpu.SemaphoreType.DMA((2,))],
        limit=4,
    )


def stack_kernel(*refs):
    lines = refs[-1]
    for r in range(lines.shape[0]):
        lines[r] = refs[r][...]


def stack(pieces, *after, work=0):
    return small(
        stack_kernel,
        "stack",
        [(len(pieces),) + pieces[0].shape],
        "v" * len(pieces) + "o" * len(after),
        (*pieces, *after),
        work=work,
    )[0]


def relay_kernel(came, part, _, __, ___, line, tokens, table, following):
    line[0] = came[...]
    tokens[0] = came[:, :tokens.shape[2]]
    table[0] = came[:, tokens.shape[2]:]
    following[...] = part[...]


def relay(came, part, *after):
    piece, width = came.shape[0], came.shape[1] - 128
    return small(
        relay_kernel, "relay", [(1,) + came.shape, (1, piece, width), (1, piece, 128), part.shape], "vvooo", (came, part, *after)
    )


def turn_kernel(gate, up, *refs):
    gate_t, up_t = refs[-2:]
    tile = 128
    for source, target in ((gate, gate_t), (up, up_t)):
        for e in range(source.shape[0]):
            for at in range(0, source.shape[2], tile):
                target[e, at:at + tile] = source[e, :, at:at + tile].astype(jnp.float32).T.astype(
                    jnp.bfloat16
                )


def turn(saved_gate, saved_up, *after):
    count, units, slots = saved_gate.shape
    return small(
        turn_kernel,
        "turn",
        [(count, slots, units)] * 2,
        "vv" + "o" * len(after),
        (saved_gate, saved_up, *after),
        limit=12,
    )


def corner_kernel(far, first, over, table, side, whole_over, left, right):
    middle = left.shape[2]
    whole_over[0] = first[...]
    whole_over[1:, :, :2 * middle] = over[...]
    whole_over[1:, :, 2 * middle:] = table[...]
    left[0] = first[:, :middle]
    left[1:] = over[:, :, :middle]
    right[0] = far[:, middle:]
    right[1:] = side[:, :, middle:2 * middle]


def own_corner(far, first, over, table, side):
    count, piece, _ = over.shape
    width = first.shape[1]
    middle = far.shape[1] // 2
    return small(
        corner_kernel,
        "own_corner",
        [(count + 1, piece, width)] + [(count + 1, piece, middle)] * 2,
        "vvvvv",
        (far, first, over, table, side),
    )


def plain_corner_kernel(over, side, _, left, right):
    middle = left.shape[-1]
    left[...] = over[:, :, :middle]
    right[...] = side[:, :, middle:2 * middle]


def corner(over, side, middle, after, work=0):
    return small(
        plain_corner_kernel,
        "corner",
        [over.shape[:2] + (middle,)] * 2,
        "vvo",
        (over, side, after),
        work=work,
    )


def join_kernel(left, right, *refs):
    result = refs[-1]
    middle = left.shape[-1]
    result[:, :, :middle] = left[...]
    result[:, :, middle:] = right[...]


def join(left, right, *after, work=0):
    dims = left.shape
    return small(
        join_kernel,
        "join",
        [dims[:-1] + (2 * dims[-1],)],
        "vv" + "o" * len(after),
        (left, right, *after),
        work=work,
    )[0]


def tokens_of(own, lines, r, offsets):
    if r == 0:
        return own[...]
    return lines[r_place(r, offsets)]


def r_place(r, offsets):
    return [offset for offset in offsets if offset != 0].index(r)


def pair_base(place, line_count, r, ry, width):
    line = lax.rem(place[2] + r, line_count)
    row = place[1] if ry == 0 else 1 - place[1]
    return pl.multiple_of((line * 2 + row) * width, width)


def route_kernel(offsets, capacity, place, own, own_c, lines, lines_c, over, over_c, pick, pick_t, gate,
                 hits, gates):
    tokens = pick.shape[2] // 2
    width = over.shape[2] - 128
    core, row, line, half = place[0], place[1], place[2], place[3]
    first = (line * 4 + row * 2 + core) * 2
    for i, r in enumerate(offsets):
        for ry in range(2):
            tables = []
            for c in range(2):
                if ry == 1:
                    table = (over, over_c)[c][i, :32, width:]
                elif r == 0:
                    table = (own, own_c)[c][:32, width:]
                else:
                    table = (lines, lines_c)[c][r_place(r, offsets), :32, width:]
                tables.append(table.astype(jnp.float32))
            swapped = core > 0
            ordered = [
                jnp.where(swapped, tables[1], tables[0]), jnp.where(swapped, tables[0], tables[1])
            ]
            for c in range(2):
                block = ordered[c]
                value = block[0:8] + block[8:16] + block[16:24]
                for e in range(2):
                    named = block[24:32] == (first + e).astype(jnp.float32)
                    at = ((i * 2 + ry) * 2 + c) * 2 + e
                    hits[at:at + 1] = jnp.sum(named.astype(jnp.float32), axis=0, keepdims=True)
                    gates[at:at + 1] = jnp.sum(
                        jnp.where(named, value, 0.0), axis=0, keepdims=True
                    )
    earlier = lax.broadcasted_iota(jnp.int32, (tokens, tokens), 0) < lax.broadcasted_iota(
        jnp.int32, (tokens, tokens), 1
    )
    hit = hits[...]
    slot = jnp.dot(
        hit.astype(jnp.bfloat16),
        earlier.astype(jnp.float32).astype(jnp.bfloat16),
        preferred_element_type=jnp.float32,
    )
    slot = jnp.where(hit > 0.5, slot, -1.0)
    turned = half > 0
    slot = jnp.where(turned, pltpu.roll(slot, tokens // 2, 1), slot)
    weight = jnp.where(turned, pltpu.roll(gates[...], tokens // 2, 1), gates[...])
    order = lax.broadcasted_iota(jnp.int32, (capacity, tokens), 0).astype(jnp.float32)
    for p in range(pick.shape[0]):
        rows = []
        for e in range(2):
            for c in range(2):
                at = (p * 2 + c) * 2 + e
                ones = (order == slot[at:at + 1]).astype(jnp.float32)
                column = jnp.sum(ones * weight[at:at + 1], axis=1, keepdims=True)
                place_in = (e * 2 + c) * capacity
                gate[p, place_in:place_in + capacity] = jnp.broadcast_to(
                    column, (capacity, gate.shape[2])
                )
                own_core = (core == c).astype(jnp.float32)
                rows.append(jnp.concatenate([ones * own_core, ones * (1.0 - own_core)], axis=1))
        matrix = jnp.concatenate(rows, axis=0)
        pick[p] = matrix.astype(jnp.bfloat16)
        count = matrix.shape[0]
        square = jnp.concatenate(
            [matrix, jnp.zeros((2 * tokens - count, 2 * tokens), jnp.float32)], axis=0
        )
        pick_t[p] = square.T[:, :count].astype(jnp.bfloat16)


def route(offsets, place, table, table_c, lines, lines_c, over, over_c, capacity):
    tokens = 2 * over.shape[1]
    pairs = 2 * len(offsets)
    rows = 4 * capacity
    return small(
        functools.partial(route_kernel, offsets, capacity),
        "route",
        [
            (pairs, rows, 2 * tokens),
            (pairs, 2 * tokens, rows),
            jax.ShapeDtypeStruct((pairs, rows, 128), jnp.float32),
        ],
        "s" + "v" * 6,
        (place, table, table_c, lines, lines_c, over, over_c),
        [pltpu.VMEM((4 * pairs, tokens), jnp.float32)] * 2,
    )


def hidden_kernel(offsets, rows_of, line_count, place, *refs):
    *sources, pick, gate, w_down, saved_gate, saved_up, _, grads, slots = refs
    sources = [sources[at:at + 2] for at in range(0, len(sources), 2)]
    near, far = (sources.pop(0), sources.pop(0)) if offsets[0] == 0 and 0 in rows_of else (None, None)
    lines, side = (sources.pop(0), sources.pop(0)) if 0 in rows_of else (None, None)
    over, diag = (sources.pop(0), sources.pop(0)) if 1 in rows_of else (None, None)
    width = w_down.shape[2]
    rows = pick.shape[1] // 2
    units = w_down.shape[1]
    pairs = [(i, r, ry) for i, r in enumerate(offsets) for ry in rows_of]

    @pl.loop(0, width // TILE)
    def _(k):
        at = pl.ds(pl.multiple_of(k * TILE, TILE), TILE)
        for q, (i, r, ry) in enumerate(pairs):
            parts = []
            for c in range(2):
                if ry == 1:
                    parts += [over[c][i, :, at], diag[c][i, :, at]]
                elif r == 0:
                    parts += [near[c][:, at], far[c][:, at]]
                else:
                    j = r_place(r, offsets)
                    parts += [lines[c][j, :, at], side[c][j, :, at]]
            p = i * 2 + ry
            picked = jnp.dot(
                pick[p], jnp.concatenate(parts, axis=0), preferred_element_type=jnp.float32
            )
            weight = gate[p]
            weight = jnp.concatenate([weight] * (TILE // weight.shape[1]), axis=1)
            scaled = (picked * weight).astype(jnp.bfloat16)
            slots[0, q * rows:(q + 1) * rows, at] = scaled[:rows]
            slots[1, q * rows:(q + 1) * rows, at] = scaled[rows:]

    for e in range(2):
        total = lax.dot_general(
            slots[e], w_down[e], (((1,), (1,)), ((), ())), preferred_element_type=jnp.float32
        )
        for q, (i, r, ry) in enumerate(pairs):
            mine = slice(q * rows, (q + 1) * rows)
            saved = pl.ds(pair_base(place, line_count, r, ry, rows), rows)
            hidden_grad = total[mine]
            gate_value = saved_gate[e, saved, :].astype(jnp.float32)
            up_value = saved_up[e, saved, :].astype(jnp.float32)
            sigmoid_gate = jax.nn.sigmoid(gate_value)
            grads[e, mine, units:] = (hidden_grad * gate_value * sigmoid_gate).astype(jnp.bfloat16)
            grads[e, mine, :units] = (
                hidden_grad * up_value * sigmoid_gate * (1.0 + gate_value * (1.0 - sigmoid_gate))
            ).astype(jnp.bfloat16)


def hidden(offsets, rows_of, line_count, place, sources, pick, gate, w_down, saved, after):
    _, units, width = w_down.shape
    count = len(offsets) * len(rows_of) * pick.shape[1] // 2
    return small(
        functools.partial(hidden_kernel, offsets, rows_of, line_count),
        "hidden",
        [(2, count, 2 * units)],
        "s" + "v" * (len(sources) + 5) + "o",
        (place, *sources, pick, gate, w_down, *saved, after),
        [pltpu.VMEM((2, count, width), jnp.bfloat16)],
        limit=12,
    )[0]


def sums_kernel(offset, pairs, grads, w_gate, w_up, pick_t, _, keep, send, slots):
    rows = pick_t.shape[2] // 2
    tokens = pick_t.shape[1] // 2

    @pl.loop(0, keep.shape[2] // TILE)
    def _(k):
        at = pl.ds(pl.multiple_of(k * TILE, TILE), TILE)
        source = pl.ds(pl.multiple_of(offset + k * TILE, TILE), TILE)
        for e in range(2):
            weights = jnp.concatenate([w_gate[e, :, source], w_up[e, :, source]], axis=0)
            slots[e] = jnp.dot(grads[e], weights, preferred_element_type=jnp.float32).astype(
                jnp.bfloat16
            )
        for q, p in enumerate(pairs):
            mine = slice(q * rows, (q + 1) * rows)
            both = jnp.concatenate([slots[0, mine], slots[1, mine]], axis=0)
            total = jnp.dot(pick_t[p], both, preferred_element_type=jnp.float32).astype(
                jnp.bfloat16
            )
            keep[q, :, at] = total[:tokens]
            send[q, :, at] = total[tokens:]


def sums(offset, width, pairs, grads, w_gate, w_up, pick_t, after, work=0):
    tokens = pick_t.shape[1]
    count = grads.shape[1]
    return small(
        functools.partial(sums_kernel, offset, pairs),
        "sums",
        [(len(pairs), tokens // 2, width)] * 2,
        "vvvvo",
        (grads, w_gate, w_up, pick_t, after),
        [pltpu.VMEM((2, count, TILE), jnp.bfloat16)],
        limit=8,
        work=work,
    )


def first_left_kernel(keep, came, _, send, kept):
    piece = kept.shape[1]
    kept[...] = keep[:, :piece] + came[:, :piece]
    send[...] = keep[:, piece:] + came[:, piece:]


def first_left(keep, came, after):
    pairs, tokens, width = keep.shape
    return small(
        first_left_kernel,
        "first_left",
        [(pairs, tokens // 2, width)] * 2,
        "vvo",
        (keep, came, after),
    )


def first_right_kernel(keep, came, _, send, kept):
    for i in range(kept.shape[0]):
        kept[i] = keep[2 * i] + came[2 * i]
        send[i] = keep[2 * i + 1] + came[2 * i + 1]


def first_right(keep, came, after):
    pairs, tokens, width = keep.shape
    return small(
        first_right_kernel,
        "first_right",
        [(pairs // 2, tokens, width)] * 2,
        "vvo",
        (keep, came, after),
    )


def second_kernel(keep_l, came_l, keep_r, came_r, _, send_l, left, send_r, right):
    piece = left.shape[1]
    for i in range(left.shape[0]):
        left[i] = keep_l[2 * i] + came_l[2 * i]
        send_l[i] = keep_l[2 * i + 1] + came_l[2 * i + 1]
        right[i] = keep_r[i, :piece] + came_r[i, :piece]
        send_r[i] = keep_r[i, piece:] + came_r[i, piece:]


def second_sum(keep_l, came_l, keep_r, came_r, after):
    lines = keep_r.shape[0]
    _, piece, middle = keep_l.shape
    return small(
        second_kernel,
        "second_sum",
        [(lines, piece, middle)] * 4,
        "vvvvo",
        (keep_l, came_l, keep_r, came_r, after),
        work=1 << 36,
    )


def third_kernel(left, came_l, right, came_r, _, *outs):
    middle = left.shape[-1]
    for columns, one, other in ((slice(0, middle), left, came_l), (slice(middle, None), right, came_r)):
        for i, out in enumerate(outs):
            out[:, columns] = (one[i].astype(jnp.float32) + other[i].astype(jnp.float32)).astype(
                out.dtype
            )


def third_sum(offsets, left, came_l, right, came_r, after):
    _, piece, middle = left.shape
    return small(
        third_kernel,
        "third_sum",
        [
            jax.ShapeDtypeStruct((piece, 2 * middle), jnp.float32 if r == 0 else jnp.bfloat16)
            for r in offsets
        ],
        "vvvvo",
        (left, came_l, right, came_r, after),
        work=1 << 36,
    )


def last_kernel(*refs):
    total = refs[0][...]
    for ref in refs[1:-1]:
        total = total + ref[...].astype(jnp.float32)
    refs[-1][...] = total


def tokens_body(cotangent, gates, expert_ids, saved_gate, saved_up, w_gate, w_up, w_down):
    owners = lax.axis_size("expert")
    row_count, feature_dim = cotangent.shape
    capacity = saved_gate.shape[2] // owners
    lines = owners // 4
    piece = row_count // 2
    middle = feature_dim // 2
    me, half = lax.axis_index("expert"), lax.axis_index("tp")
    place = jnp.stack([me % 2, me // 2 % 2, me // 4, half]).astype(jnp.int32)

    part, far = prepare(place, cotangent, gates.T, expert_ids.T, piece)
    first = swap(part, "expert", 2)
    near_c, far_c = swap(part, "expert", 1), swap(far, "expert", 1)
    own = [part, near_c, far, far_c]

    def routed(offsets, moved):
        line, line_c, _, _, over, over_c = moved[:6]
        return route(offsets, place, own[0], near_c, line, line_c, over, over_c, capacity)

    def sums_by_token(offset, width, pairs, grads, pick_t, after):
        keep, send = sums(offset, width, pairs, grads, w_gate, w_up, pick_t, after)
        return [keep, swap(send, "expert", 1)], send

    def both_cores(arrays):
        return [each for array in arrays for each in (array, swap(array, "expert", 1))]

    def step_left(keep, came, after):
        send, keep = first_left(keep, came, after)
        return keep, swap(send, "tp", 1), send

    def step_right(keep, came, after):
        send, keep = first_right(keep, came, after)
        return keep, swap(send, "expert", 2), send

    (_, near), (third, second) = CHUNKS
    line, tokens, table, part = relay(along_line(part, -near), part, first, near_c, far_c)
    side, over = swap(tokens, "tp", 1), swap(tokens, "expert", 2)
    table = swap(table, "expert", 2)
    came = [along_line(part, -third), along_line(part, -second)]
    line_c = swap(line, "expert", 1)
    saved = turn(saved_gate, saved_up, line)
    over, left, right = own_corner(far, first, over, table, side)
    left, right = swap(left, "tp", 1), swap(right, "expert", 2)
    moved = [line, line_c] + both_cores([side, over])
    line = stack(came, saved[0], work=68719476736)
    line = stack([line], moved[5])[0]
    moved += both_cores([join(left, right, line)])
    pick, pick_t, gate = routed(CHUNKS[0], moved)

    side, over = swap(line, "tp", 1), swap(line, "expert", 2)
    grads = hidden(CHUNKS[0], (0, 1), lines, place, own + moved, pick, gate, w_down, saved, line)
    early_l, after = sums_by_token(0, middle, (0, 1, 2, 3), grads, pick_t, grads)
    early_r, after = sums_by_token(middle, middle, (0, 1, 2, 3), grads, pick_t, after)
    left, right = corner(over, side, middle, after, work=68719476736)
    after = left
    left, right = swap(left, "tp", 1), swap(right, "expert", 2)
    moved = both_cores([line, side, over])
    diag = join(left, right, after, work=8589934592)
    early_l = step_left(*early_l, diag)
    early_r = step_right(*early_r, early_l[-1])
    moved += both_cores([diag])
    pick, pick_t, gate = routed(CHUNKS[1], moved)
    grads = hidden(CHUNKS[1], (0, 1), lines, place, moved, pick, gate, w_down, saved, early_r[-1])
    late_l, after = sums_by_token(0, middle, (0, 1, 2, 3), grads, pick_t, grads)
    late_r, _ = sums_by_token(middle, middle, (0, 1, 2, 3), grads, pick_t, after)

    def second_step(offsets, sums_of_two, after, came):
        send_l, left, send_r, right = second_sum(*sums_of_two, after)
        came_l, came_r = swap(send_l, "expert", 2), swap(send_r, "tp", 1)
        rows = third_sum(offsets, left, came_l, right, came_r, send_l if came is None else came)
        return rows[0], [row if r == 0 else along_line(row, r) for r, row in zip(offsets, rows)], send_l

    done, early, after = second_step(CHUNKS[0], early_l[:2] + early_r[:2], early_r[-1], None)
    late_l = step_left(*late_l, after)
    late_r = step_right(*late_r, late_l[-1])
    _, late, _ = second_step(CHUNKS[1], late_l[:2] + late_r[:2], done, early[-1])
    terms = early + late
    return pl.pallas_call(
        last_kernel,
        out_shape=jax.ShapeDtypeStruct((piece, feature_dim), jnp.float32),
        compiler_params=pltpu.CompilerParams(vmem_limit_bytes=8 << 20),
        name="last_sum",
    )(*terms)


def body(*arrays):
    cotangent, gates, _, saved_gate = arrays[:4]
    owners = lax.axis_size("expert")
    fits = (
        owners == 16
        and lax.axis_size("tp") == 2
        and cotangent.shape[0] == 128
        and cotangent.shape[1] % (2 * TILE) == 0
        and gates.shape[1] == 8
        and saved_gate.shape[0] == 2
        and saved_gate.shape[2] // owners % 16 == 0
        and 4 * saved_gate.shape[2] // owners <= 256
    )
    return (tokens_body if fits else slots_body)(*arrays)


def solution(mesh):
    in_specs = (
        P("expert", None),
        P("expert", None),
        P("expert", None),
        P("expert", "tp", None),
        P("expert", "tp", None),
        P("expert", "tp", None),
        P("expert", "tp", None),
        P("expert", "tp", None),
    )
    out_specs = P(("expert", "tp"), None)
    return jax.shard_map(body, mesh=mesh, in_specs=in_specs, out_specs=out_specs, check_vma=False)
```

```python
import functools

import jax
import jax.numpy as jnp
from jax import lax
from jax.experimental import pallas as pl
from jax.experimental.pallas import tpu as pltpu
from jax.sharding import PartitionSpec as P


def route_slots(expert_ids, expert_total):
    flat_ids = expert_ids.reshape(-1)
    one_hot = (flat_ids[:, None] == jnp.arange(expert_total, dtype=jnp.int32)[None, :]).astype(
        jnp.int32
    )
    before = jnp.cumsum(one_hot, axis=0) - one_hot
    return (flat_ids, jnp.sum(before * one_hot, axis=1))


def expert_step(arrived, saved_gate, saved_up, w_gate, w_up, w_down):
    hidden_grad = jnp.einsum("efd,esd->efs", w_down, arrived, preferred_element_type=jnp.float32)
    gate_value = saved_gate.astype(jnp.float32)
    up_value = saved_up.astype(jnp.float32)
    sigmoid_gate = jax.nn.sigmoid(gate_value)
    up_grad = (hidden_grad * gate_value * sigmoid_gate).astype(jnp.bfloat16)
    gate_grad = (
        hidden_grad * up_value * sigmoid_gate * (1.0 + gate_value * (1.0 - sigmoid_gate))
    ).astype(jnp.bfloat16)
    partial_value = jnp.einsum(
        "efs,efd->esd", gate_grad, w_gate, preferred_element_type=jnp.float32
    )
    partial_value = partial_value + jnp.einsum(
        "efs,efd->esd", up_grad, w_up, preferred_element_type=jnp.float32
    )
    return partial_value.astype(jnp.bfloat16)


def slots_body(cotangent, gates, expert_ids, saved_gate, saved_up, w_gate, w_up, w_down):
    owners = lax.axis_size("expert")
    row_count, feature_dim = cotangent.shape
    top_count = expert_ids.shape[1]
    local_count, _, slot_count = saved_gate.shape
    capacity = slot_count // owners
    flat_ids, slot_pos = route_slots(expert_ids, local_count * owners)
    target = flat_ids % local_count * slot_count + flat_ids // local_count * capacity + slot_pos
    scaled = (gates[:, :, None] * cotangent.astype(jnp.float32)[:, None, :]).astype(jnp.bfloat16)
    scaled = scaled.reshape(row_count * top_count, feature_dim)
    outgoing = (
        jnp.zeros((local_count * slot_count, feature_dim), jnp.bfloat16).at[target].set(scaled)
    )
    outgoing = outgoing.reshape(local_count, slot_count, feature_dim)
    arrived = lax.all_to_all(outgoing, "expert", split_axis=1, concat_axis=1, tiled=True)
    partial_value = expert_step(arrived, saved_gate, saved_up, w_gate, w_up, w_down)
    returned = lax.all_to_all(partial_value, "expert", split_axis=1, concat_axis=1, tiled=True)
    picked = returned.reshape(local_count * slot_count, feature_dim)[target].astype(jnp.float32)
    combined = jnp.sum(picked.reshape(row_count, top_count, feature_dim), axis=1)
    return lax.psum_scatter(combined, "tp", scatter_dimension=0, tiled=True)


CHUNKS = ((0, 2), (1, 3))
TILE = 512


def swap(value, axis, step):
    count = lax.axis_size(axis)
    return lax.ppermute(value, axis, [(i, i ^ step) for i in range(count)])


def along_line(value, shift):
    count = lax.axis_size("expert")
    return lax.ppermute(value, "expert", [(i, (i + 4 * shift) % count) for i in range(count)])


def small(kernel, name, outs, kinds, operands, scratch=(), limit=8, work=0):
    spaces = {"s": pltpu.SMEM, "v": pltpu.VMEM, "h": pltpu.HBM, "o": pl.ANY}
    return pl.pallas_call(
        kernel,
        out_shape=[
            out if hasattr(out, "dtype") else jax.ShapeDtypeStruct(out, jnp.bfloat16) for out in outs
        ],
        in_specs=[pl.BlockSpec(memory_space=spaces[kind]) for kind in kinds],
        scratch_shapes=list(scratch),
        compiler_params=pltpu.CompilerParams(vmem_limit_bytes=limit << 20),
        cost_estimate=pl.CostEstimate(flops=work, bytes_accessed=work >> 8, transcendentals=0),
        name=name,
    )(*operands)


def prepare_kernel(place, tokens, gates_any, ids_any, first, table, gates, ids, sems):
    piece = first.shape[0]
    width = first.shape[1] - table.shape[1]
    near = pl.multiple_of(place[3] * piece, piece)
    copies = [
        pltpu.make_async_copy(gates_any, gates, sems.at[0]),
        pltpu.make_async_copy(ids_any, ids, sems.at[1]),
        pltpu.make_async_copy(
            tokens.at[pl.ds(near, piece), :], first.at[:, pl.ds(0, width)], sems.at[2]
        ),
    ]
    for copy in copies:
        copy.start()
    copies[0].wait()
    copies[1].wait()
    rest = gates[...]
    terms = []
    for _ in range(3):
        term = rest.astype(jnp.bfloat16).astype(jnp.float32)
        terms.append(term)
        rest = rest - term
    terms.append(ids[...].astype(jnp.float32))
    unused = piece - 4 * gates.shape[0]
    terms.append(jnp.zeros((unused, gates.shape[1]), jnp.float32))
    packed = jnp.concatenate(terms, axis=0).astype(jnp.bfloat16)
    first[:, width:] = packed
    table[...] = packed
    copies[2].wait()


def prepare(place, cotangent, gates, ids, piece):
    return small(
        prepare_kernel,
        "prepare",
        [(piece, cotangent.shape[1] + 128), (piece, 128)],
        "shhh",
        (place, cotangent, gates, ids),
        [
            pltpu.VMEM(gates.shape, jnp.float32),
            pltpu.VMEM(ids.shape, jnp.int32),
            pltpu.SemaphoreType.DMA((3,)),
        ],
        limit=4,
    )


def stack_kernel(*refs):
    lines = refs[-1]
    for r in range(lines.shape[0]):
        lines[r] = refs[r][...]


def stack(pieces, *after):
    return small(
        stack_kernel,
        "stack",
        [(len(pieces),) + pieces[0].shape],
        "v" * len(pieces) + "o" * len(after),
        (*pieces, *after),
    )[0]


def relay_kernel(came, part, line, following):
    line[0] = came[...]
    following[...] = part[...]


def relay(came, part):
    return small(
        relay_kernel, "relay", [(1,) + came.shape, part.shape], "vv", (came, part)
    )


def turn_kernel(gate, up, _, gate_t, up_t):
    tile = 128
    for e in range(gate.shape[0]):
        for at in range(0, gate.shape[2], tile):
            gate_value = gate[e, :, at:at + tile].astype(jnp.float32)
            up_value = up[e, :, at:at + tile].astype(jnp.float32)
            sigmoid_gate = jax.nn.sigmoid(gate_value)
            up_t[e, at:at + tile] = (gate_value * sigmoid_gate).T
            gate_t[e, at:at + tile] = (
                up_value * sigmoid_gate * (1.0 + gate_value * (1.0 - sigmoid_gate))
            ).T


def turn(saved_gate, saved_up, after):
    count, units, slots = saved_gate.shape
    return small(
        turn_kernel,
        "turn",
        [jax.ShapeDtypeStruct((count, slots, units), jnp.float32)] * 2,
        "vvo",
        (saved_gate, saved_up, after),
        limit=16,
    )


def corner_kernel(place, tokens, first, over, side, whole_over, left, right, sem):
    _, piece, middle = left.shape
    far = pl.multiple_of((1 - place[3]) * piece, piece)
    copy = pltpu.make_async_copy(
        tokens.at[pl.ds(far, piece), pl.ds(middle, middle)], right.at[0], sem.at[0]
    )
    copy.start()
    whole_over[0] = first[...]
    whole_over[1:] = over[...]
    left[0] = first[:, :middle]
    left[1:] = over[:, :, :middle]
    right[1:] = side[:, :, middle:2 * middle]
    copy.wait()


def own_corner(place, cotangent, first, over, side):
    count, piece, width = over.shape
    middle = cotangent.shape[1] // 2
    return small(
        corner_kernel,
        "own_corner",
        [(count + 1, piece, width)] + [(count + 1, piece, middle)] * 2,
        "shvvv",
        (place, cotangent, first, over, side),
        (pltpu.SemaphoreType.DMA((1,)),),
    )


def plain_corner_kernel(over, side, _, left, right):
    middle = left.shape[-1]
    left[...] = over[:, :, :middle]
    right[...] = side[:, :, middle:2 * middle]


def corner(over, side, middle, after):
    return small(
        plain_corner_kernel,
        "corner",
        [over.shape[:2] + (middle,)] * 2,
        "vvo",
        (over, side, after),
    )


def join_kernel(left, right, *refs):
    result = refs[-1]
    middle = left.shape[-1]
    result[:, :, :middle] = left[...]
    result[:, :, middle:] = right[...]


def join(left, right, *after, work=0):
    dims = left.shape
    return small(
        join_kernel,
        "join",
        [dims[:-1] + (2 * dims[-1],)],
        "vv" + "o" * len(after),
        (left, right, *after),
        work=work,
    )[0]


def tokens_of(own, lines, r, offsets):
    if r == 0:
        return own[...]
    return lines[r_place(r, offsets)]


def r_place(r, offsets):
    return [offset for offset in offsets if offset != 0].index(r)


def pair_base(place, line_count, r, ry, width):
    line = lax.rem(place[2] + r, line_count)
    row = place[1] if ry == 0 else 1 - place[1]
    return pl.multiple_of((line * 2 + row) * width, width)


def route_kernel(offsets, capacity, place, own, own_c, lines, lines_c, over, over_c, pick, pick_t, gate,
                 hits, gates):
    tokens = pick.shape[2] // 2
    width = over.shape[2] - 128
    core, row, line, half = place[0], place[1], place[2], place[3]
    first = (line * 4 + row * 2 + core) * 2
    for i, r in enumerate(offsets):
        for ry in range(2):
            tables = []
            for c in range(2):
                if ry == 1:
                    table = (over, over_c)[c][i, :32, width:]
                elif r == 0:
                    table = (own, own_c)[c][:32]
                else:
                    table = (lines, lines_c)[c][r_place(r, offsets), :32, width:]
                tables.append(table.astype(jnp.float32))
            swapped = core > 0
            ordered = [
                jnp.where(swapped, tables[1], tables[0]), jnp.where(swapped, tables[0], tables[1])
            ]
            for c in range(2):
                block = ordered[c]
                value = block[0:8] + block[8:16] + block[16:24]
                for e in range(2):
                    named = block[24:32] == (first + e).astype(jnp.float32)
                    at = ((i * 2 + ry) * 2 + c) * 2 + e
                    hits[at:at + 1] = jnp.sum(named.astype(jnp.float32), axis=0, keepdims=True)
                    gates[at:at + 1] = jnp.sum(
                        jnp.where(named, value, 0.0), axis=0, keepdims=True
                    )
    earlier = lax.broadcasted_iota(jnp.int32, (tokens, tokens), 0) < lax.broadcasted_iota(
        jnp.int32, (tokens, tokens), 1
    )
    hit = hits[...]
    slot = jnp.dot(
        hit.astype(jnp.bfloat16),
        earlier.astype(jnp.float32).astype(jnp.bfloat16),
        preferred_element_type=jnp.float32,
    )
    slot = jnp.where(hit > 0.5, slot, -1.0)
    turned = half > 0
    slot = jnp.where(turned, pltpu.roll(slot, tokens // 2, 1), slot)
    weight = jnp.where(turned, pltpu.roll(gates[...], tokens // 2, 1), gates[...])
    order = lax.broadcasted_iota(jnp.int32, (capacity, tokens), 0).astype(jnp.float32)
    for p in range(pick.shape[0]):
        rows = []
        for e in range(2):
            for c in range(2):
                at = (p * 2 + c) * 2 + e
                ones = (order == slot[at:at + 1]).astype(jnp.float32)
                column = jnp.sum(ones * weight[at:at + 1], axis=1, keepdims=True)
                place_in = (e * 2 + c) * capacity
                gate[p, place_in:place_in + capacity] = jnp.broadcast_to(
                    column, (capacity, gate.shape[2])
                )
                own_core = (core == c).astype(jnp.float32)
                rows.append(jnp.concatenate([ones * own_core, ones * (1.0 - own_core)], axis=1))
        matrix = jnp.concatenate(rows, axis=0)
        pick[p] = matrix.astype(jnp.bfloat16)
        count = matrix.shape[0]
        square = jnp.concatenate(
            [matrix, jnp.zeros((2 * tokens - count, 2 * tokens), jnp.float32)], axis=0
        )
        pick_t[p] = square.T[:, :count].astype(jnp.bfloat16)


def route(offsets, place, table, table_c, lines, lines_c, over, over_c, capacity):
    tokens = 2 * over.shape[1]
    pairs = 2 * len(offsets)
    rows = 4 * capacity
    return small(
        functools.partial(route_kernel, offsets, capacity),
        "route",
        [
            (pairs, rows, 2 * tokens),
            (pairs, 2 * tokens, rows),
            jax.ShapeDtypeStruct((pairs, rows, 128), jnp.float32),
        ],
        "s" + "v" * 6,
        (place, table, table_c, lines, lines_c, over, over_c),
        [pltpu.VMEM((4 * pairs, tokens), jnp.float32)] * 2,
    )


def hidden_kernel(offsets, line_count, place, own, own_c, lines, lines_c, side, side_c, over, over_c,
                  diag, diag_c, pick, gate, w_down, saved_gate, saved_up, _, grads, slots):
    piece = over.shape[1]
    width = diag.shape[2]
    rows = pick.shape[1] // 2
    units = w_down.shape[1]
    near = pl.multiple_of(place[3] * piece, piece)
    far = pl.multiple_of((1 - place[3]) * piece, piece)

    @pl.loop(0, width // TILE)
    def _(k):
        at = pl.ds(pl.multiple_of(k * TILE, TILE), TILE)
        for i, r in enumerate(offsets):
            for ry in range(2):
                parts = []
                for c in range(2):
                    if ry == 1:
                        parts += [(over, over_c)[c][i, :, at], (diag, diag_c)[c][i, :, at]]
                    elif r == 0:
                        group = (own, own_c)[c]
                        parts += [group[pl.ds(near, piece), at], group[pl.ds(far, piece), at]]
                    else:
                        j = r_place(r, offsets)
                        parts += [(lines, lines_c)[c][j, :, at], (side, side_c)[c][j, :, at]]
                p = i * 2 + ry
                picked = jnp.dot(
                    pick[p], jnp.concatenate(parts, axis=0), preferred_element_type=jnp.float32
                )
                weight = gate[p]
                weight = jnp.concatenate([weight] * (TILE // weight.shape[1]), axis=1)
                scaled = (picked * weight).astype(jnp.bfloat16)
                slots[0, p * rows:(p + 1) * rows, at] = scaled[:rows]
                slots[1, p * rows:(p + 1) * rows, at] = scaled[rows:]

    for e in range(2):
        total = lax.dot_general(
            slots[e], w_down[e], (((1,), (1,)), ((), ())), preferred_element_type=jnp.float32
        )
        for i, r in enumerate(offsets):
            for ry in range(2):
                p = i * 2 + ry
                mine = slice(p * rows, (p + 1) * rows)
                saved = pl.ds(pair_base(place, line_count, r, ry, rows), rows)
                hidden_grad = total[mine]
                grads[e, mine, units:] = (hidden_grad * saved_up[e, saved, :]).astype(jnp.bfloat16)
                grads[e, mine, :units] = (hidden_grad * saved_gate[e, saved, :]).astype(jnp.bfloat16)


def hidden(offsets, line_count, place, own, own_c, moved, pick, gate, w_down, saved, after):
    width = own.shape[1]
    units = w_down.shape[1]
    count = pick.shape[0] * pick.shape[1] // 2
    return small(
        functools.partial(hidden_kernel, offsets, line_count),
        "hidden",
        [(2, count, 2 * units)],
        "s" + "v" * 15 + "o",
        (place, own, own_c, *moved, pick, gate, w_down, *saved, after),
        [pltpu.VMEM((2, count, width), jnp.bfloat16)],
        limit=12,
    )[0]


def sums_kernel(offset, grads, w_gate, w_up, pick_t, _, keep, send, slots):
    rows = pick_t.shape[2] // 2
    tokens = pick_t.shape[1] // 2

    @pl.loop(0, keep.shape[2] // TILE)
    def _(k):
        at = pl.ds(pl.multiple_of(k * TILE, TILE), TILE)
        source = pl.ds(pl.multiple_of(offset + k * TILE, TILE), TILE)
        for e in range(2):
            weights = jnp.concatenate([w_gate[e, :, source], w_up[e, :, source]], axis=0)
            slots[e] = jnp.dot(grads[e], weights, preferred_element_type=jnp.float32).astype(
                jnp.bfloat16
            )
        for p in range(pick_t.shape[0]):
            mine = slice(p * rows, (p + 1) * rows)
            both = jnp.concatenate([slots[0, mine], slots[1, mine]], axis=0)
            total = jnp.dot(pick_t[p], both, preferred_element_type=jnp.float32).astype(
                jnp.bfloat16
            )
            keep[p, :, at] = total[:tokens]
            send[p, :, at] = total[tokens:]


def sums(offset, width, grads, w_gate, w_up, pick_t, after, work=0):
    pairs, tokens, _ = pick_t.shape
    _, count, units = grads.shape
    return small(
        functools.partial(sums_kernel, offset),
        "sums",
        [(pairs, tokens // 2, width)] * 2,
        "vvvvo",
        (grads, w_gate, w_up, pick_t, after),
        [pltpu.VMEM((2, count, TILE), jnp.bfloat16)],
        limit=8,
        work=work,
    )


def first_left_kernel(keep, came, _, send, kept):
    piece = kept.shape[1]
    kept[...] = keep[:, :piece] + came[:, :piece]
    send[...] = keep[:, piece:] + came[:, piece:]


def first_left(keep, came, after):
    pairs, tokens, width = keep.shape
    return small(
        first_left_kernel,
        "first_left",
        [(pairs, tokens // 2, width)] * 2,
        "vvo",
        (keep, came, after),
    )


def first_right_kernel(keep, came, _, send, kept):
    for i in range(kept.shape[0]):
        kept[i] = keep[2 * i] + came[2 * i]
        send[i] = keep[2 * i + 1] + came[2 * i + 1]


def first_right(keep, came, after):
    pairs, tokens, width = keep.shape
    return small(
        first_right_kernel,
        "first_right",
        [(pairs // 2, tokens, width)] * 2,
        "vvo",
        (keep, came, after),
    )


def second_kernel(keep_l, came_l, keep_r, came_r, _, send_l, left, send_r, right):
    piece = left.shape[1]
    for i in range(left.shape[0]):
        left[i] = keep_l[2 * i] + came_l[2 * i]
        send_l[i] = keep_l[2 * i + 1] + came_l[2 * i + 1]
        right[i] = keep_r[i, :piece] + came_r[i, :piece]
        send_r[i] = keep_r[i, piece:] + came_r[i, piece:]


def second_sum(keep_l, came_l, keep_r, came_r, after):
    lines = keep_r.shape[0]
    _, piece, middle = keep_l.shape
    return small(
        second_kernel,
        "second_sum",
        [(lines, piece, middle)] * 4,
        "vvvvo",
        (keep_l, came_l, keep_r, came_r, after),
        work=1 << 36,
    )


def third_kernel(left, came_l, right, came_r, _, *outs):
    middle = left.shape[-1]
    for columns, one, other in ((slice(0, middle), left, came_l), (slice(middle, None), right, came_r)):
        for i, out in enumerate(outs):
            out[:, columns] = (one[i].astype(jnp.float32) + other[i].astype(jnp.float32)).astype(
                out.dtype
            )


def third_sum(offsets, left, came_l, right, came_r, after):
    _, piece, middle = left.shape
    return small(
        third_kernel,
        "third_sum",
        [
            jax.ShapeDtypeStruct((piece, 2 * middle), jnp.float32 if r == 0 else jnp.bfloat16)
            for r in offsets
        ],
        "vvvvo",
        (left, came_l, right, came_r, after),
        work=1 << 36,
    )


def last_kernel(*refs):
    total = refs[0][...]
    for ref in refs[1:-1]:
        total = total + ref[...].astype(jnp.float32)
    refs[-1][...] = total


def tokens_body(cotangent, gates, expert_ids, saved_gate, saved_up, w_gate, w_up, w_down):
    owners = lax.axis_size("expert")
    row_count, feature_dim = cotangent.shape
    capacity = saved_gate.shape[2] // owners
    lines = owners // 4
    piece = row_count // 2
    middle = feature_dim // 2
    me, half = lax.axis_index("expert"), lax.axis_index("tp")
    place = jnp.stack([me % 2, me // 2 % 2, me // 4, half]).astype(jnp.int32)

    part, table = prepare(place, cotangent, gates.T, expert_ids.T, piece)
    first = swap(part, "expert", 2)
    own_c, table_c = swap(cotangent, "expert", 1), swap(table, "expert", 1)
    gathered, saved = [], None

    def compute(index, after):
        offsets, moved = CHUNKS[index], gathered[index]
        line, line_c, _, _, over, over_c = moved[:6]
        pick, pick_t, gate = route(
            offsets, place, table, table_c, line, line_c, over, over_c, capacity
        )
        grads = hidden(
            offsets, lines, place, cotangent, own_c, moved, pick, gate, w_down, saved, after
        )
        return grads, pick_t

    def sums_by_token(offset, grads, pick_t, after, work=0):
        keep, send = sums(offset, middle, grads, w_gate, w_up, pick_t, after, work)
        return [keep, swap(send, "expert", 1)], send

    for offsets in CHUNKS:
        pieces = [along_line(part, -r) for r in offsets if r != 0]
        if saved is None:
            line, part = relay(pieces[0], part)
            saved = turn(saved_gate, saved_up, line)
        else:
            line = stack(pieces, saved[0])
        side, over = swap(line, "tp", 1), swap(line, "expert", 2)
        if offsets[0] == 0:
            over, left, right = own_corner(place, cotangent, first, over, side)
            after = (left,)
        else:
            early = compute(0, line)
            grads, pick_t = early
            early_l, after = sums_by_token(0, grads, pick_t, grads)
            left, right = corner(over, side, middle, after)
            early_r, after = sums_by_token(middle, grads, pick_t, left, 68719476736)
            after = (after,)
        diag = join(swap(left, "tp", 1), swap(right, "expert", 2), *after, work=8589934592)
        moved = []
        for array in (line, side, over, diag):
            moved += [array, swap(array, "expert", 1)]
        gathered.append(moved)

    def first_step(keep_l, came_l, keep_r, came_r, after):
        send_l, keep_l = first_left(keep_l, came_l, after)
        send_r, keep_r = first_right(keep_r, came_r, send_l)
        return keep_l, swap(send_l, "tp", 1), keep_r, swap(send_r, "expert", 2), send_r

    def second_step(offsets, sums_of_two, after, came):
        send_l, left, send_r, right = second_sum(*sums_of_two, after)
        came_l, came_r = swap(send_l, "expert", 2), swap(send_r, "tp", 1)
        rows = third_sum(offsets, left, came_l, right, came_r, send_l if came is None else came)
        return rows[0], [row if r == 0 else along_line(row, r) for r, row in zip(offsets, rows)], send_l

    early = first_step(*early_l, *early_r, gathered[1][6])
    grads, pick_t = compute(1, early[4])
    late_l, after = sums_by_token(0, grads, pick_t, grads)
    late_r, _ = sums_by_token(middle, grads, pick_t, after)
    done, early, after = second_step(CHUNKS[0], early[:4], early[4], None)
    late = first_step(*late_l, *late_r, after)
    _, late, _ = second_step(CHUNKS[1], late[:4], done, early[-1])
    terms = early + late
    return pl.pallas_call(
        last_kernel,
        out_shape=jax.ShapeDtypeStruct((piece, feature_dim), jnp.float32),
        compiler_params=pltpu.CompilerParams(vmem_limit_bytes=8 << 20),
        name="last_sum",
    )(*terms)


def body(*arrays):
    cotangent, gates, _, saved_gate = arrays[:4]
    owners = lax.axis_size("expert")
    fits = (
        owners == 16
        and lax.axis_size("tp") == 2
        and cotangent.shape[0] == 128
        and cotangent.shape[1] % (2 * TILE) == 0
        and gates.shape[1] == 8
        and saved_gate.shape[0] == 2
        and saved_gate.shape[2] // owners % 16 == 0
        and 4 * saved_gate.shape[2] // owners <= 256
    )
    return (tokens_body if fits else slots_body)(*arrays)


def solution(mesh):
    in_specs = (
        P("expert", None),
        P("expert", None),
        P("expert", None),
        P("expert", "tp", None),
        P("expert", "tp", None),
        P("expert", "tp", None),
        P("expert", "tp", None),
        P("expert", "tp", None),
    )
    out_specs = P(("expert", "tp"), None)
    return jax.shard_map(body, mesh=mesh, in_specs=in_specs, out_specs=out_specs, check_vma=False)
```

```python
import functools

import jax
import jax.numpy as jnp
from jax import lax
from jax.experimental import pallas as pl
from jax.experimental.pallas import tpu as pltpu
from jax.sharding import PartitionSpec as P


def route_slots(expert_ids, expert_total):
    flat_ids = expert_ids.reshape(-1)
    one_hot = (flat_ids[:, None] == jnp.arange(expert_total, dtype=jnp.int32)[None, :]).astype(
        jnp.int32
    )
    before = jnp.cumsum(one_hot, axis=0) - one_hot
    return (flat_ids, jnp.sum(before * one_hot, axis=1))


def expert_step(arrived, saved_gate, saved_up, w_gate, w_up, w_down):
    hidden_grad = jnp.einsum("efd,esd->efs", w_down, arrived, preferred_element_type=jnp.float32)
    gate_value = saved_gate.astype(jnp.float32)
    up_value = saved_up.astype(jnp.float32)
    sigmoid_gate = jax.nn.sigmoid(gate_value)
    up_grad = (hidden_grad * gate_value * sigmoid_gate).astype(jnp.bfloat16)
    gate_grad = (
        hidden_grad * up_value * sigmoid_gate * (1.0 + gate_value * (1.0 - sigmoid_gate))
    ).astype(jnp.bfloat16)
    partial_value = jnp.einsum(
        "efs,efd->esd", gate_grad, w_gate, preferred_element_type=jnp.float32
    )
    partial_value = partial_value + jnp.einsum(
        "efs,efd->esd", up_grad, w_up, preferred_element_type=jnp.float32
    )
    return partial_value.astype(jnp.bfloat16)


def slots_body(cotangent, gates, expert_ids, saved_gate, saved_up, w_gate, w_up, w_down):
    owners = lax.axis_size("expert")
    row_count, feature_dim = cotangent.shape
    top_count = expert_ids.shape[1]
    local_count, _, slot_count = saved_gate.shape
    capacity = slot_count // owners
    flat_ids, slot_pos = route_slots(expert_ids, local_count * owners)
    target = flat_ids % local_count * slot_count + flat_ids // local_count * capacity + slot_pos
    scaled = (gates[:, :, None] * cotangent.astype(jnp.float32)[:, None, :]).astype(jnp.bfloat16)
    scaled = scaled.reshape(row_count * top_count, feature_dim)
    outgoing = (
        jnp.zeros((local_count * slot_count, feature_dim), jnp.bfloat16).at[target].set(scaled)
    )
    outgoing = outgoing.reshape(local_count, slot_count, feature_dim)
    arrived = lax.all_to_all(outgoing, "expert", split_axis=1, concat_axis=1, tiled=True)
    partial_value = expert_step(arrived, saved_gate, saved_up, w_gate, w_up, w_down)
    returned = lax.all_to_all(partial_value, "expert", split_axis=1, concat_axis=1, tiled=True)
    picked = returned.reshape(local_count * slot_count, feature_dim)[target].astype(jnp.float32)
    combined = jnp.sum(picked.reshape(row_count, top_count, feature_dim), axis=1)
    return lax.psum_scatter(combined, "tp", scatter_dimension=0, tiled=True)


CHUNKS = ((0, 2), (1, 3))
TILE = 512


def swap(value, axis, step):
    count = lax.axis_size(axis)
    return lax.ppermute(value, axis, [(i, i ^ step) for i in range(count)])


def along_line(value, shift):
    count = lax.axis_size("expert")
    return lax.ppermute(value, "expert", [(i, (i + 4 * shift) % count) for i in range(count)])


def small(kernel, name, outs, kinds, operands, scratch=(), limit=8, work=0):
    spaces = {"s": pltpu.SMEM, "v": pltpu.VMEM, "h": pltpu.HBM, "o": pl.ANY}
    return pl.pallas_call(
        kernel,
        out_shape=[
            out if hasattr(out, "dtype") else jax.ShapeDtypeStruct(out, jnp.bfloat16) for out in outs
        ],
        in_specs=[pl.BlockSpec(memory_space=spaces[kind]) for kind in kinds],
        scratch_shapes=list(scratch),
        compiler_params=pltpu.CompilerParams(vmem_limit_bytes=limit << 20),
        cost_estimate=pl.CostEstimate(flops=work, bytes_accessed=work >> 8, transcendentals=0),
        name=name,
    )(*operands)


def prepare_kernel(place, tokens, gates_any, ids_any, first, table, gates, ids, sems):
    piece = first.shape[0]
    width = first.shape[1] - table.shape[1]
    near = pl.multiple_of(place[3] * piece, piece)
    copies = [
        pltpu.make_async_copy(gates_any, gates, sems.at[0]),
        pltpu.make_async_copy(ids_any, ids, sems.at[1]),
        pltpu.make_async_copy(
            tokens.at[pl.ds(near, piece), :], first.at[:, pl.ds(0, width)], sems.at[2]
        ),
    ]
    for copy in copies:
        copy.start()
    copies[0].wait()
    copies[1].wait()
    rest = gates[...]
    terms = []
    for _ in range(3):
        term = rest.astype(jnp.bfloat16).astype(jnp.float32)
        terms.append(term)
        rest = rest - term
    terms.append(ids[...].astype(jnp.float32))
    unused = piece - 4 * gates.shape[0]
    terms.append(jnp.zeros((unused, gates.shape[1]), jnp.float32))
    packed = jnp.concatenate(terms, axis=0).astype(jnp.bfloat16)
    first[:, width:] = packed
    table[...] = packed
    copies[2].wait()


def prepare(place, cotangent, gates, ids, piece):
    return small(
        prepare_kernel,
        "prepare",
        [(piece, cotangent.shape[1] + 128), (piece, 128)],
        "shhh",
        (place, cotangent, gates, ids),
        [
            pltpu.VMEM(gates.shape, jnp.float32),
            pltpu.VMEM(ids.shape, jnp.int32),
            pltpu.SemaphoreType.DMA((3,)),
        ],
        limit=4,
    )


def stack_kernel(*refs):
    lines = refs[-1]
    for r in range(lines.shape[0]):
        lines[r] = refs[r][...]


def stack(pieces, *after):
    return small(
        stack_kernel,
        "stack",
        [(len(pieces),) + pieces[0].shape],
        "v" * len(pieces) + "o" * len(after),
        (*pieces, *after),
    )[0]


def relay_kernel(came, part, line, following):
    line[0] = came[...]
    following[...] = part[...]


def relay(came, part):
    return small(
        relay_kernel, "relay", [(1,) + came.shape, part.shape], "vv", (came, part)
    )


def turn_kernel(gate, up, _, gate_t, up_t):
    tile = 128
    for e in range(gate.shape[0]):
        for at in range(0, gate.shape[2], tile):
            gate_value = gate[e, :, at:at + tile].astype(jnp.float32)
            up_value = up[e, :, at:at + tile].astype(jnp.float32)
            sigmoid_gate = jax.nn.sigmoid(gate_value)
            up_t[e, at:at + tile] = (gate_value * sigmoid_gate).T
            gate_t[e, at:at + tile] = (
                up_value * sigmoid_gate * (1.0 + gate_value * (1.0 - sigmoid_gate))
            ).T


def turn(saved_gate, saved_up, after):
    count, units, slots = saved_gate.shape
    return small(
        turn_kernel,
        "turn",
        [jax.ShapeDtypeStruct((count, slots, units), jnp.float32)] * 2,
        "vvo",
        (saved_gate, saved_up, after),
        limit=16,
    )


def corner_kernel(place, tokens, first, over, side, whole_over, left, right, sem):
    _, piece, middle = left.shape
    far = pl.multiple_of((1 - place[3]) * piece, piece)
    copy = pltpu.make_async_copy(
        tokens.at[pl.ds(far, piece), pl.ds(middle, middle)], right.at[0], sem.at[0]
    )
    copy.start()
    whole_over[0] = first[...]
    whole_over[1:] = over[...]
    left[0] = first[:, :middle]
    left[1:] = over[:, :, :middle]
    right[1:] = side[:, :, middle:2 * middle]
    copy.wait()


def own_corner(place, cotangent, first, over, side):
    count, piece, width = over.shape
    middle = cotangent.shape[1] // 2
    return small(
        corner_kernel,
        "own_corner",
        [(count + 1, piece, width)] + [(count + 1, piece, middle)] * 2,
        "shvvv",
        (place, cotangent, first, over, side),
        (pltpu.SemaphoreType.DMA((1,)),),
    )


def plain_corner_kernel(over, side, _, left, right):
    middle = left.shape[-1]
    left[...] = over[:, :, :middle]
    right[...] = side[:, :, middle:2 * middle]


def corner(over, side, middle, after):
    return small(
        plain_corner_kernel,
        "corner",
        [over.shape[:2] + (middle,)] * 2,
        "vvo",
        (over, side, after),
    )


def join_kernel(left, right, *refs):
    result = refs[-1]
    middle = left.shape[-1]
    result[:, :, :middle] = left[...]
    result[:, :, middle:] = right[...]


def join(left, right, *after, work=0):
    dims = left.shape
    return small(
        join_kernel,
        "join",
        [dims[:-1] + (2 * dims[-1],)],
        "vv" + "o" * len(after),
        (left, right, *after),
        work=work,
    )[0]


def tokens_of(own, lines, r, offsets):
    if r == 0:
        return own[...]
    return lines[r_place(r, offsets)]


def r_place(r, offsets):
    return [offset for offset in offsets if offset != 0].index(r)


def pair_base(place, line_count, r, ry, width):
    line = lax.rem(place[2] + r, line_count)
    row = place[1] if ry == 0 else 1 - place[1]
    return pl.multiple_of((line * 2 + row) * width, width)


def route_kernel(offsets, capacity, place, own, own_c, lines, lines_c, over, over_c, pick, pick_t, gate,
                 hits, gates):
    tokens = pick.shape[2] // 2
    width = over.shape[2] - 128
    core, row, line, half = place[0], place[1], place[2], place[3]
    first = (line * 4 + row * 2 + core) * 2
    for i, r in enumerate(offsets):
        for ry in range(2):
            tables = []
            for c in range(2):
                if ry == 1:
                    table = (over, over_c)[c][i, :32, width:]
                elif r == 0:
                    table = (own, own_c)[c][:32]
                else:
                    table = (lines, lines_c)[c][r_place(r, offsets), :32, width:]
                tables.append(table.astype(jnp.float32))
            swapped = core > 0
            ordered = [
                jnp.where(swapped, tables[1], tables[0]), jnp.where(swapped, tables[0], tables[1])
            ]
            for c in range(2):
                block = ordered[c]
                value = block[0:8] + block[8:16] + block[16:24]
                for e in range(2):
                    named = block[24:32] == (first + e).astype(jnp.float32)
                    at = ((i * 2 + ry) * 2 + c) * 2 + e
                    hits[at:at + 1] = jnp.sum(named.astype(jnp.float32), axis=0, keepdims=True)
                    gates[at:at + 1] = jnp.sum(
                        jnp.where(named, value, 0.0), axis=0, keepdims=True
                    )
    earlier = lax.broadcasted_iota(jnp.int32, (tokens, tokens), 0) < lax.broadcasted_iota(
        jnp.int32, (tokens, tokens), 1
    )
    hit = hits[...]
    slot = jnp.dot(
        hit.astype(jnp.bfloat16),
        earlier.astype(jnp.float32).astype(jnp.bfloat16),
        preferred_element_type=jnp.float32,
    )
    slot = jnp.where(hit > 0.5, slot, -1.0)
    turned = half > 0
    slot = jnp.where(turned, pltpu.roll(slot, tokens // 2, 1), slot)
    weight = jnp.where(turned, pltpu.roll(gates[...], tokens // 2, 1), gates[...])
    order = lax.broadcasted_iota(jnp.int32, (capacity, tokens), 0).astype(jnp.float32)
    for p in range(pick.shape[0]):
        rows = []
        for e in range(2):
            for c in range(2):
                at = (p * 2 + c) * 2 + e
                ones = (order == slot[at:at + 1]).astype(jnp.float32)
                column = jnp.sum(ones * weight[at:at + 1], axis=1, keepdims=True)
                place_in = (e * 2 + c) * capacity
                gate[p, place_in:place_in + capacity] = jnp.broadcast_to(
                    column, (capacity, gate.shape[2])
                )
                own_core = (core == c).astype(jnp.float32)
                rows.append(jnp.concatenate([ones * own_core, ones * (1.0 - own_core)], axis=1))
        matrix = jnp.concatenate(rows, axis=0)
        pick[p] = matrix.astype(jnp.bfloat16)
        count = matrix.shape[0]
        square = jnp.concatenate(
            [matrix, jnp.zeros((2 * tokens - count, 2 * tokens), jnp.float32)], axis=0
        )
        pick_t[p] = square.T[:, :count].astype(jnp.bfloat16)


def route(offsets, place, table, table_c, lines, lines_c, over, over_c, capacity):
    tokens = 2 * over.shape[1]
    pairs = 2 * len(offsets)
    rows = 4 * capacity
    return small(
        functools.partial(route_kernel, offsets, capacity),
        "route",
        [
            (pairs, rows, 2 * tokens),
            (pairs, 2 * tokens, rows),
            jax.ShapeDtypeStruct((pairs, rows, 128), jnp.float32),
        ],
        "s" + "v" * 6,
        (place, table, table_c, lines, lines_c, over, over_c),
        [pltpu.VMEM((4 * pairs, tokens), jnp.float32)] * 2,
    )


def hidden_kernel(offsets, line_count, place, own, own_c, lines, lines_c, side, side_c, over, over_c,
                  diag, diag_c, pick, gate, w_down, saved_gate, saved_up, _, grads, slots):
    piece = over.shape[1]
    width = diag.shape[2]
    rows = pick.shape[1] // 2
    units = w_down.shape[1]
    near = pl.multiple_of(place[3] * piece, piece)
    far = pl.multiple_of((1 - place[3]) * piece, piece)

    @pl.loop(0, width // TILE)
    def _(k):
        at = pl.ds(pl.multiple_of(k * TILE, TILE), TILE)
        for i, r in enumerate(offsets):
            for ry in range(2):
                parts = []
                for c in range(2):
                    if ry == 1:
                        parts += [(over, over_c)[c][i, :, at], (diag, diag_c)[c][i, :, at]]
                    elif r == 0:
                        group = (own, own_c)[c]
                        parts += [group[pl.ds(near, piece), at], group[pl.ds(far, piece), at]]
                    else:
                        j = r_place(r, offsets)
                        parts += [(lines, lines_c)[c][j, :, at], (side, side_c)[c][j, :, at]]
                p = i * 2 + ry
                picked = jnp.dot(
                    pick[p], jnp.concatenate(parts, axis=0), preferred_element_type=jnp.float32
                )
                weight = gate[p]
                weight = jnp.concatenate([weight] * (TILE // weight.shape[1]), axis=1)
                scaled = (picked * weight).astype(jnp.bfloat16)
                slots[0, p * rows:(p + 1) * rows, at] = scaled[:rows]
                slots[1, p * rows:(p + 1) * rows, at] = scaled[rows:]

    for e in range(2):
        total = lax.dot_general(
            slots[e], w_down[e], (((1,), (1,)), ((), ())), preferred_element_type=jnp.float32
        )
        for i, r in enumerate(offsets):
            for ry in range(2):
                p = i * 2 + ry
                mine = slice(p * rows, (p + 1) * rows)
                saved = pl.ds(pair_base(place, line_count, r, ry, rows), rows)
                hidden_grad = total[mine]
                grads[e, mine, units:] = (hidden_grad * saved_up[e, saved, :]).astype(jnp.bfloat16)
                grads[e, mine, :units] = (hidden_grad * saved_gate[e, saved, :]).astype(jnp.bfloat16)


def hidden(offsets, line_count, place, own, own_c, moved, pick, gate, w_down, saved, after):
    width = own.shape[1]
    units = w_down.shape[1]
    count = pick.shape[0] * pick.shape[1] // 2
    return small(
        functools.partial(hidden_kernel, offsets, line_count),
        "hidden",
        [(2, count, 2 * units)],
        "s" + "v" * 15 + "o",
        (place, own, own_c, *moved, pick, gate, w_down, *saved, after),
        [pltpu.VMEM((2, count, width), jnp.bfloat16)],
        limit=12,
    )[0]


def sums_kernel(offset, grads, w_gate, w_up, pick_t, _, keep, send, slots):
    rows = pick_t.shape[2] // 2
    tokens = pick_t.shape[1] // 2

    @pl.loop(0, keep.shape[2] // TILE)
    def _(k):
        at = pl.ds(pl.multiple_of(k * TILE, TILE), TILE)
        source = pl.ds(pl.multiple_of(offset + k * TILE, TILE), TILE)
        for e in range(2):
            weights = jnp.concatenate([w_gate[e, :, source], w_up[e, :, source]], axis=0)
            slots[e] = jnp.dot(grads[e], weights, preferred_element_type=jnp.float32).astype(
                jnp.bfloat16
            )
        for p in range(pick_t.shape[0]):
            mine = slice(p * rows, (p + 1) * rows)
            both = jnp.concatenate([slots[0, mine], slots[1, mine]], axis=0)
            total = jnp.dot(pick_t[p], both, preferred_element_type=jnp.float32).astype(
                jnp.bfloat16
            )
            keep[p, :, at] = total[:tokens]
            send[p, :, at] = total[tokens:]


def sums(offset, width, grads, w_gate, w_up, pick_t, after, work=0):
    pairs, tokens, _ = pick_t.shape
    _, count, units = grads.shape
    return small(
        functools.partial(sums_kernel, offset),
        "sums",
        [(pairs, tokens // 2, width)] * 2,
        "vvvvo",
        (grads, w_gate, w_up, pick_t, after),
        [pltpu.VMEM((2, count, TILE), jnp.bfloat16)],
        limit=8,
        work=work,
    )


def first_left_kernel(keep, came, _, send, kept):
    piece = kept.shape[1]
    kept[...] = keep[:, :piece] + came[:, :piece]
    send[...] = keep[:, piece:] + came[:, piece:]


def first_left(keep, came, after):
    pairs, tokens, width = keep.shape
    return small(
        first_left_kernel,
        "first_left",
        [(pairs, tokens // 2, width)] * 2,
        "vvo",
        (keep, came, after),
    )


def first_right_kernel(keep, came, _, send, kept):
    for i in range(kept.shape[0]):
        kept[i] = keep[2 * i] + came[2 * i]
        send[i] = keep[2 * i + 1] + came[2 * i + 1]


def first_right(keep, came, after):
    pairs, tokens, width = keep.shape
    return small(
        first_right_kernel,
        "first_right",
        [(pairs // 2, tokens, width)] * 2,
        "vvo",
        (keep, came, after),
    )


def second_kernel(keep_l, came_l, keep_r, came_r, _, send_l, left, send_r, right):
    piece = left.shape[1]
    for i in range(left.shape[0]):
        left[i] = keep_l[2 * i] + came_l[2 * i]
        send_l[i] = keep_l[2 * i + 1] + came_l[2 * i + 1]
        right[i] = keep_r[i, :piece] + came_r[i, :piece]
        send_r[i] = keep_r[i, piece:] + came_r[i, piece:]


def second_sum(keep_l, came_l, keep_r, came_r, after):
    lines = keep_r.shape[0]
    _, piece, middle = keep_l.shape
    return small(
        second_kernel,
        "second_sum",
        [(lines, piece, middle)] * 4,
        "vvvvo",
        (keep_l, came_l, keep_r, came_r, after),
        work=1 << 36,
    )


def second_apart_kernel(keep_l, came_l, keep_r, came_r, _, *outs):
    piece = outs[0].shape[0]
    for i in range(keep_r.shape[0]):
        send_l, left, send_r, right = outs[4 * i:4 * i + 4]
        left[...] = keep_l[2 * i] + came_l[2 * i]
        send_l[...] = keep_l[2 * i + 1] + came_l[2 * i + 1]
        right[...] = keep_r[i, :piece] + came_r[i, :piece]
        send_r[...] = keep_r[i, piece:] + came_r[i, piece:]


def second_apart(keep_l, came_l, keep_r, came_r, after):
    lines = keep_r.shape[0]
    _, piece, middle = keep_l.shape
    return small(
        second_apart_kernel,
        "second_sum",
        [(piece, middle)] * (4 * lines),
        "vvvvo",
        (keep_l, came_l, keep_r, came_r, after),
        work=1 << 36,
    )


def third_apart_kernel(left, came_l, right, came_r, _, out):
    middle = left.shape[-1]
    out[:, :middle] = left[...] + came_l[...]
    out[:, middle:] = right[...] + came_r[...]


def third_apart(left, came_l, right, came_r, after):
    piece, middle = left.shape
    return small(
        third_apart_kernel,
        "third_sum",
        [(piece, 2 * middle)],
        "vvvvo",
        (left, came_l, right, came_r, after),
    )[0]


def third_kernel(left, came_l, right, came_r, _, *outs):
    middle = left.shape[-1]
    for columns, one, other in ((slice(0, middle), left, came_l), (slice(middle, None), right, came_r)):
        for i, out in enumerate(outs):
            out[:, columns] = (one[i].astype(jnp.float32) + other[i].astype(jnp.float32)).astype(
                out.dtype
            )


def third_sum(offsets, left, came_l, right, came_r, after):
    _, piece, middle = left.shape
    return small(
        third_kernel,
        "third_sum",
        [
            jax.ShapeDtypeStruct((piece, 2 * middle), jnp.float32 if r == 0 else jnp.bfloat16)
            for r in offsets
        ],
        "vvvvo",
        (left, came_l, right, came_r, after),
        work=1 << 36,
    )


def last_kernel(*refs):
    total = refs[0][...]
    for ref in refs[1:-1]:
        total = total + ref[...].astype(jnp.float32)
    refs[-1][...] = total


def add_up(terms, name, work=0):
    return small(
        last_kernel,
        name,
        [jax.ShapeDtypeStruct(terms[0].shape, jnp.float32)],
        "v" * len(terms),
        terms,
        work=work,
    )[0]


def tokens_body(cotangent, gates, expert_ids, saved_gate, saved_up, w_gate, w_up, w_down):
    owners = lax.axis_size("expert")
    row_count, feature_dim = cotangent.shape
    capacity = saved_gate.shape[2] // owners
    lines = owners // 4
    piece = row_count // 2
    middle = feature_dim // 2
    me, half = lax.axis_index("expert"), lax.axis_index("tp")
    place = jnp.stack([me % 2, me // 2 % 2, me // 4, half]).astype(jnp.int32)

    part, table = prepare(place, cotangent, gates.T, expert_ids.T, piece)
    first = swap(part, "expert", 2)
    own_c, table_c = swap(cotangent, "expert", 1), swap(table, "expert", 1)
    gathered, saved = [], None

    def compute(index, after):
        offsets, moved = CHUNKS[index], gathered[index]
        line, line_c, _, _, over, over_c = moved[:6]
        pick, pick_t, gate = route(
            offsets, place, table, table_c, line, line_c, over, over_c, capacity
        )
        grads = hidden(
            offsets, lines, place, cotangent, own_c, moved, pick, gate, w_down, saved, after
        )
        return grads, pick_t

    def sums_by_token(offset, grads, pick_t, after, work=0):
        keep, send = sums(offset, middle, grads, w_gate, w_up, pick_t, after, work)
        return [keep, swap(send, "expert", 1)], send

    for offsets in CHUNKS:
        pieces = [along_line(part, -r) for r in offsets if r != 0]
        if saved is None:
            line, part = relay(pieces[0], part)
            saved = turn(saved_gate, saved_up, line)
        else:
            line = stack(pieces, saved[0])
        side, over = swap(line, "tp", 1), swap(line, "expert", 2)
        if offsets[0] == 0:
            over, left, right = own_corner(place, cotangent, first, over, side)
            after = (left,)
        else:
            early = compute(0, line)
            grads, pick_t = early
            early_l, after = sums_by_token(0, grads, pick_t, grads)
            left, right = corner(over, side, middle, after)
            early_r, after = sums_by_token(middle, grads, pick_t, left, 68719476736)
            after = (after,)
        diag = join(swap(left, "tp", 1), swap(right, "expert", 2), *after, work=8589934592)
        moved = []
        for array in (line, side, over, diag):
            moved += [array, swap(array, "expert", 1)]
        gathered.append(moved)

    def first_step(keep_l, came_l, keep_r, came_r, after):
        send_l, keep_l = first_left(keep_l, came_l, after)
        send_r, keep_r = first_right(keep_r, came_r, send_l)
        return keep_l, swap(send_l, "tp", 1), keep_r, swap(send_r, "expert", 2), send_r

    def second_step(offsets, sums_of_two, after, came):
        send_l, left, send_r, right = second_sum(*sums_of_two, after)
        came_l, came_r = swap(send_l, "expert", 2), swap(send_r, "tp", 1)
        rows = third_sum(offsets, left, came_l, right, came_r, send_l if came is None else came)
        return rows[0], [row if r == 0 else along_line(row, r) for r, row in zip(offsets, rows)], send_l

    early = first_step(*early_l, *early_r, gathered[1][6])
    grads, pick_t = compute(1, early[4])
    late_l, after = sums_by_token(0, grads, pick_t, grads)
    late_r, _ = sums_by_token(middle, grads, pick_t, after)
    done, early, after = second_step(CHUNKS[0], early[:4], early[4], None)
    late = first_step(*late_l, *late_r, after)
    parts = second_apart(*late[:4], done)
    after, total = early[-1], None
    for i, r in enumerate(CHUNKS[1]):
        send_l, left, send_r, right = parts[4 * i:4 * i + 4]
        came_l, came_r = swap(send_l, "expert", 2), swap(send_r, "tp", 1)
        after = third_apart(left, came_l, right, came_r, after)
        came = along_line(after, r)
        if total is None:
            total = add_up(early + [came], "middle_sum", work=0)
    return add_up([total, came], "last_sum")


def body(*arrays):
    cotangent, gates, _, saved_gate = arrays[:4]
    owners = lax.axis_size("expert")
    fits = (
        owners == 16
        and lax.axis_size("tp") == 2
        and cotangent.shape[0] == 128
        and cotangent.shape[1] % (2 * TILE) == 0
        and gates.shape[1] == 8
        and saved_gate.shape[0] == 2
        and saved_gate.shape[2] // owners % 16 == 0
        and 4 * saved_gate.shape[2] // owners <= 256
    )
    return (tokens_body if fits else slots_body)(*arrays)


def solution(mesh):
    in_specs = (
        P("expert", None),
        P("expert", None),
        P("expert", None),
        P("expert", "tp", None),
        P("expert", "tp", None),
        P("expert", "tp", None),
        P("expert", "tp", None),
        P("expert", "tp", None),
    )
    out_specs = P(("expert", "tp"), None)
    return jax.shard_map(body, mesh=mesh, in_specs=in_specs, out_specs=out_specs, check_vma=False)
```

```python
import functools

import jax
import jax.numpy as jnp
from jax import lax
from jax.experimental import pallas as pl
from jax.experimental.pallas import tpu as pltpu
from jax.sharding import PartitionSpec as P


def route_slots(expert_ids, expert_total):
    flat_ids = expert_ids.reshape(-1)
    one_hot = (flat_ids[:, None] == jnp.arange(expert_total, dtype=jnp.int32)[None, :]).astype(
        jnp.int32
    )
    before = jnp.cumsum(one_hot, axis=0) - one_hot
    return (flat_ids, jnp.sum(before * one_hot, axis=1))


def expert_step(arrived, saved_gate, saved_up, w_gate, w_up, w_down):
    hidden_grad = jnp.einsum("efd,esd->efs", w_down, arrived, preferred_element_type=jnp.float32)
    gate_value = saved_gate.astype(jnp.float32)
    up_value = saved_up.astype(jnp.float32)
    sigmoid_gate = jax.nn.sigmoid(gate_value)
    up_grad = (hidden_grad * gate_value * sigmoid_gate).astype(jnp.bfloat16)
    gate_grad = (
        hidden_grad * up_value * sigmoid_gate * (1.0 + gate_value * (1.0 - sigmoid_gate))
    ).astype(jnp.bfloat16)
    partial_value = jnp.einsum(
        "efs,efd->esd", gate_grad, w_gate, preferred_element_type=jnp.float32
    )
    partial_value = partial_value + jnp.einsum(
        "efs,efd->esd", up_grad, w_up, preferred_element_type=jnp.float32
    )
    return partial_value.astype(jnp.bfloat16)


def slots_body(cotangent, gates, expert_ids, saved_gate, saved_up, w_gate, w_up, w_down):
    owners = lax.axis_size("expert")
    row_count, feature_dim = cotangent.shape
    top_count = expert_ids.shape[1]
    local_count, _, slot_count = saved_gate.shape
    capacity = slot_count // owners
    flat_ids, slot_pos = route_slots(expert_ids, local_count * owners)
    target = flat_ids % local_count * slot_count + flat_ids // local_count * capacity + slot_pos
    scaled = (gates[:, :, None] * cotangent.astype(jnp.float32)[:, None, :]).astype(jnp.bfloat16)
    scaled = scaled.reshape(row_count * top_count, feature_dim)
    outgoing = (
        jnp.zeros((local_count * slot_count, feature_dim), jnp.bfloat16).at[target].set(scaled)
    )
    outgoing = outgoing.reshape(local_count, slot_count, feature_dim)
    arrived = lax.all_to_all(outgoing, "expert", split_axis=1, concat_axis=1, tiled=True)
    partial_value = expert_step(arrived, saved_gate, saved_up, w_gate, w_up, w_down)
    returned = lax.all_to_all(partial_value, "expert", split_axis=1, concat_axis=1, tiled=True)
    picked = returned.reshape(local_count * slot_count, feature_dim)[target].astype(jnp.float32)
    combined = jnp.sum(picked.reshape(row_count, top_count, feature_dim), axis=1)
    return lax.psum_scatter(combined, "tp", scatter_dimension=0, tiled=True)


CHUNKS = ((0, 2), (1, 3))
TILE = 512


def swap(value, axis, step):
    count = lax.axis_size(axis)
    return lax.ppermute(value, axis, [(i, i ^ step) for i in range(count)])


def along_line(value, shift):
    count = lax.axis_size("expert")
    return lax.ppermute(value, "expert", [(i, (i + 4 * shift) % count) for i in range(count)])


def small(kernel, name, outs, kinds, operands, scratch=(), limit=8, work=0):
    spaces = {"s": pltpu.SMEM, "v": pltpu.VMEM, "h": pltpu.HBM, "o": pl.ANY}
    return pl.pallas_call(
        kernel,
        out_shape=[
            out if hasattr(out, "dtype") else jax.ShapeDtypeStruct(out, jnp.bfloat16) for out in outs
        ],
        in_specs=[pl.BlockSpec(memory_space=spaces[kind]) for kind in kinds],
        scratch_shapes=list(scratch),
        compiler_params=pltpu.CompilerParams(vmem_limit_bytes=limit << 20),
        cost_estimate=pl.CostEstimate(flops=work, bytes_accessed=work >> 8, transcendentals=0),
        name=name,
    )(*operands)


def prepare_kernel(place, tokens, gates_any, ids_any, first, table, gates, ids, sems):
    piece = first.shape[0]
    width = first.shape[1] - table.shape[1]
    near = pl.multiple_of(place[3] * piece, piece)
    copies = [
        pltpu.make_async_copy(gates_any, gates, sems.at[0]),
        pltpu.make_async_copy(ids_any, ids, sems.at[1]),
        pltpu.make_async_copy(
            tokens.at[pl.ds(near, piece), :], first.at[:, pl.ds(0, width)], sems.at[2]
        ),
    ]
    for copy in copies:
        copy.start()
    copies[0].wait()
    copies[1].wait()
    rest = gates[...]
    terms = []
    for _ in range(3):
        term = rest.astype(jnp.bfloat16).astype(jnp.float32)
        terms.append(term)
        rest = rest - term
    terms.append(ids[...].astype(jnp.float32))
    unused = piece - 4 * gates.shape[0]
    terms.append(jnp.zeros((unused, gates.shape[1]), jnp.float32))
    packed = jnp.concatenate(terms, axis=0).astype(jnp.bfloat16)
    first[:, width:] = packed
    table[...] = packed
    copies[2].wait()


def prepare(place, cotangent, gates, ids, piece):
    return small(
        prepare_kernel,
        "prepare",
        [(piece, cotangent.shape[1] + 128), (piece, 128)],
        "shhh",
        (place, cotangent, gates, ids),
        [
            pltpu.VMEM(gates.shape, jnp.float32),
            pltpu.VMEM(ids.shape, jnp.int32),
            pltpu.SemaphoreType.DMA((3,)),
        ],
        limit=4,
    )


def stack_kernel(*refs):
    lines = refs[-1]
    for r in range(lines.shape[0]):
        lines[r] = refs[r][...]


def stack(pieces, *after):
    return small(
        stack_kernel,
        "stack",
        [(len(pieces),) + pieces[0].shape],
        "v" * len(pieces) + "o" * len(after),
        (*pieces, *after),
    )[0]


def relay_kernel(came, part, line, following):
    line[0] = came[...]
    following[...] = part[...]


def relay(came, part):
    return small(
        relay_kernel, "relay", [(1,) + came.shape, part.shape], "vv", (came, part)
    )


def hold_kernel(*refs):
    count = (len(refs) - 1) // 2
    for source, target in zip(refs[:count], refs[count + 1:]):
        target[...] = source[...]


def hold(arrays, after):
    return small(
        hold_kernel, "hold", [array.shape for array in arrays], "v" * len(arrays) + "o", (*arrays, after)
    )


def turn_kernel(gate, up, _, gate_t, up_t):
    tile = 128
    for e in range(gate.shape[0]):
        for at in range(0, gate.shape[2], tile):
            gate_value = gate[e, :, at:at + tile].astype(jnp.float32)
            up_value = up[e, :, at:at + tile].astype(jnp.float32)
            sigmoid_gate = jax.nn.sigmoid(gate_value)
            up_t[e, at:at + tile] = (gate_value * sigmoid_gate).T
            gate_t[e, at:at + tile] = (
                up_value * sigmoid_gate * (1.0 + gate_value * (1.0 - sigmoid_gate))
            ).T


def turn(saved_gate, saved_up, after):
    count, units, slots = saved_gate.shape
    return small(
        turn_kernel,
        "turn",
        [jax.ShapeDtypeStruct((count, slots, units), jnp.float32)] * 2,
        "vvo",
        (saved_gate, saved_up, after),
        limit=16,
    )


def corner_kernel(place, tokens, first, over, side, whole_over, left, right, sem):
    _, piece, middle = left.shape
    far = pl.multiple_of((1 - place[3]) * piece, piece)
    copy = pltpu.make_async_copy(
        tokens.at[pl.ds(far, piece), pl.ds(middle, middle)], right.at[0], sem.at[0]
    )
    copy.start()
    whole_over[0] = first[...]
    whole_over[1:] = over[...]
    left[0] = first[:, :middle]
    left[1:] = over[:, :, :middle]
    right[1:] = side[:, :, middle:2 * middle]
    copy.wait()


def own_corner(place, cotangent, first, over, side):
    count, piece, width = over.shape
    middle = cotangent.shape[1] // 2
    return small(
        corner_kernel,
        "own_corner",
        [(count + 1, piece, width)] + [(count + 1, piece, middle)] * 2,
        "shvvv",
        (place, cotangent, first, over, side),
        (pltpu.SemaphoreType.DMA((1,)),),
    )


def plain_corner_kernel(over, side, _, left, right):
    middle = left.shape[-1]
    left[...] = over[:, :, :middle]
    right[...] = side[:, :, middle:2 * middle]


def corner(over, side, middle, after):
    return small(
        plain_corner_kernel,
        "corner",
        [over.shape[:2] + (middle,)] * 2,
        "vvo",
        (over, side, after),
    )


def join_kernel(left, right, *refs):
    result = refs[-1]
    middle = left.shape[-1]
    result[:, :, :middle] = left[...]
    result[:, :, middle:] = right[...]


def join(left, right, *after, work=0):
    dims = left.shape
    return small(
        join_kernel,
        "join",
        [dims[:-1] + (2 * dims[-1],)],
        "vv" + "o" * len(after),
        (left, right, *after),
        work=work,
    )[0]


def tokens_of(own, lines, r, offsets):
    if r == 0:
        return own[...]
    return lines[r_place(r, offsets)]


def r_place(r, offsets):
    return [offset for offset in offsets if offset != 0].index(r)


def pair_base(place, line_count, r, ry, width):
    line = lax.rem(place[2] + r, line_count)
    row = place[1] if ry == 0 else 1 - place[1]
    return pl.multiple_of((line * 2 + row) * width, width)


def route_kernel(offsets, capacity, place, own, own_c, lines, lines_c, over, over_c, pick, pick_t, gate,
                 hits, gates):
    tokens = pick.shape[2] // 2
    width = over.shape[2] - 128
    core, row, line, half = place[0], place[1], place[2], place[3]
    first = (line * 4 + row * 2 + core) * 2
    for i, r in enumerate(offsets):
        for ry in range(2):
            tables = []
            for c in range(2):
                if ry == 1:
                    table = (over, over_c)[c][i, :32, width:]
                elif r == 0:
                    table = (own, own_c)[c][:32]
                else:
                    table = (lines, lines_c)[c][r_place(r, offsets), :32, width:]
                tables.append(table.astype(jnp.float32))
            swapped = core > 0
            ordered = [
                jnp.where(swapped, tables[1], tables[0]), jnp.where(swapped, tables[0], tables[1])
            ]
            for c in range(2):
                block = ordered[c]
                value = block[0:8] + block[8:16] + block[16:24]
                for e in range(2):
                    named = block[24:32] == (first + e).astype(jnp.float32)
                    at = ((i * 2 + ry) * 2 + c) * 2 + e
                    hits[at:at + 1] = jnp.sum(named.astype(jnp.float32), axis=0, keepdims=True)
                    gates[at:at + 1] = jnp.sum(
                        jnp.where(named, value, 0.0), axis=0, keepdims=True
                    )
    earlier = lax.broadcasted_iota(jnp.int32, (tokens, tokens), 0) < lax.broadcasted_iota(
        jnp.int32, (tokens, tokens), 1
    )
    hit = hits[...]
    slot = jnp.dot(
        hit.astype(jnp.bfloat16),
        earlier.astype(jnp.float32).astype(jnp.bfloat16),
        preferred_element_type=jnp.float32,
    )
    slot = jnp.where(hit > 0.5, slot, -1.0)
    turned = half > 0
    slot = jnp.where(turned, pltpu.roll(slot, tokens // 2, 1), slot)
    weight = jnp.where(turned, pltpu.roll(gates[...], tokens // 2, 1), gates[...])
    order = lax.broadcasted_iota(jnp.int32, (capacity, tokens), 0).astype(jnp.float32)
    for p in range(pick.shape[0]):
        rows = []
        for e in range(2):
            for c in range(2):
                at = (p * 2 + c) * 2 + e
                ones = (order == slot[at:at + 1]).astype(jnp.float32)
                column = jnp.sum(ones * weight[at:at + 1], axis=1, keepdims=True)
                place_in = (e * 2 + c) * capacity
                gate[p, place_in:place_in + capacity] = jnp.broadcast_to(
                    column, (capacity, gate.shape[2])
                )
                own_core = (core == c).astype(jnp.float32)
                rows.append(jnp.concatenate([ones * own_core, ones * (1.0 - own_core)], axis=1))
        matrix = jnp.concatenate(rows, axis=0)
        pick[p] = matrix.astype(jnp.bfloat16)
        count = matrix.shape[0]
        square = jnp.concatenate(
            [matrix, jnp.zeros((2 * tokens - count, 2 * tokens), jnp.float32)], axis=0
        )
        pick_t[p] = square.T[:, :count].astype(jnp.bfloat16)


def route(offsets, place, table, table_c, lines, lines_c, over, over_c, capacity):
    tokens = 2 * over.shape[1]
    pairs = 2 * len(offsets)
    rows = 4 * capacity
    return small(
        functools.partial(route_kernel, offsets, capacity),
        "route",
        [
            (pairs, rows, 2 * tokens),
            (pairs, 2 * tokens, rows),
            jax.ShapeDtypeStruct((pairs, rows, 128), jnp.float32),
        ],
        "s" + "v" * 6,
        (place, table, table_c, lines, lines_c, over, over_c),
        [pltpu.VMEM((4 * pairs, tokens), jnp.float32)] * 2,
    )


def hidden_kernel(offsets, line_count, place, own, own_c, lines, lines_c, side, side_c, over, over_c,
                  diag, diag_c, pick, gate, w_down, saved_gate, saved_up, _, grads, slots):
    piece = over.shape[1]
    width = diag.shape[2]
    rows = pick.shape[1] // 2
    units = w_down.shape[1]
    near = pl.multiple_of(place[3] * piece, piece)
    far = pl.multiple_of((1 - place[3]) * piece, piece)

    @pl.loop(0, width // TILE)
    def _(k):
        at = pl.ds(pl.multiple_of(k * TILE, TILE), TILE)
        for i, r in enumerate(offsets):
            for ry in range(2):
                parts = []
                for c in range(2):
                    if ry == 1:
                        parts += [(over, over_c)[c][i, :, at], (diag, diag_c)[c][i, :, at]]
                    elif r == 0:
                        group = (own, own_c)[c]
                        parts += [group[pl.ds(near, piece), at], group[pl.ds(far, piece), at]]
                    else:
                        j = r_place(r, offsets)
                        parts += [(lines, lines_c)[c][j, :, at], (side, side_c)[c][j, :, at]]
                p = i * 2 + ry
                picked = jnp.dot(
                    pick[p], jnp.concatenate(parts, axis=0), preferred_element_type=jnp.float32
                )
                weight = gate[p]
                weight = jnp.concatenate([weight] * (TILE // weight.shape[1]), axis=1)
                scaled = (picked * weight).astype(jnp.bfloat16)
                slots[0, p * rows:(p + 1) * rows, at] = scaled[:rows]
                slots[1, p * rows:(p + 1) * rows, at] = scaled[rows:]

    for e in range(2):
        total = lax.dot_general(
            slots[e], w_down[e], (((1,), (1,)), ((), ())), preferred_element_type=jnp.float32
        )
        for i, r in enumerate(offsets):
            for ry in range(2):
                p = i * 2 + ry
                mine = slice(p * rows, (p + 1) * rows)
                saved = pl.ds(pair_base(place, line_count, r, ry, rows), rows)
                hidden_grad = total[mine]
                grads[e, mine, units:] = (hidden_grad * saved_up[e, saved, :]).astype(jnp.bfloat16)
                grads[e, mine, :units] = (hidden_grad * saved_gate[e, saved, :]).astype(jnp.bfloat16)


def hidden(offsets, line_count, place, own, own_c, moved, pick, gate, w_down, saved, after):
    width = own.shape[1]
    units = w_down.shape[1]
    count = pick.shape[0] * pick.shape[1] // 2
    return small(
        functools.partial(hidden_kernel, offsets, line_count),
        "hidden",
        [(2, count, 2 * units)],
        "s" + "v" * 15 + "o",
        (place, own, own_c, *moved, pick, gate, w_down, *saved, after),
        [pltpu.VMEM((2, count, width), jnp.bfloat16)],
        limit=12,
    )[0]


def sums_kernel(offset, grads, w_gate, w_up, pick_t, _, keep, send, slots):
    rows = pick_t.shape[2] // 2
    tokens = pick_t.shape[1] // 2

    @pl.loop(0, keep.shape[2] // TILE)
    def _(k):
        at = pl.ds(pl.multiple_of(k * TILE, TILE), TILE)
        source = pl.ds(pl.multiple_of(offset + k * TILE, TILE), TILE)
        for e in range(2):
            weights = jnp.concatenate([w_gate[e, :, source], w_up[e, :, source]], axis=0)
            slots[e] = jnp.dot(grads[e], weights, preferred_element_type=jnp.float32).astype(
                jnp.bfloat16
            )
        for p in range(pick_t.shape[0]):
            mine = slice(p * rows, (p + 1) * rows)
            both = jnp.concatenate([slots[0, mine], slots[1, mine]], axis=0)
            total = jnp.dot(pick_t[p], both, preferred_element_type=jnp.float32).astype(
                jnp.bfloat16
            )
            keep[p, :, at] = total[:tokens]
            send[p, :, at] = total[tokens:]


def sums(offset, width, grads, w_gate, w_up, pick_t, after, work=0):
    pairs, tokens, _ = pick_t.shape
    _, count, units = grads.shape
    return small(
        functools.partial(sums_kernel, offset),
        "sums",
        [(pairs, tokens // 2, width)] * 2,
        "vvvvo",
        (grads, w_gate, w_up, pick_t, after),
        [pltpu.VMEM((2, count, TILE), jnp.bfloat16)],
        limit=8,
        work=work,
    )


def first_left_kernel(keep, came, _, send, kept):
    piece = kept.shape[1]
    kept[...] = keep[:, :piece] + came[:, :piece]
    send[...] = keep[:, piece:] + came[:, piece:]


def first_left(keep, came, after):
    pairs, tokens, width = keep.shape
    return small(
        first_left_kernel,
        "first_left",
        [(pairs, tokens // 2, width)] * 2,
        "vvo",
        (keep, came, after),
    )


def first_right_kernel(keep, came, _, send, kept):
    for i in range(kept.shape[0]):
        kept[i] = keep[2 * i] + came[2 * i]
        send[i] = keep[2 * i + 1] + came[2 * i + 1]


def first_right(keep, came, after):
    pairs, tokens, width = keep.shape
    return small(
        first_right_kernel,
        "first_right",
        [(pairs // 2, tokens, width)] * 2,
        "vvo",
        (keep, came, after),
    )


def second_kernel(keep_l, came_l, keep_r, came_r, _, send_l, left, send_r, right):
    piece = left.shape[1]
    for i in range(left.shape[0]):
        left[i] = keep_l[2 * i] + came_l[2 * i]
        send_l[i] = keep_l[2 * i + 1] + came_l[2 * i + 1]
        right[i] = keep_r[i, :piece] + came_r[i, :piece]
        send_r[i] = keep_r[i, piece:] + came_r[i, piece:]


def second_sum(keep_l, came_l, keep_r, came_r, after):
    lines = keep_r.shape[0]
    _, piece, middle = keep_l.shape
    return small(
        second_kernel,
        "second_sum",
        [(lines, piece, middle)] * 4,
        "vvvvo",
        (keep_l, came_l, keep_r, came_r, after),
        work=1 << 36,
    )


def first_lines_left_kernel(keep, came, _, *outs):
    piece = outs[0].shape[1]
    for i in range(len(outs) // 2):
        for ry in range(2):
            outs[2 * i][ry] = keep[2 * i + ry, piece:] + came[2 * i + ry, piece:]
            outs[2 * i + 1][ry] = keep[2 * i + ry, :piece] + came[2 * i + ry, :piece]


def first_lines_right_kernel(keep, came, _, *outs):
    for i in range(len(outs) // 2):
        outs[2 * i][0] = keep[2 * i + 1] + came[2 * i + 1]
        outs[2 * i + 1][0] = keep[2 * i] + came[2 * i]


def first_lines(kernel, dims, keep, came, after):
    lines = keep.shape[0] // 2
    return small(kernel, "first_lines", [dims] * (2 * lines), "vvo", (keep, came, after))


def second_apart_kernel(keep_l, came_l, keep_r, came_r, _, *outs):
    piece = outs[0].shape[0]
    for i in range(keep_r.shape[0]):
        send_l, left, send_r, right = outs[4 * i:4 * i + 4]
        left[...] = keep_l[2 * i] + came_l[2 * i]
        send_l[...] = keep_l[2 * i + 1] + came_l[2 * i + 1]
        right[...] = keep_r[i, :piece] + came_r[i, :piece]
        send_r[...] = keep_r[i, piece:] + came_r[i, piece:]


def second_apart(keep_l, came_l, keep_r, came_r, after, work=1 << 36):
    lines = keep_r.shape[0]
    _, piece, middle = keep_l.shape
    return small(
        second_apart_kernel,
        "second_sum",
        [(piece, middle)] * (4 * lines),
        "vvvvo",
        (keep_l, came_l, keep_r, came_r, after),
        work=work,
    )


def third_apart_kernel(left, came_l, right, came_r, _, out):
    middle = left.shape[-1]
    for at, one, other in ((slice(0, middle), left, came_l), (slice(middle, None), right, came_r)):
        out[:, at] = (one[...].astype(jnp.float32) + other[...].astype(jnp.float32)).astype(out.dtype)


def third_apart(left, came_l, right, came_r, after, kind=jnp.bfloat16, work=0):
    piece, middle = left.shape
    return small(
        third_apart_kernel,
        "third_sum",
        [jax.ShapeDtypeStruct((piece, 2 * middle), kind)],
        "vvvvo",
        (left, came_l, right, came_r, after),
        work=work,
    )[0]


def third_kernel(left, came_l, right, came_r, _, *outs):
    middle = left.shape[-1]
    for columns, one, other in ((slice(0, middle), left, came_l), (slice(middle, None), right, came_r)):
        for i, out in enumerate(outs):
            out[:, columns] = (one[i].astype(jnp.float32) + other[i].astype(jnp.float32)).astype(
                out.dtype
            )


def third_sum(offsets, left, came_l, right, came_r, after):
    _, piece, middle = left.shape
    return small(
        third_kernel,
        "third_sum",
        [
            jax.ShapeDtypeStruct((piece, 2 * middle), jnp.float32 if r == 0 else jnp.bfloat16)
            for r in offsets
        ],
        "vvvvo",
        (left, came_l, right, came_r, after),
        work=1 << 36,
    )


def last_kernel(*refs):
    total = refs[0][...]
    for ref in refs[1:-1]:
        total = total + ref[...].astype(jnp.float32)
    refs[-1][...] = total


def add_up(terms, name, work=0):
    return small(
        last_kernel,
        name,
        [jax.ShapeDtypeStruct(terms[0].shape, jnp.float32)],
        "v" * len(terms),
        terms,
        work=work,
    )[0]


def tokens_body(cotangent, gates, expert_ids, saved_gate, saved_up, w_gate, w_up, w_down):
    owners = lax.axis_size("expert")
    row_count, feature_dim = cotangent.shape
    capacity = saved_gate.shape[2] // owners
    lines = owners // 4
    piece = row_count // 2
    middle = feature_dim // 2
    me, half = lax.axis_index("expert"), lax.axis_index("tp")
    place = jnp.stack([me % 2, me // 2 % 2, me // 4, half]).astype(jnp.int32)

    part, table = prepare(place, cotangent, gates.T, expert_ids.T, piece)
    first = swap(part, "expert", 2)
    own_c, table_c = swap(cotangent, "expert", 1), swap(table, "expert", 1)
    gathered, saved = [], None

    def compute(index, after):
        offsets, moved = CHUNKS[index], gathered[index]
        line, line_c, _, _, over, over_c = moved[:6]
        pick, pick_t, gate = route(
            offsets, place, table, table_c, line, line_c, over, over_c, capacity
        )
        grads = hidden(
            offsets, lines, place, cotangent, own_c, moved, pick, gate, w_down, saved, after
        )
        return grads, pick_t

    def sums_by_token(offset, grads, pick_t, after, work=0):
        keep, send = sums(offset, middle, grads, w_gate, w_up, pick_t, after, work)
        return [keep, swap(send, "expert", 1)], send

    near = CHUNKS[0][1]
    for offsets in CHUNKS:
        pieces = [along_line(part, -r) for r in offsets if r != 0]
        if saved is None:
            line, part = relay(pieces[0], part)
            saved = turn(saved_gate, saved_up, line)
        else:
            line = stack(pieces, saved[0])
        side, over = swap(line, "tp", 1), swap(line, "expert", 2)
        if offsets[0] == 0:
            over, left, right = own_corner(place, cotangent, first, over, side)
            after = (left,)
        else:
            early = compute(0, line)
            grads, pick_t = early
            early_l, after = sums_by_token(0, grads, pick_t, grads)
            left, right = corner(over, side, middle, after)
            early_r, after = sums_by_token(middle, grads, pick_t, left, 68719476736)
            after = (after,)
        diag = join(swap(left, "tp", 1), swap(right, "expert", 2), *after, work=6074000999)
        moved = []
        for array in (line, side, over, diag):
            moved += [array, swap(array, "expert", 1)]
        gathered.append(moved)

    def first_step(keep_l, came_l, keep_r, came_r, after):
        send_l, keep_l = first_left(keep_l, came_l, after)
        send_r, keep_r = first_right(keep_r, came_r, send_l)
        return keep_l, swap(send_l, "tp", 1), keep_r, swap(send_r, "expert", 2), send_r

    def second_step(keep_l, send_l, keep_r, send_r, after, works, kind=jnp.bfloat16):
        came_l, came_r = swap(send_l, "tp", 1), swap(send_r, "expert", 2)
        send_l, left, send_r, right = second_apart(keep_l, came_l, keep_r, came_r, after, works[0])
        came_l, came_r = swap(send_l, "expert", 2), swap(send_r, "tp", 1)
        return third_apart(left, came_l, right, came_r, send_l, kind, works[1]), send_l

    send_l0, keep_l0, send_l2, keep_l2 = first_lines(
        first_lines_left_kernel, (2, piece, middle), *early_l, gathered[1][6]
    )
    send_r0, keep_r0, send_r2, keep_r2 = first_lines(
        first_lines_right_kernel, (1, 2 * piece, middle), *early_r, send_l2
    )
    grads, pick_t = compute(1, send_r2)
    late_l, after = sums_by_token(0, grads, pick_t, grads)
    late_r, _ = sums_by_token(middle, grads, pick_t, after)
    done, after = second_step(keep_l2, send_l2, keep_r2, send_r2, send_r2, (1 << 36, 1 << 36))
    early = along_line(done, near)
    late = first_step(*late_l, *late_r, after)
    parts = second_apart(*late[:4], done)
    after, total = early, None
    for i, r in enumerate(CHUNKS[1]):
        send_l, left, send_r, right = parts[4 * i:4 * i + 4]
        came_l, came_r = swap(send_l, "expert", 2), swap(send_r, "tp", 1)
        after = third_apart(left, came_l, right, came_r, after)
        came = along_line(after, r)
        if total is None:
            send_l0, send_r0 = hold([send_l0, send_r0], parts[0])
            own, _ = second_step(keep_l0, send_l0, keep_r0, send_r0, send_r0, (0, 0), jnp.float32)
            total = add_up([own, early, came], "middle_sum")
    return add_up([total, came], "last_sum")


def body(*arrays):
    cotangent, gates, _, saved_gate = arrays[:4]
    owners = lax.axis_size("expert")
    fits = (
        owners == 16
        and lax.axis_size("tp") == 2
        and cotangent.shape[0] == 128
        and cotangent.shape[1] % (2 * TILE) == 0
        and gates.shape[1] == 8
        and saved_gate.shape[0] == 2
        and saved_gate.shape[2] // owners % 16 == 0
        and 4 * saved_gate.shape[2] // owners <= 256
    )
    return (tokens_body if fits else slots_body)(*arrays)


def solution(mesh):
    in_specs = (
        P("expert", None),
        P("expert", None),
        P("expert", None),
        P("expert", "tp", None),
        P("expert", "tp", None),
        P("expert", "tp", None),
        P("expert", "tp", None),
        P("expert", "tp", None),
    )
    out_specs = P(("expert", "tp"), None)
    return jax.shard_map(body, mesh=mesh, in_specs=in_specs, out_specs=out_specs, check_vma=False)
```

```python
import functools

import jax
import jax.numpy as jnp
from jax import lax
from jax.experimental import pallas as pl
from jax.experimental.pallas import tpu as pltpu
from jax.sharding import PartitionSpec as P


def route_slots(expert_ids, expert_total):
    flat_ids = expert_ids.reshape(-1)
    one_hot = (flat_ids[:, None] == jnp.arange(expert_total, dtype=jnp.int32)[None, :]).astype(
        jnp.int32
    )
    before = jnp.cumsum(one_hot, axis=0) - one_hot
    return (flat_ids, jnp.sum(before * one_hot, axis=1))


def expert_step(arrived, saved_gate, saved_up, w_gate, w_up, w_down):
    hidden_grad = jnp.einsum("efd,esd->efs", w_down, arrived, preferred_element_type=jnp.float32)
    gate_value = saved_gate.astype(jnp.float32)
    up_value = saved_up.astype(jnp.float32)
    sigmoid_gate = jax.nn.sigmoid(gate_value)
    up_grad = (hidden_grad * gate_value * sigmoid_gate).astype(jnp.bfloat16)
    gate_grad = (
        hidden_grad * up_value * sigmoid_gate * (1.0 + gate_value * (1.0 - sigmoid_gate))
    ).astype(jnp.bfloat16)
    partial_value = jnp.einsum(
        "efs,efd->esd", gate_grad, w_gate, preferred_element_type=jnp.float32
    )
    partial_value = partial_value + jnp.einsum(
        "efs,efd->esd", up_grad, w_up, preferred_element_type=jnp.float32
    )
    return partial_value.astype(jnp.bfloat16)


def slots_body(cotangent, gates, expert_ids, saved_gate, saved_up, w_gate, w_up, w_down):
    owners = lax.axis_size("expert")
    row_count, feature_dim = cotangent.shape
    top_count = expert_ids.shape[1]
    local_count, _, slot_count = saved_gate.shape
    capacity = slot_count // owners
    flat_ids, slot_pos = route_slots(expert_ids, local_count * owners)
    target = flat_ids % local_count * slot_count + flat_ids // local_count * capacity + slot_pos
    scaled = (gates[:, :, None] * cotangent.astype(jnp.float32)[:, None, :]).astype(jnp.bfloat16)
    scaled = scaled.reshape(row_count * top_count, feature_dim)
    outgoing = (
        jnp.zeros((local_count * slot_count, feature_dim), jnp.bfloat16).at[target].set(scaled)
    )
    outgoing = outgoing.reshape(local_count, slot_count, feature_dim)
    arrived = lax.all_to_all(outgoing, "expert", split_axis=1, concat_axis=1, tiled=True)
    partial_value = expert_step(arrived, saved_gate, saved_up, w_gate, w_up, w_down)
    returned = lax.all_to_all(partial_value, "expert", split_axis=1, concat_axis=1, tiled=True)
    picked = returned.reshape(local_count * slot_count, feature_dim)[target].astype(jnp.float32)
    combined = jnp.sum(picked.reshape(row_count, top_count, feature_dim), axis=1)
    return lax.psum_scatter(combined, "tp", scatter_dimension=0, tiled=True)


CHUNKS = ((0, 2), (1, 3))
TILE = 512


def swap(value, axis, step):
    count = lax.axis_size(axis)
    return lax.ppermute(value, axis, [(i, i ^ step) for i in range(count)])


def along_line(value, shift):
    count = lax.axis_size("expert")
    return lax.ppermute(value, "expert", [(i, (i + 4 * shift) % count) for i in range(count)])


def small(kernel, name, outs, kinds, operands, scratch=(), limit=8, work=0):
    spaces = {"s": pltpu.SMEM, "v": pltpu.VMEM, "h": pltpu.HBM, "o": pl.ANY}
    return pl.pallas_call(
        kernel,
        out_shape=[
            out if hasattr(out, "dtype") else jax.ShapeDtypeStruct(out, jnp.bfloat16) for out in outs
        ],
        in_specs=[pl.BlockSpec(memory_space=spaces[kind]) for kind in kinds],
        scratch_shapes=list(scratch),
        compiler_params=pltpu.CompilerParams(vmem_limit_bytes=limit << 20),
        cost_estimate=pl.CostEstimate(flops=work, bytes_accessed=work >> 8, transcendentals=0),
        name=name,
    )(*operands)


def prepare_kernel(place, tokens, gates_any, ids_any, first, table, gates, ids, sems):
    piece = first.shape[0]
    width = first.shape[1] - table.shape[1]
    near = pl.multiple_of(place[3] * piece, piece)
    copies = [
        pltpu.make_async_copy(gates_any, gates, sems.at[0]),
        pltpu.make_async_copy(ids_any, ids, sems.at[1]),
        pltpu.make_async_copy(
            tokens.at[pl.ds(near, piece), :], first.at[:, pl.ds(0, width)], sems.at[2]
        ),
    ]
    for copy in copies:
        copy.start()
    copies[0].wait()
    copies[1].wait()
    rest = gates[...]
    terms = []
    for _ in range(3):
        term = rest.astype(jnp.bfloat16).astype(jnp.float32)
        terms.append(term)
        rest = rest - term
    terms.append(ids[...].astype(jnp.float32))
    unused = piece - 4 * gates.shape[0]
    terms.append(jnp.zeros((unused, gates.shape[1]), jnp.float32))
    packed = jnp.concatenate(terms, axis=0).astype(jnp.bfloat16)
    first[:, width:] = packed
    table[...] = packed
    copies[2].wait()


def prepare(place, cotangent, gates, ids, piece):
    return small(
        prepare_kernel,
        "prepare",
        [(piece, cotangent.shape[1] + 128), (piece, 128)],
        "shhh",
        (place, cotangent, gates, ids),
        [
            pltpu.VMEM(gates.shape, jnp.float32),
            pltpu.VMEM(ids.shape, jnp.int32),
            pltpu.SemaphoreType.DMA((3,)),
        ],
        limit=4,
    )


def stack_kernel(*refs):
    lines = refs[-1]
    for r in range(lines.shape[0]):
        lines[r] = refs[r][...]


def stack(pieces, *after):
    return small(
        stack_kernel,
        "stack",
        [(len(pieces),) + pieces[0].shape],
        "v" * len(pieces) + "o" * len(after),
        (*pieces, *after),
    )[0]


def relay_kernel(came, part, line, following):
    line[0] = came[...]
    following[...] = part[...]


def relay(came, part):
    return small(
        relay_kernel, "relay", [(1,) + came.shape, part.shape], "vv", (came, part)
    )


def hold_kernel(*refs):
    count = (len(refs) - 1) // 2
    for source, target in zip(refs[:count], refs[count + 1:]):
        target[...] = source[...]


def hold(arrays, after):
    return small(
        hold_kernel, "hold", [array.shape for array in arrays], "v" * len(arrays) + "o", (*arrays, after)
    )


def turn_kernel(gate, up, _, gate_t, up_t):
    tile = 128
    for e in range(gate.shape[0]):
        for at in range(0, gate.shape[2], tile):
            gate_value = gate[e, :, at:at + tile].astype(jnp.float32)
            up_value = up[e, :, at:at + tile].astype(jnp.float32)
            sigmoid_gate = jax.nn.sigmoid(gate_value)
            up_t[e, at:at + tile] = (gate_value * sigmoid_gate).T
            gate_t[e, at:at + tile] = (
                up_value * sigmoid_gate * (1.0 + gate_value * (1.0 - sigmoid_gate))
            ).T


def turn(saved_gate, saved_up, after):
    count, units, slots = saved_gate.shape
    return small(
        turn_kernel,
        "turn",
        [jax.ShapeDtypeStruct((count, slots, units), jnp.float32)] * 2,
        "vvo",
        (saved_gate, saved_up, after),
        limit=16,
    )


def corner_kernel(place, tokens, first, over, side, whole_over, left, right, sem):
    _, piece, middle = left.shape
    far = pl.multiple_of((1 - place[3]) * piece, piece)
    copy = pltpu.make_async_copy(
        tokens.at[pl.ds(far, piece), pl.ds(middle, middle)], right.at[0], sem.at[0]
    )
    copy.start()
    whole_over[0] = first[...]
    whole_over[1:] = over[...]
    left[0] = first[:, :middle]
    left[1:] = over[:, :, :middle]
    right[1:] = side[:, :, middle:2 * middle]
    copy.wait()


def own_corner(place, cotangent, first, over, side):
    count, piece, width = over.shape
    middle = cotangent.shape[1] // 2
    return small(
        corner_kernel,
        "own_corner",
        [(count + 1, piece, width)] + [(count + 1, piece, middle)] * 2,
        "shvvv",
        (place, cotangent, first, over, side),
        (pltpu.SemaphoreType.DMA((1,)),),
    )


def plain_corner_kernel(over, side, _, left, right):
    middle = left.shape[-1]
    left[...] = over[:, :, :middle]
    right[...] = side[:, :, middle:2 * middle]


def corner(over, side, middle, after):
    return small(
        plain_corner_kernel,
        "corner",
        [over.shape[:2] + (middle,)] * 2,
        "vvo",
        (over, side, after),
    )


def join_kernel(left, right, *refs):
    result = refs[-1]
    middle = left.shape[-1]
    result[:, :, :middle] = left[...]
    result[:, :, middle:] = right[...]


def join(left, right, *after, work=0):
    dims = left.shape
    return small(
        join_kernel,
        "join",
        [dims[:-1] + (2 * dims[-1],)],
        "vv" + "o" * len(after),
        (left, right, *after),
        work=work,
    )[0]


def tokens_of(own, lines, r, offsets):
    if r == 0:
        return own[...]
    return lines[r_place(r, offsets)]


def r_place(r, offsets):
    return [offset for offset in offsets if offset != 0].index(r)


def pair_base(place, line_count, r, ry, width):
    line = lax.rem(place[2] + r, line_count)
    row = place[1] if ry == 0 else 1 - place[1]
    return pl.multiple_of((line * 2 + row) * width, width)


def route_kernel(offsets, capacity, place, own, own_c, lines, lines_c, over, over_c, pick, pick_t, gate,
                 hits, gates):
    tokens = pick.shape[2] // 2
    width = over.shape[2] - 128
    core, row, line, half = place[0], place[1], place[2], place[3]
    first = (line * 4 + row * 2 + core) * 2
    for i, r in enumerate(offsets):
        for ry in range(2):
            tables = []
            for c in range(2):
                if ry == 1:
                    table = (over, over_c)[c][i, :32, width:]
                elif r == 0:
                    table = (own, own_c)[c][:32]
                else:
                    table = (lines, lines_c)[c][r_place(r, offsets), :32, width:]
                tables.append(table.astype(jnp.float32))
            swapped = core > 0
            ordered = [
                jnp.where(swapped, tables[1], tables[0]), jnp.where(swapped, tables[0], tables[1])
            ]
            for c in range(2):
                block = ordered[c]
                value = block[0:8] + block[8:16] + block[16:24]
                for e in range(2):
                    named = block[24:32] == (first + e).astype(jnp.float32)
                    at = ((i * 2 + ry) * 2 + c) * 2 + e
                    hits[at:at + 1] = jnp.sum(named.astype(jnp.float32), axis=0, keepdims=True)
                    gates[at:at + 1] = jnp.sum(
                        jnp.where(named, value, 0.0), axis=0, keepdims=True
                    )
    earlier = lax.broadcasted_iota(jnp.int32, (tokens, tokens), 0) < lax.broadcasted_iota(
        jnp.int32, (tokens, tokens), 1
    )
    hit = hits[...]
    slot = jnp.dot(
        hit.astype(jnp.bfloat16),
        earlier.astype(jnp.float32).astype(jnp.bfloat16),
        preferred_element_type=jnp.float32,
    )
    slot = jnp.where(hit > 0.5, slot, -1.0)
    turned = half > 0
    slot = jnp.where(turned, pltpu.roll(slot, tokens // 2, 1), slot)
    weight = jnp.where(turned, pltpu.roll(gates[...], tokens // 2, 1), gates[...])
    order = lax.broadcasted_iota(jnp.int32, (capacity, tokens), 0).astype(jnp.float32)
    for p in range(pick.shape[0]):
        rows = []
        for e in range(2):
            for c in range(2):
                at = (p * 2 + c) * 2 + e
                ones = (order == slot[at:at + 1]).astype(jnp.float32)
                column = jnp.sum(ones * weight[at:at + 1], axis=1, keepdims=True)
                place_in = (e * 2 + c) * capacity
                gate[p, place_in:place_in + capacity] = jnp.broadcast_to(
                    column, (capacity, gate.shape[2])
                )
                own_core = (core == c).astype(jnp.float32)
                rows.append(jnp.concatenate([ones * own_core, ones * (1.0 - own_core)], axis=1))
        matrix = jnp.concatenate(rows, axis=0)
        pick[p] = matrix.astype(jnp.bfloat16)
        count = matrix.shape[0]
        square = jnp.concatenate(
            [matrix, jnp.zeros((2 * tokens - count, 2 * tokens), jnp.float32)], axis=0
        )
        pick_t[p] = square.T[:, :count].astype(jnp.bfloat16)


def route(offsets, place, table, table_c, lines, lines_c, over, over_c, capacity):
    tokens = 2 * over.shape[1]
    pairs = 2 * len(offsets)
    rows = 4 * capacity
    return small(
        functools.partial(route_kernel, offsets, capacity),
        "route",
        [
            (pairs, rows, 2 * tokens),
            (pairs, 2 * tokens, rows),
            jax.ShapeDtypeStruct((pairs, rows, 128), jnp.float32),
        ],
        "s" + "v" * 6,
        (place, table, table_c, lines, lines_c, over, over_c),
        [pltpu.VMEM((4 * pairs, tokens), jnp.float32)] * 2,
    )


def hidden_kernel(offsets, line_count, place, own, own_c, lines, lines_c, side, side_c, over, over_c,
                  diag, diag_c, pick, gate, w_down, saved_gate, saved_up, _, grads, slots):
    piece = over.shape[1]
    width = diag.shape[2]
    rows = pick.shape[1] // 2
    units = w_down.shape[1]
    near = pl.multiple_of(place[3] * piece, piece)
    far = pl.multiple_of((1 - place[3]) * piece, piece)

    @pl.loop(0, width // TILE)
    def _(k):
        at = pl.ds(pl.multiple_of(k * TILE, TILE), TILE)
        for i, r in enumerate(offsets):
            for ry in range(2):
                parts = []
                for c in range(2):
                    if ry == 1:
                        parts += [(over, over_c)[c][i, :, at], (diag, diag_c)[c][i, :, at]]
                    elif r == 0:
                        group = (own, own_c)[c]
                        parts += [group[pl.ds(near, piece), at], group[pl.ds(far, piece), at]]
                    else:
                        j = r_place(r, offsets)
                        parts += [(lines, lines_c)[c][j, :, at], (side, side_c)[c][j, :, at]]
                p = i * 2 + ry
                picked = jnp.dot(
                    pick[p], jnp.concatenate(parts, axis=0), preferred_element_type=jnp.float32
                )
                weight = gate[p]
                weight = jnp.concatenate([weight] * (TILE // weight.shape[1]), axis=1)
                scaled = (picked * weight).astype(jnp.bfloat16)
                slots[0, p * rows:(p + 1) * rows, at] = scaled[:rows]
                slots[1, p * rows:(p + 1) * rows, at] = scaled[rows:]

    for e in range(2):
        total = lax.dot_general(
            slots[e], w_down[e], (((1,), (1,)), ((), ())), preferred_element_type=jnp.float32
        )
        for i, r in enumerate(offsets):
            for ry in range(2):
                p = i * 2 + ry
                mine = slice(p * rows, (p + 1) * rows)
                saved = pl.ds(pair_base(place, line_count, r, ry, rows), rows)
                hidden_grad = total[mine]
                grads[e, mine, units:] = (hidden_grad * saved_up[e, saved, :]).astype(jnp.bfloat16)
                grads[e, mine, :units] = (hidden_grad * saved_gate[e, saved, :]).astype(jnp.bfloat16)


def hidden(offsets, line_count, place, own, own_c, moved, pick, gate, w_down, saved, after):
    width = own.shape[1]
    units = w_down.shape[1]
    count = pick.shape[0] * pick.shape[1] // 2
    return small(
        functools.partial(hidden_kernel, offsets, line_count),
        "hidden",
        [(2, count, 2 * units)],
        "s" + "v" * 15 + "o",
        (place, own, own_c, *moved, pick, gate, w_down, *saved, after),
        [pltpu.VMEM((2, count, width), jnp.bfloat16)],
        limit=12,
    )[0]


def sums_kernel(offset, grads, w_gate, w_up, pick_t, _, keep, send, slots):
    rows = pick_t.shape[2] // 2
    tokens = pick_t.shape[1] // 2

    @pl.loop(0, keep.shape[2] // TILE)
    def _(k):
        at = pl.ds(pl.multiple_of(k * TILE, TILE), TILE)
        source = pl.ds(pl.multiple_of(offset + k * TILE, TILE), TILE)
        for e in range(2):
            weights = jnp.concatenate([w_gate[e, :, source], w_up[e, :, source]], axis=0)
            slots[e] = jnp.dot(grads[e], weights, preferred_element_type=jnp.float32).astype(
                jnp.bfloat16
            )
        for p in range(pick_t.shape[0]):
            mine = slice(p * rows, (p + 1) * rows)
            both = jnp.concatenate([slots[0, mine], slots[1, mine]], axis=0)
            total = jnp.dot(pick_t[p], both, preferred_element_type=jnp.float32).astype(
                jnp.bfloat16
            )
            keep[p, :, at] = total[:tokens]
            send[p, :, at] = total[tokens:]


def sums(offset, width, grads, w_gate, w_up, pick_t, after, work=0):
    pairs, tokens, _ = pick_t.shape
    _, count, units = grads.shape
    return small(
        functools.partial(sums_kernel, offset),
        "sums",
        [(pairs, tokens // 2, width)] * 2,
        "vvvvo",
        (grads, w_gate, w_up, pick_t, after),
        [pltpu.VMEM((2, count, TILE), jnp.bfloat16)],
        limit=8,
        work=work,
    )


def first_left_kernel(keep, came, _, send, kept):
    piece = kept.shape[1]
    kept[...] = keep[:, :piece] + came[:, :piece]
    send[...] = keep[:, piece:] + came[:, piece:]


def first_left(keep, came, after):
    pairs, tokens, width = keep.shape
    return small(
        first_left_kernel,
        "first_left",
        [(pairs, tokens // 2, width)] * 2,
        "vvo",
        (keep, came, after),
    )


def first_right_kernel(keep, came, _, send, kept):
    for i in range(kept.shape[0]):
        kept[i] = keep[2 * i] + came[2 * i]
        send[i] = keep[2 * i + 1] + came[2 * i + 1]


def first_right(keep, came, after):
    pairs, tokens, width = keep.shape
    return small(
        first_right_kernel,
        "first_right",
        [(pairs // 2, tokens, width)] * 2,
        "vvo",
        (keep, came, after),
    )


def second_apart_kernel(keep_l, came_l, keep_r, came_r, _, *outs):
    piece = outs[0].shape[0]
    for i in range(keep_r.shape[0]):
        send_l, left, send_r, right = outs[4 * i:4 * i + 4]
        left[...] = keep_l[2 * i] + came_l[2 * i]
        send_l[...] = keep_l[2 * i + 1] + came_l[2 * i + 1]
        right[...] = keep_r[i, :piece] + came_r[i, :piece]
        send_r[...] = keep_r[i, piece:] + came_r[i, piece:]


def second_apart(keep_l, came_l, keep_r, came_r, after):
    lines = keep_r.shape[0]
    _, piece, middle = keep_l.shape
    return small(
        second_apart_kernel,
        "second_sum",
        [(piece, middle)] * (4 * lines),
        "vvvvo",
        (keep_l, came_l, keep_r, came_r, after),
        work=1 << 36,
    )


def third_apart_kernel(left, came_l, right, came_r, _, out):
    middle = left.shape[-1]
    for at, one, other in ((slice(0, middle), left, came_l), (slice(middle, None), right, came_r)):
        out[:, at] = (one[...].astype(jnp.float32) + other[...].astype(jnp.float32)).astype(out.dtype)


def third_apart(left, came_l, right, came_r, after, kind=jnp.bfloat16, work=0):
    piece, middle = left.shape
    return small(
        third_apart_kernel,
        "third_sum",
        [jax.ShapeDtypeStruct((piece, 2 * middle), kind)],
        "vvvvo",
        (left, came_l, right, came_r, after),
        work=work,
    )[0]


def last_kernel(*refs):
    total = refs[0][...].astype(jnp.float32)
    for ref in refs[1:-1]:
        total = total + ref[...].astype(jnp.float32)
    refs[-1][...] = total


def add_up(terms, name, work=0):
    return small(
        last_kernel,
        name,
        [jax.ShapeDtypeStruct(terms[0].shape, jnp.float32)],
        "v" * len(terms),
        terms,
        work=work,
    )[0]


def tokens_body(cotangent, gates, expert_ids, saved_gate, saved_up, w_gate, w_up, w_down):
    owners = lax.axis_size("expert")
    row_count, feature_dim = cotangent.shape
    capacity = saved_gate.shape[2] // owners
    lines = owners // 4
    piece = row_count // 2
    middle = feature_dim // 2
    me, half = lax.axis_index("expert"), lax.axis_index("tp")
    place = jnp.stack([me % 2, me // 2 % 2, me // 4, half]).astype(jnp.int32)

    part, table = prepare(place, cotangent, gates.T, expert_ids.T, piece)
    first = swap(part, "expert", 2)
    own_c, table_c = swap(cotangent, "expert", 1), swap(table, "expert", 1)
    gathered, saved = [], None

    def compute(index, after):
        offsets, moved = CHUNKS[index], gathered[index]
        line, line_c, _, _, over, over_c = moved[:6]
        pick, pick_t, gate = route(
            offsets, place, table, table_c, line, line_c, over, over_c, capacity
        )
        grads = hidden(
            offsets, lines, place, cotangent, own_c, moved, pick, gate, w_down, saved, after
        )
        return grads, pick_t

    def sums_by_token(offset, grads, pick_t, after, work=0):
        keep, send = sums(offset, middle, grads, w_gate, w_up, pick_t, after, work)
        return [keep, swap(send, "expert", 1)], send

    for offsets in CHUNKS:
        pieces = [along_line(part, -r) for r in offsets if r != 0]
        if saved is None:
            line, part = relay(pieces[0], part)
            saved = turn(saved_gate, saved_up, line)
        else:
            line = stack(pieces, saved[0])
        side, over = swap(line, "tp", 1), swap(line, "expert", 2)
        if offsets[0] == 0:
            over, left, right = own_corner(place, cotangent, first, over, side)
            after = (left,)
        else:
            early = compute(0, line)
            grads, pick_t = early
            early_l, after = sums_by_token(0, grads, pick_t, grads)
            left, right = corner(over, side, middle, after)
            early_r, after = sums_by_token(middle, grads, pick_t, left, 68719476736)
            after = (after,)
        diag = join(swap(left, "tp", 1), swap(right, "expert", 2), *after, work=8589934592)
        moved = []
        for array in (line, side, over, diag):
            moved += [array, swap(array, "expert", 1)]
        gathered.append(moved)

    def first_step(keep_l, came_l, keep_r, came_r, after):
        send_l, keep_l = first_left(keep_l, came_l, after)
        send_r, keep_r = first_right(keep_r, came_r, send_l)
        return keep_l, swap(send_l, "tp", 1), keep_r, swap(send_r, "expert", 2), send_r

    def across(send_l, left, send_r, right, after, kind=jnp.bfloat16, work=0):
        came_l, came_r = swap(send_l, "expert", 2), swap(send_r, "tp", 1)
        return third_apart(left, came_l, right, came_r, after, kind, work)

    early = first_step(*early_l, *early_r, gathered[1][6])
    grads, pick_t = compute(1, early[4])
    late_l, after = sums_by_token(0, grads, pick_t, grads)
    late_r, _ = sums_by_token(middle, grads, pick_t, after)
    parts = second_apart(*early[:4], early[4])
    (send_l, left, send_r, right), out = parts[:4], parts[4:]
    done = across(*out, out[0], work=1 << 36)
    early, after = along_line(done, CHUNKS[0][1]), out[0]
    late = first_step(*late_l, *late_r, after)
    parts = second_apart(*late[:4], done)
    after, total = early, None
    for i, r in enumerate(CHUNKS[1]):
        after = across(*parts[4 * i:4 * i + 4], after)
        came = along_line(after, r)
        if total is None:
            total = add_up([early, came], "middle_sum")
    send_l, send_r = hold([send_l, send_r], after)
    own = across(send_l, left, send_r, right, after, jnp.float32)
    return add_up([total, own, came], "last_sum")


def body(*arrays):
    cotangent, gates, _, saved_gate = arrays[:4]
    owners = lax.axis_size("expert")
    fits = (
        owners == 16
        and lax.axis_size("tp") == 2
        and cotangent.shape[0] == 128
        and cotangent.shape[1] % (2 * TILE) == 0
        and gates.shape[1] == 8
        and saved_gate.shape[0] == 2
        and saved_gate.shape[2] // owners % 16 == 0
        and 4 * saved_gate.shape[2] // owners <= 256
    )
    return (tokens_body if fits else slots_body)(*arrays)


def solution(mesh):
    in_specs = (
        P("expert", None),
        P("expert", None),
        P("expert", None),
        P("expert", "tp", None),
        P("expert", "tp", None),
        P("expert", "tp", None),
        P("expert", "tp", None),
        P("expert", "tp", None),
    )
    out_specs = P(("expert", "tp"), None)
    return jax.shard_map(body, mesh=mesh, in_specs=in_specs, out_specs=out_specs, check_vma=False)
```

```python
import functools

import jax
import jax.numpy as jnp
from jax import lax
from jax.experimental import pallas as pl
from jax.experimental.pallas import tpu as pltpu
from jax.sharding import PartitionSpec as P


def route_slots(expert_ids, expert_total):
    flat_ids = expert_ids.reshape(-1)
    one_hot = (flat_ids[:, None] == jnp.arange(expert_total, dtype=jnp.int32)[None, :]).astype(
        jnp.int32
    )
    before = jnp.cumsum(one_hot, axis=0) - one_hot
    return (flat_ids, jnp.sum(before * one_hot, axis=1))


def expert_step(arrived, saved_gate, saved_up, w_gate, w_up, w_down):
    hidden_grad = jnp.einsum("efd,esd->efs", w_down, arrived, preferred_element_type=jnp.float32)
    gate_value = saved_gate.astype(jnp.float32)
    up_value = saved_up.astype(jnp.float32)
    sigmoid_gate = jax.nn.sigmoid(gate_value)
    up_grad = (hidden_grad * gate_value * sigmoid_gate).astype(jnp.bfloat16)
    gate_grad = (
        hidden_grad * up_value * sigmoid_gate * (1.0 + gate_value * (1.0 - sigmoid_gate))
    ).astype(jnp.bfloat16)
    partial_value = jnp.einsum(
        "efs,efd->esd", gate_grad, w_gate, preferred_element_type=jnp.float32
    )
    partial_value = partial_value + jnp.einsum(
        "efs,efd->esd", up_grad, w_up, preferred_element_type=jnp.float32
    )
    return partial_value.astype(jnp.bfloat16)


def slots_body(cotangent, gates, expert_ids, saved_gate, saved_up, w_gate, w_up, w_down):
    owners = lax.axis_size("expert")
    row_count, feature_dim = cotangent.shape
    top_count = expert_ids.shape[1]
    local_count, _, slot_count = saved_gate.shape
    capacity = slot_count // owners
    flat_ids, slot_pos = route_slots(expert_ids, local_count * owners)
    target = flat_ids % local_count * slot_count + flat_ids // local_count * capacity + slot_pos
    scaled = (gates[:, :, None] * cotangent.astype(jnp.float32)[:, None, :]).astype(jnp.bfloat16)
    scaled = scaled.reshape(row_count * top_count, feature_dim)
    outgoing = (
        jnp.zeros((local_count * slot_count, feature_dim), jnp.bfloat16).at[target].set(scaled)
    )
    outgoing = outgoing.reshape(local_count, slot_count, feature_dim)
    arrived = lax.all_to_all(outgoing, "expert", split_axis=1, concat_axis=1, tiled=True)
    partial_value = expert_step(arrived, saved_gate, saved_up, w_gate, w_up, w_down)
    returned = lax.all_to_all(partial_value, "expert", split_axis=1, concat_axis=1, tiled=True)
    picked = returned.reshape(local_count * slot_count, feature_dim)[target].astype(jnp.float32)
    combined = jnp.sum(picked.reshape(row_count, top_count, feature_dim), axis=1)
    return lax.psum_scatter(combined, "tp", scatter_dimension=0, tiled=True)


CHUNKS = ((0, 2), (1, 3))
TILE = 512


def swap(value, axis, step):
    count = lax.axis_size(axis)
    return lax.ppermute(value, axis, [(i, i ^ step) for i in range(count)])


def along_line(value, shift):
    count = lax.axis_size("expert")
    return lax.ppermute(value, "expert", [(i, (i + 4 * shift) % count) for i in range(count)])


def small(kernel, name, outs, kinds, operands, scratch=(), limit=8, work=0):
    spaces = {"s": pltpu.SMEM, "v": pltpu.VMEM, "h": pltpu.HBM, "o": pl.ANY}
    return pl.pallas_call(
        kernel,
        out_shape=[
            out if hasattr(out, "dtype") else jax.ShapeDtypeStruct(out, jnp.bfloat16) for out in outs
        ],
        in_specs=[pl.BlockSpec(memory_space=spaces[kind]) for kind in kinds],
        scratch_shapes=list(scratch),
        compiler_params=pltpu.CompilerParams(vmem_limit_bytes=limit << 20),
        cost_estimate=pl.CostEstimate(flops=work, bytes_accessed=work >> 8, transcendentals=0),
        name=name,
    )(*operands)


def prepare_kernel(place, tokens, routing_any, first, table, routing, sems):
    piece = first.shape[0]
    width = first.shape[1] - table.shape[1]
    near = pl.multiple_of(place[3] * piece, piece)
    copies = [
        pltpu.make_async_copy(routing_any, routing, sems.at[0]),
        pltpu.make_async_copy(
            tokens.at[pl.ds(near, piece), :], first.at[:, pl.ds(0, width)], sems.at[1]
        ),
    ]
    for copy in copies:
        copy.start()
    copies[0].wait()
    count = routing.shape[0] // 2
    rest = routing[:count]
    terms = []
    for _ in range(3):
        term = rest.astype(jnp.bfloat16).astype(jnp.float32)
        terms.append(term)
        rest = rest - term
    terms.append(routing[count:])
    unused = piece - 4 * count
    terms.append(jnp.zeros((unused, routing.shape[1]), jnp.float32))
    packed = jnp.concatenate(terms, axis=0).astype(jnp.bfloat16)
    first[:, width:] = packed
    table[...] = packed
    copies[1].wait()


def prepare(place, cotangent, routing, piece):
    return small(
        prepare_kernel,
        "prepare",
        [(piece, cotangent.shape[1] + 128), (piece, 128)],
        "shh",
        (place, cotangent, routing),
        [pltpu.VMEM(routing.shape, jnp.float32), pltpu.SemaphoreType.DMA((2,))],
        limit=4,
    )


def stack_kernel(*refs):
    lines = refs[-1]
    for r in range(lines.shape[0]):
        lines[r] = refs[r][...]


def stack(pieces, *after):
    return small(
        stack_kernel,
        "stack",
        [(len(pieces),) + pieces[0].shape],
        "v" * len(pieces) + "o" * len(after),
        (*pieces, *after),
    )[0]


def relay_kernel(came, part, line, following):
    line[0] = came[...]
    following[...] = part[...]


def relay(came, part):
    return small(
        relay_kernel, "relay", [(1,) + came.shape, part.shape], "vv", (came, part)
    )


def hold_kernel(*refs):
    count = (len(refs) - 1) // 2
    for source, target in zip(refs[:count], refs[count + 1:]):
        target[...] = source[...]


def hold(arrays, after):
    return small(
        hold_kernel, "hold", [array.shape for array in arrays], "v" * len(arrays) + "o", (*arrays, after)
    )


def turn_kernel(gate, up, _, gate_t, up_t):
    tile = 128
    for e in range(gate.shape[0]):
        for at in range(0, gate.shape[2], tile):
            gate_value = gate[e, :, at:at + tile].astype(jnp.float32)
            up_value = up[e, :, at:at + tile].astype(jnp.float32)
            sigmoid_gate = jax.nn.sigmoid(gate_value)
            up_t[e, at:at + tile] = (gate_value * sigmoid_gate).T
            gate_t[e, at:at + tile] = (
                up_value * sigmoid_gate * (1.0 + gate_value * (1.0 - sigmoid_gate))
            ).T


def turn(saved_gate, saved_up, after):
    count, units, slots = saved_gate.shape
    return small(
        turn_kernel,
        "turn",
        [jax.ShapeDtypeStruct((count, slots, units), jnp.float32)] * 2,
        "vvo",
        (saved_gate, saved_up, after),
        limit=16,
    )


def corner_kernel(place, tokens, first, over, side, whole_over, left, right, sem):
    _, piece, middle = left.shape
    far = pl.multiple_of((1 - place[3]) * piece, piece)
    copy = pltpu.make_async_copy(
        tokens.at[pl.ds(far, piece), pl.ds(middle, middle)], right.at[0], sem.at[0]
    )
    copy.start()
    whole_over[0] = first[...]
    whole_over[1:] = over[...]
    left[0] = first[:, :middle]
    left[1:] = over[:, :, :middle]
    right[1:] = side[:, :, middle:2 * middle]
    copy.wait()


def own_corner(place, cotangent, first, over, side):
    count, piece, width = over.shape
    middle = cotangent.shape[1] // 2
    return small(
        corner_kernel,
        "own_corner",
        [(count + 1, piece, width)] + [(count + 1, piece, middle)] * 2,
        "shvvv",
        (place, cotangent, first, over, side),
        (pltpu.SemaphoreType.DMA((1,)),),
    )


def plain_corner_kernel(over, side, _, left, right):
    middle = left.shape[-1]
    left[...] = over[:, :, :middle]
    right[...] = side[:, :, middle:2 * middle]


def corner(over, side, middle, after):
    return small(
        plain_corner_kernel,
        "corner",
        [over.shape[:2] + (middle,)] * 2,
        "vvo",
        (over, side, after),
    )


def join_kernel(left, right, *refs):
    result = refs[-1]
    middle = left.shape[-1]
    result[:, :, :middle] = left[...]
    result[:, :, middle:] = right[...]


def join(left, right, *after, work=0):
    dims = left.shape
    return small(
        join_kernel,
        "join",
        [dims[:-1] + (2 * dims[-1],)],
        "vv" + "o" * len(after),
        (left, right, *after),
        work=work,
    )[0]


def tokens_of(own, lines, r, offsets):
    if r == 0:
        return own[...]
    return lines[r_place(r, offsets)]


def r_place(r, offsets):
    return [offset for offset in offsets if offset != 0].index(r)


def pair_base(place, line_count, r, ry, width):
    line = lax.rem(place[2] + r, line_count)
    row = place[1] if ry == 0 else 1 - place[1]
    return pl.multiple_of((line * 2 + row) * width, width)


def route_kernel(offsets, capacity, place, own, own_c, lines, lines_c, over, over_c, pick, pick_t, gate,
                 hits, gates):
    tokens = pick.shape[2] // 2
    width = over.shape[2] - 128
    core, row, line, half = place[0], place[1], place[2], place[3]
    first = (line * 4 + row * 2 + core) * 2
    for i, r in enumerate(offsets):
        for ry in range(2):
            tables = []
            for c in range(2):
                if ry == 1:
                    table = (over, over_c)[c][i, :32, width:]
                elif r == 0:
                    table = (own, own_c)[c][:32]
                else:
                    table = (lines, lines_c)[c][r_place(r, offsets), :32, width:]
                tables.append(table.astype(jnp.float32))
            swapped = core > 0
            ordered = [
                jnp.where(swapped, tables[1], tables[0]), jnp.where(swapped, tables[0], tables[1])
            ]
            for c in range(2):
                block = ordered[c]
                value = block[0:8] + block[8:16] + block[16:24]
                for e in range(2):
                    named = block[24:32] == (first + e).astype(jnp.float32)
                    at = ((i * 2 + ry) * 2 + c) * 2 + e
                    hits[at:at + 1] = jnp.sum(named.astype(jnp.float32), axis=0, keepdims=True)
                    gates[at:at + 1] = jnp.sum(
                        jnp.where(named, value, 0.0), axis=0, keepdims=True
                    )
    earlier = lax.broadcasted_iota(jnp.int32, (tokens, tokens), 0) < lax.broadcasted_iota(
        jnp.int32, (tokens, tokens), 1
    )
    hit = hits[...]
    slot = jnp.dot(
        hit.astype(jnp.bfloat16),
        earlier.astype(jnp.float32).astype(jnp.bfloat16),
        preferred_element_type=jnp.float32,
    )
    slot = jnp.where(hit > 0.5, slot, -1.0)
    turned = half > 0
    slot = jnp.where(turned, pltpu.roll(slot, tokens // 2, 1), slot)
    weight = jnp.where(turned, pltpu.roll(gates[...], tokens // 2, 1), gates[...])
    order = lax.broadcasted_iota(jnp.int32, (capacity, tokens), 0).astype(jnp.float32)
    for p in range(pick.shape[0]):
        rows = []
        for e in range(2):
            for c in range(2):
                at = (p * 2 + c) * 2 + e
                ones = (order == slot[at:at + 1]).astype(jnp.float32)
                column = jnp.sum(ones * weight[at:at + 1], axis=1, keepdims=True)
                place_in = (e * 2 + c) * capacity
                gate[p, place_in:place_in + capacity] = jnp.broadcast_to(
                    column, (capacity, gate.shape[2])
                )
                own_core = (core == c).astype(jnp.float32)
                rows.append(jnp.concatenate([ones * own_core, ones * (1.0 - own_core)], axis=1))
        matrix = jnp.concatenate(rows, axis=0)
        pick[p] = matrix.astype(jnp.bfloat16)
        count = matrix.shape[0]
        square = jnp.concatenate(
            [matrix, jnp.zeros((2 * tokens - count, 2 * tokens), jnp.float32)], axis=0
        )
        pick_t[p] = square.T[:, :count].astype(jnp.bfloat16)


def route(offsets, place, table, table_c, lines, lines_c, over, over_c, capacity):
    tokens = 2 * over.shape[1]
    pairs = 2 * len(offsets)
    rows = 4 * capacity
    return small(
        functools.partial(route_kernel, offsets, capacity),
        "route",
        [
            (pairs, rows, 2 * tokens),
            (pairs, 2 * tokens, rows),
            jax.ShapeDtypeStruct((pairs, rows, 128), jnp.float32),
        ],
        "s" + "v" * 6,
        (place, table, table_c, lines, lines_c, over, over_c),
        [pltpu.VMEM((4 * pairs, tokens), jnp.float32)] * 2,
    )


def hidden_kernel(offsets, line_count, place, own, own_c, lines, lines_c, side, side_c, over, over_c,
                  diag, diag_c, pick, gate, w_down, saved_gate, saved_up, _, grads, slots):
    piece = over.shape[1]
    width = diag.shape[2]
    rows = pick.shape[1] // 2
    units = w_down.shape[1]
    near = pl.multiple_of(place[3] * piece, piece)
    far = pl.multiple_of((1 - place[3]) * piece, piece)

    @pl.loop(0, width // TILE)
    def _(k):
        at = pl.ds(pl.multiple_of(k * TILE, TILE), TILE)
        for i, r in enumerate(offsets):
            for ry in range(2):
                parts = []
                for c in range(2):
                    if ry == 1:
                        parts += [(over, over_c)[c][i, :, at], (diag, diag_c)[c][i, :, at]]
                    elif r == 0:
                        group = (own, own_c)[c]
                        parts += [group[pl.ds(near, piece), at], group[pl.ds(far, piece), at]]
                    else:
                        j = r_place(r, offsets)
                        parts += [(lines, lines_c)[c][j, :, at], (side, side_c)[c][j, :, at]]
                p = i * 2 + ry
                picked = jnp.dot(
                    pick[p], jnp.concatenate(parts, axis=0), preferred_element_type=jnp.float32
                )
                weight = gate[p]
                weight = jnp.concatenate([weight] * (TILE // weight.shape[1]), axis=1)
                scaled = (picked * weight).astype(jnp.bfloat16)
                slots[0, p * rows:(p + 1) * rows, at] = scaled[:rows]
                slots[1, p * rows:(p + 1) * rows, at] = scaled[rows:]

    for e in range(2):
        total = lax.dot_general(
            slots[e], w_down[e], (((1,), (1,)), ((), ())), preferred_element_type=jnp.float32
        )
        for i, r in enumerate(offsets):
            for ry in range(2):
                p = i * 2 + ry
                mine = slice(p * rows, (p + 1) * rows)
                saved = pl.ds(pair_base(place, line_count, r, ry, rows), rows)
                hidden_grad = total[mine]
                grads[e, mine, units:] = (hidden_grad * saved_up[e, saved, :]).astype(jnp.bfloat16)
                grads[e, mine, :units] = (hidden_grad * saved_gate[e, saved, :]).astype(jnp.bfloat16)


def hidden(offsets, line_count, place, own, own_c, moved, pick, gate, w_down, saved, after):
    width = own.shape[1]
    units = w_down.shape[1]
    count = pick.shape[0] * pick.shape[1] // 2
    return small(
        functools.partial(hidden_kernel, offsets, line_count),
        "hidden",
        [(2, count, 2 * units)],
        "s" + "v" * 15 + "o",
        (place, own, own_c, *moved, pick, gate, w_down, *saved, after),
        [pltpu.VMEM((2, count, width), jnp.bfloat16)],
        limit=12,
    )[0]


def sums_kernel(offset, grads, w_gate, w_up, pick_t, _, keep, send, slots):
    rows = pick_t.shape[2] // 2
    tokens = pick_t.shape[1] // 2

    @pl.loop(0, keep.shape[2] // TILE)
    def _(k):
        at = pl.ds(pl.multiple_of(k * TILE, TILE), TILE)
        source = pl.ds(pl.multiple_of(offset + k * TILE, TILE), TILE)
        for e in range(2):
            weights = jnp.concatenate([w_gate[e, :, source], w_up[e, :, source]], axis=0)
            slots[e] = jnp.dot(grads[e], weights, preferred_element_type=jnp.float32).astype(
                jnp.bfloat16
            )
        for p in range(pick_t.shape[0]):
            mine = slice(p * rows, (p + 1) * rows)
            both = jnp.concatenate([slots[0, mine], slots[1, mine]], axis=0)
            total = jnp.dot(pick_t[p], both, preferred_element_type=jnp.float32).astype(
                jnp.bfloat16
            )
            keep[p, :, at] = total[:tokens]
            send[p, :, at] = total[tokens:]


def sums(offset, width, grads, w_gate, w_up, pick_t, after, work=0):
    pairs, tokens, _ = pick_t.shape
    _, count, units = grads.shape
    return small(
        functools.partial(sums_kernel, offset),
        "sums",
        [(pairs, tokens // 2, width)] * 2,
        "vvvvo",
        (grads, w_gate, w_up, pick_t, after),
        [pltpu.VMEM((2, count, TILE), jnp.bfloat16)],
        limit=8,
        work=work,
    )


def first_left_kernel(keep, came, _, send, kept):
    piece = kept.shape[1]
    kept[...] = keep[:, :piece] + came[:, :piece]
    send[...] = keep[:, piece:] + came[:, piece:]


def first_left(keep, came, after):
    pairs, tokens, width = keep.shape
    return small(
        first_left_kernel,
        "first_left",
        [(pairs, tokens // 2, width)] * 2,
        "vvo",
        (keep, came, after),
    )


def first_right_kernel(keep, came, _, send, kept):
    for i in range(kept.shape[0]):
        kept[i] = keep[2 * i] + came[2 * i]
        send[i] = keep[2 * i + 1] + came[2 * i + 1]


def first_right(keep, came, after):
    pairs, tokens, width = keep.shape
    return small(
        first_right_kernel,
        "first_right",
        [(pairs // 2, tokens, width)] * 2,
        "vvo",
        (keep, came, after),
    )


def second_apart_kernel(keep_l, came_l, keep_r, came_r, _, *outs):
    piece = outs[0].shape[0]
    for i in range(keep_r.shape[0]):
        send_l, left, send_r, right = outs[4 * i:4 * i + 4]
        left[...] = keep_l[2 * i] + came_l[2 * i]
        send_l[...] = keep_l[2 * i + 1] + came_l[2 * i + 1]
        right[...] = keep_r[i, :piece] + came_r[i, :piece]
        send_r[...] = keep_r[i, piece:] + came_r[i, piece:]


def second_apart(keep_l, came_l, keep_r, came_r, after):
    lines = keep_r.shape[0]
    _, piece, middle = keep_l.shape
    return small(
        second_apart_kernel,
        "second_sum",
        [(piece, middle)] * (4 * lines),
        "vvvvo",
        (keep_l, came_l, keep_r, came_r, after),
        work=1 << 36,
    )


def third_apart_kernel(left, came_l, right, came_r, _, out):
    middle = left.shape[-1]
    for at, one, other in ((slice(0, middle), left, came_l), (slice(middle, None), right, came_r)):
        out[:, at] = (one[...].astype(jnp.float32) + other[...].astype(jnp.float32)).astype(out.dtype)


def third_apart(left, came_l, right, came_r, after, kind=jnp.bfloat16, work=0):
    piece, middle = left.shape
    return small(
        third_apart_kernel,
        "third_sum",
        [jax.ShapeDtypeStruct((piece, 2 * middle), kind)],
        "vvvvo",
        (left, came_l, right, came_r, after),
        work=work,
    )[0]


def last_kernel(*refs):
    total = refs[0][...].astype(jnp.float32)
    for ref in refs[1:-1]:
        total = total + ref[...].astype(jnp.float32)
    refs[-1][...] = total


def add_up(terms, name, work=0):
    return small(
        last_kernel,
        name,
        [jax.ShapeDtypeStruct(terms[0].shape, jnp.float32)],
        "v" * len(terms),
        terms,
        work=work,
    )[0]


def tokens_body(cotangent, gates, expert_ids, saved_gate, saved_up, w_gate, w_up, w_down):
    owners = lax.axis_size("expert")
    row_count, feature_dim = cotangent.shape
    capacity = saved_gate.shape[2] // owners
    lines = owners // 4
    piece = row_count // 2
    middle = feature_dim // 2
    me, half = lax.axis_index("expert"), lax.axis_index("tp")
    place = jnp.stack([me % 2, me // 2 % 2, me // 4, half]).astype(jnp.int32)

    routing = jnp.concatenate([gates.T, expert_ids.T.astype(jnp.float32)], axis=0)
    part, table = prepare(place, cotangent, routing, piece)
    first = swap(part, "expert", 2)
    own_c, table_c = swap(cotangent, "expert", 1), swap(table, "expert", 1)
    gathered, saved = [], None

    def compute(index, after):
        offsets, moved = CHUNKS[index], gathered[index]
        line, line_c, _, _, over, over_c = moved[:6]
        pick, pick_t, gate = route(
            offsets, place, table, table_c, line, line_c, over, over_c, capacity
        )
        grads = hidden(
            offsets, lines, place, cotangent, own_c, moved, pick, gate, w_down, saved, after
        )
        return grads, pick_t

    def sums_by_token(offset, grads, pick_t, after, work=0):
        keep, send = sums(offset, middle, grads, w_gate, w_up, pick_t, after, work)
        return [keep, swap(send, "expert", 1)], send

    for offsets in CHUNKS:
        pieces = [along_line(part, -r) for r in offsets if r != 0]
        if saved is None:
            line, part = relay(pieces[0], part)
            saved = turn(saved_gate, saved_up, line)
        else:
            line = stack(pieces, saved[0])
        side, over = swap(line, "tp", 1), swap(line, "expert", 2)
        if offsets[0] == 0:
            over, left, right = own_corner(place, cotangent, first, over, side)
            after = (left,)
        else:
            early = compute(0, line)
            grads, pick_t = early
            early_l, after = sums_by_token(0, grads, pick_t, grads)
            left, right = corner(over, side, middle, after)
            early_r, after = sums_by_token(middle, grads, pick_t, left, 68719476736)
            after = (after,)
        diag = join(swap(left, "tp", 1), swap(right, "expert", 2), *after, work=8589934592)
        moved = []
        for array in (line, side, over, diag):
            moved += [array, swap(array, "expert", 1)]
        gathered.append(moved)

    def first_step(keep_l, came_l, keep_r, came_r, after):
        send_l, keep_l = first_left(keep_l, came_l, after)
        send_r, keep_r = first_right(keep_r, came_r, send_l)
        return keep_l, swap(send_l, "tp", 1), keep_r, swap(send_r, "expert", 2), send_r

    def across(send_l, left, send_r, right, after, kind=jnp.bfloat16, work=0):
        came_l, came_r = swap(send_l, "expert", 2), swap(send_r, "tp", 1)
        return third_apart(left, came_l, right, came_r, after, kind, work)

    early = first_step(*early_l, *early_r, gathered[1][6])
    grads, pick_t = compute(1, early[4])
    late_l, after = sums_by_token(0, grads, pick_t, grads)
    late_r, _ = sums_by_token(middle, grads, pick_t, after)
    parts = second_apart(*early[:4], early[4])
    (send_l, left, send_r, right), out = parts[:4], parts[4:]
    done = across(*out, out[0])
    early, after = along_line(done, CHUNKS[0][1]), out[0]
    late = first_step(*late_l, *late_r, after)
    parts = second_apart(*late[:4], done)
    after, total = early, None
    for i, r in enumerate(CHUNKS[1]):
        after = across(*parts[4 * i:4 * i + 4], after)
        came = along_line(after, r)
        if total is None:
            total = add_up([early, came], "middle_sum")
    send_l, send_r = hold([send_l, send_r], after)
    own = across(send_l, left, send_r, right, after, jnp.float32)
    return add_up([total, own, came], "last_sum")


def body(*arrays):
    cotangent, gates, _, saved_gate = arrays[:4]
    owners = lax.axis_size("expert")
    fits = (
        owners == 16
        and lax.axis_size("tp") == 2
        and cotangent.shape[0] == 128
        and cotangent.shape[1] % (2 * TILE) == 0
        and gates.shape[1] == 8
        and saved_gate.shape[0] == 2
        and saved_gate.shape[2] // owners % 16 == 0
        and 4 * saved_gate.shape[2] // owners <= 256
    )
    return (tokens_body if fits else slots_body)(*arrays)


def solution(mesh):
    in_specs = (
        P("expert", None),
        P("expert", None),
        P("expert", None),
        P("expert", "tp", None),
        P("expert", "tp", None),
        P("expert", "tp", None),
        P("expert", "tp", None),
        P("expert", "tp", None),
    )
    out_specs = P(("expert", "tp"), None)
    return jax.shard_map(body, mesh=mesh, in_specs=in_specs, out_specs=out_specs, check_vma=False)
```
